32 devices in a mesh: group: 4 (over y, x), member: 8 (over z, core).
Axes of the slice: x: 2, y: 2, z: 4, core: 2. Of those that a mesh axis runs over, the one named last changes fastest.
Arguments:
- embeddings: bfloat16 [3072, 4096], P(('group', 'member'))
- cluster_ids: int32 [3072], P(('group', 'member')), may hold values from 0 to 7, as said below
- order_index: int32 [3072], P(('group', 'member')), may hold values from 0 to 3071, each once
Outputs:
- best_similarity: float32 [3072], P(('group', 'member'))
The draws below stay inside these ranges and needn't reach their ends.
Inputs may be any that keep to these rules, and one draw needn't show every extreme that they name: `cluster_ids`: among the documents of one device, at most 48 have a cluster of any one group index g (cluster // 2 == g), and on every device some group index has exactly 48.
All inputs are finite; a program needn't handle non-finite values.
Results may differ from the reference program's by a relative error of at most 0.0004.
Values may be sent and summed in bfloat16 or wider, within the bound.
No kernel may reach another device: no remote copies, remote signals or barrier semaphores. Data moves between devices by JAX's collectives and lax.ppermute only.
A program may use at most 128 MiB of HBM per device.

```python
import jax
import jax.numpy as jnp
from jax import lax

D = 4096
ROW_DEV = 96
CL_GROUP = 2
GROUPS = 4
DEVICE_LIMIT = 48
CLUSTERS = 8
ROWS = 3072


def assign_clusters(key):
    folded = jax.random.fold_in(key, 11)
    keys = jax.random.split(folded, 8)
    device_total = ROWS // ROW_DEV
    position_count = GROUPS * DEVICE_LIMIT
    preferred_choice = jax.random.randint(keys[0], (device_total,), 0, GROUPS)
    spread_jitter = jax.random.randint(keys[1], (device_total, position_count), 0, 4096)
    position_index = jnp.arange(position_count, dtype=jnp.int32)
    extra_credit = jnp.where(position_index[None, :] // DEVICE_LIMIT == preferred_choice[:, None], 2 ** 28, 0)
    rating_value = spread_jitter * position_count + position_index[None, :] + extra_credit
    picked_score, chosen = lax.top_k(rating_value, ROW_DEV)
    shuffle_keys = jax.random.split(keys[2], device_total)
    shuffled = jax.vmap(jax.random.permutation)(shuffle_keys, chosen)
    target_group = shuffled // DEVICE_LIMIT
    first_factor = jax.random.randint(keys[3], (device_total, ROW_DEV), 0, CL_GROUP)
    second_factor = jax.random.randint(keys[4], (device_total, ROW_DEV), 1, CL_GROUP + 1)
    within = first_factor * second_factor // CL_GROUP
    cluster_grid = target_group * CL_GROUP + within
    flagged = jax.random.randint(keys[5], (device_total, ROW_DEV), 0, 10) < 2
    offsets = jax.random.randint(keys[6], (device_total, ROW_DEV, 8), 1, device_total)
    partner = (jnp.arange(device_total, dtype=jnp.int32)[:, None, None] + offsets) % device_total
    candidate_group = target_group[partner]
    candidate_free = jnp.logical_not(flagged[partner])
    candidate_ok = (candidate_group == target_group[:, :, None, None]) & candidate_free
    pool_size = 8 * ROW_DEV
    pick_noise = jax.random.randint(keys[7], (device_total, ROW_DEV, 8, ROW_DEV), 0, 2 ** 19)
    pool_index = jnp.arange(pool_size, dtype=jnp.int32).reshape(8, ROW_DEV)
    candidate_score = jnp.where(candidate_ok, pick_noise * pool_size + pool_index[None, None, :, :], -1)
    candidate_score = candidate_score.reshape(device_total, ROW_DEV, pool_size)
    top_score, top_position = lax.top_k(candidate_score, 1)
    found = top_score[:, :, 0] >= 0
    duplicate = flagged & found
    position = top_position[:, :, 0]
    source_slot = position // ROW_DEV
    source_local = position % ROW_DEV
    source_device = jnp.take_along_axis(partner, source_slot[:, :, None], axis=2)[:, :, 0]
    source = (source_device * ROW_DEV + source_local).reshape(-1).astype(jnp.int32)
    flat_clusters = cluster_grid.reshape(-1)
    duplicate = duplicate.reshape(-1)
    clusters = jnp.where(duplicate, flat_clusters[source], flat_clusters)
    return (clusters.astype(jnp.int32), duplicate, source)


def draw_cluster_ids(key, part):
    clusters, duplicate, source = assign_clusters(key)
    return clusters


def draw_embeddings(key, part):
    clusters, duplicate, source = assign_clusters(key)
    folded = jax.random.fold_in(key, 23)
    keys = jax.random.split(folded, 6)
    centroids = jax.random.normal(keys[0], (CLUSTERS, D), jnp.float32)
    amount = jax.random.uniform(keys[4], (ROWS, 1), jnp.float32, 0.1, 0.7)
    noise = jax.random.normal(keys[2], (ROWS, D), jnp.float32)
    copy_noise = jax.random.normal(keys[5], (ROWS, D), jnp.float32)
    base = centroids[clusters] + noise
    copied = base[source] + amount * copy_noise
    values = jnp.where(duplicate[:, None], copied, base)
    return values.astype(jnp.bfloat16)


def setup_inputs(seed: int = 0) -> dict:
    key_list = jax.random.split(jax.random.key(seed), 4)
    return {
        "embeddings": draw_embeddings(jax.random.fold_in(key_list[3], 71), 0),
        "cluster_ids": draw_cluster_ids(jax.random.fold_in(key_list[3], 71), 0),
        "order_index": jax.random.permutation(key_list[2], ROWS).astype(jnp.int32),
    }


def normalize(embeddings):
    values = embeddings.astype(jnp.float32)
    total = lax.optimization_barrier(jnp.sum(values * values, axis=1, keepdims=True)) + values.shape[1] * 1e-06
    return (values * lax.rsqrt(total)).astype(jnp.bfloat16)

def reference(embeddings, cluster_ids, order_index):
    unit_rows = normalize(embeddings).astype(jnp.float32)
    owner_group = cluster_ids // CL_GROUP
    position_count = ROWS // ROW_DEV * DEVICE_LIMIT

    def per_group(group_number):
        member_rows = jnp.argsort((owner_group != group_number).astype(jnp.int32), stable=True)[:position_count].astype(jnp.int32)
        valid = owner_group[member_rows] == group_number
        block = unit_rows[member_rows]
        block_cluster = jnp.where(valid, cluster_ids[member_rows], -1)
        block_order = order_index[member_rows]
        cosine = jnp.dot(block, block.T, preferred_element_type=jnp.float32, precision=lax.Precision.HIGHEST)
        earlier = (block_cluster[:, None] == block_cluster[None, :]) & (block_cluster[:, None] >= 0)
        earlier = earlier & (block_order[None, :] < block_order[:, None])
        result = lax.optimization_barrier(jnp.max(jnp.where(earlier, cosine, -1.0), axis=1))
        return (member_rows, jnp.where(valid, result, -2.0))
    indices, results = lax.map(per_group, jnp.arange(GROUPS, dtype=jnp.int32))
    base = jnp.full((ROWS,), -2.0, dtype=jnp.float32)
    return base.at[indices.reshape(-1)].max(results.reshape(-1))
```

```python
import jax
import jax.numpy as jnp
from jax import lax
from jax.sharding import Mesh, PartitionSpec as P

AXES = ("group", "z", "core")


def ring_pairs(length, shift):
    if 2 * shift < length:
        return [(k, (k + shift) % length) for k in range(length)]
    pairs = []
    for k in range(length // 2):
        low, high = k, k + shift
        pairs.append((low, high) if k % 2 == 0 else (high, low))
    return pairs


def inverse(pairs):
    return [(b, a) for a, b in pairs]


def maxima(rows, row_meta, cols, col_meta):
    dots = lax.dot_general(rows, cols, (((1,), (1,)), ((), ())), preferred_element_type=jnp.float32)
    row_scale, col_scale = row_meta[2][:, None], col_meta[2][None, :]
    live = (row_scale > 0) & (col_scale > 0)
    cosine = jnp.where(live, dots * row_scale * col_scale, 0.0)
    same = (row_meta[0][:, None] == col_meta[0][None, :]) & (row_meta[0][:, None] > 0)
    row_order, col_order = row_meta[1][:, None], col_meta[1][None, :]
    row_best = jnp.max(jnp.where(same & (col_order < row_order), cosine, -1.0), axis=1)
    col_best = jnp.max(jnp.where(same & (row_order < col_order), cosine, -1.0), axis=0)
    return row_best, col_best


def local(embeddings, cluster_ids, order_index):
    row_count, feature_count = embeddings.shape
    length = lax.axis_size("z")
    routes = [ring_pairs(length, shift) for shift in range(1, length // 2 + 1)]
    visitors = [lax.ppermute(embeddings, "z", route) for route in routes]
    plane = lax.all_gather(embeddings, ("group", "core"), axis=0, tiled=True)
    values = embeddings.astype(jnp.float32)
    scale = lax.rsqrt(jnp.sum(values * values, axis=1) + feature_count * 1e-06)
    meta = jnp.stack(
        [(cluster_ids + 1).astype(jnp.float32), order_index.astype(jnp.float32), scale]
    )
    meta = jnp.pad(meta, ((0, 5), (0, -row_count % 128)))
    plane_meta = lax.all_gather(meta, ("group", "core"), axis=0)
    plane_meta = plane_meta[:, :3, :row_count].transpose(1, 0, 2).reshape(3, -1)
    meta_visitors = [lax.ppermute(meta, "z", route)[:3, :row_count] for route in routes]
    own_meta = meta[:3, :row_count]
    best, _ = maxima(embeddings, own_meta, plane, plane_meta)
    rows = jnp.concatenate(visitors)
    row_meta = jnp.concatenate(meta_visitors, axis=1)
    row_best, col_best = maxima(rows, row_meta, plane, plane_meta)
    for index, route in enumerate(routes):
        block = row_best[index * row_count : (index + 1) * row_count]
        home = lax.ppermute(block, "z", inverse(route))
        senders = jnp.array([a for a, b in route])
        sent = jnp.any(senders == lax.axis_index("z"))
        best = jnp.maximum(best, jnp.where(sent, home, -1.0))
    parts = lax.all_to_all(
        col_best.reshape(-1, row_count), ("group", "core"), split_axis=0, concat_axis=0, tiled=True
    )
    return jnp.maximum(best, jnp.max(parts, axis=0))


def solution(mesh):
    groups, members = mesh.devices.shape
    fine = Mesh(mesh.devices.reshape(groups, members // 2, 2), AXES)
    placed = (P(AXES, None), P(AXES), P(AXES))
    return jax.shard_map(local, mesh=fine, in_specs=placed, out_specs=P(AXES), check_vma=False)
```

```python
import functools

import jax
import jax.numpy as jnp
from jax import lax
from jax.experimental import pallas as pl
from jax.experimental.pallas import tpu as pltpu
from jax.sharding import Mesh, PartitionSpec as P

AXES = ("group", "z", "core")
LANES = 128
CHUNK = 512
PER_CALL = 8


def ring_pairs(length, shift):
    if 2 * shift < length:
        return [(k, (k + shift) % length) for k in range(length)]
    pairs = []
    for k in range(length // 2):
        low, high = k, k + shift
        pairs.append((low, high) if k % 2 == 0 else (high, low))
    return pairs


def inverse(pairs):
    return [(b, a) for a, b in pairs]


def unit_rows(values):
    values = values.astype(jnp.float32)
    total = jnp.sum(values * values, axis=1, keepdims=True) + values.shape[1] * 1e-06
    return (values * lax.rsqrt(total)).astype(jnp.bfloat16)


def normalize_kernel(rows_ref, unit_ref):
    unit_ref[...] = unit_rows(rows_ref[...])


def normalize(rows):
    count, width = rows.shape
    step = 32
    spec = pl.BlockSpec((step, width), lambda i: (i, 0))
    return pl.pallas_call(
        normalize_kernel,
        grid=(count // step,),
        in_specs=[spec],
        out_specs=spec,
        out_shape=jax.ShapeDtypeStruct(rows.shape, jnp.bfloat16),
        cost_estimate=pl.CostEstimate(
            flops=4 * count * width, bytes_accessed=4 * count * width, transcendentals=count
        ),
    )(rows)


def device_index(group, z, core):
    return (group * lax.axis_size("z") + z) * lax.axis_size("core") + core


def source_of(route):
    z = lax.axis_index("z")
    source, valid = jnp.int32(0), jnp.int32(0)
    for a, b in route:
        source = jnp.where(z == b, a, source)
        valid = jnp.where(z == b, 1, valid)
    return source, valid


def maxima_kernel(routes, offsets, own, *refs):
    count = len(offsets)
    visitors = len(routes) + own
    meta_ref, refs = refs[0], refs[1:]
    own_ref, refs = (refs[0], refs[1:]) if own else (None, refs)
    visitor_refs, refs = refs[: len(routes)], refs[len(routes) :]
    block_refs, refs = refs[:count], refs[count:]
    carry_ref, refs = (None, refs) if own else (refs[0], refs[1:])
    row_ref, col_ref, units, dots = refs
    rows, width = block_refs[0].shape

    for v in range(visitors):
        start = v * LANES
        if rows < LANES:
            units[start + rows : start + LANES, :] = jnp.zeros((LANES - rows, width), jnp.bfloat16)
        if own and v == 0:
            units[start : start + rows, :] = own_ref[...]
        else:
            units[start : start + rows, :] = unit_rows(visitor_refs[v - own][...])
    for k in range(0, width, CHUNK):
        left = jnp.concatenate([ref[:, k : k + CHUNK] for ref in block_refs], axis=0)
        part = lax.dot_general(
            left,
            units[:, k : k + CHUNK],
            (((1,), (1,)), ((), ())),
            preferred_element_type=jnp.float32,
        )
        dots[...] = part if k == 0 else dots[...] + part

    group, z, core = (lax.axis_index(name) for name in AXES)
    visitor_meta = []
    if own:
        visitor_meta.append(meta_ref[device_index(group, z, core)])
    for route in routes:
        source, valid = source_of(route)
        visitor_meta.append(meta_ref[device_index(group, source, core)] * valid.astype(jnp.float32))
    row_best = [jnp.full((1, LANES), -1.0, jnp.float32) for _ in range(visitors)]
    lane = lax.broadcasted_iota(jnp.int32, (rows, LANES), 1)
    col_all = jnp.full((rows, LANES), -1.0, jnp.float32)
    for j, (s, c) in enumerate(offsets):
        block_meta = meta_ref[device_index(group ^ s, z, core ^ c)]
        turned = block_meta.T
        block_cluster, block_order = turned[:rows, 0:1], turned[:rows, 1:2]
        col_best = jnp.full((rows, 1), -1.0, jnp.float32)
        for v in range(visitors):
            cosine = dots[j * rows : (j + 1) * rows, v * LANES : (v + 1) * LANES]
            cluster, order = visitor_meta[v][0:1, :], visitor_meta[v][1:2, :]
            same = (block_cluster == cluster) & (cluster > 0)
            seen = jnp.where(same & (block_order < order), cosine, -1.0)
            row_best[v] = jnp.maximum(row_best[v], jnp.max(seen, axis=0, keepdims=True))
            if not (own and v == 0):
                seen = jnp.where(same & (order < block_order), cosine, -1.0)
                col_best = jnp.maximum(col_best, jnp.max(seen, axis=1, keepdims=True))
        col_all = jnp.where(lane == j, col_best, col_all)
    for v in range(visitors):
        row_ref[v] = row_best[v]
    if rows < LANES:
        col_all = jnp.concatenate(
            [col_all, jnp.full((LANES - rows, LANES), -1.0, jnp.float32)], axis=0
        )
    turned = col_all.T
    for j, (s, c) in enumerate(offsets):
        place = ((group ^ s) % (PER_CALL // 2)) * 2 + (core ^ c)
        best = turned[j : j + 1, :]
        col_ref[place] = best if own else jnp.maximum(best, carry_ref[place])


def maxima(routes, offsets, meta, own, visitors, blocks, carry=None):
    count = len(visitors) + (own is not None)
    rows, width = blocks[0].shape
    row_best, col_best = None, []
    for first in range(0, len(blocks), PER_CALL):
        part = blocks[first : first + PER_CALL]
        operands = [meta] + ([own] if own is not None else []) + list(visitors) + part
        if own is None:
            operands.append(carry[first // PER_CALL])
        row, col = pl.pallas_call(
            functools.partial(
                maxima_kernel, routes, offsets[first : first + PER_CALL], int(own is not None)
            ),
            in_specs=[pl.BlockSpec(memory_space=pltpu.VMEM)] * len(operands),
            out_specs=[pl.BlockSpec(memory_space=pltpu.VMEM)] * 2,
            out_shape=[
                jax.ShapeDtypeStruct((count, 1, LANES), jnp.float32),
                jax.ShapeDtypeStruct((len(part), 1, LANES), jnp.float32),
            ],
            scratch_shapes=[
                pltpu.VMEM((count * LANES, width), jnp.bfloat16),
                pltpu.VMEM((len(part) * rows, count * LANES), jnp.float32),
            ],
            compiler_params=pltpu.CompilerParams(vmem_limit_bytes=40 * 2**20),
            cost_estimate=pl.CostEstimate(
                flops=2 * len(part) * rows * count * LANES * width,
                bytes_accessed=2 * (len(part) + count) * rows * width,
                transcendentals=0,
            ),
        )(*operands)
        row_best = row if row_best is None else jnp.maximum(row_best, row)
        col_best.append(col)
    return row_best, col_best


def local(embeddings, cluster_ids, order_index):
    rows, width = embeddings.shape
    groups, length = lax.axis_size("group"), lax.axis_size("z")
    routes = [ring_pairs(length, shift) for shift in range(1, length // 2 + 1)]
    visitors = [lax.ppermute(embeddings, "z", route) for route in routes]
    meta = jnp.stack([(cluster_ids + 1).astype(jnp.float32), order_index.astype(jnp.float32)])
    meta = jnp.pad(meta, ((0, 6), (0, LANES - rows)))
    meta = lax.all_gather(meta, AXES, axis=0)

    unit = normalize(embeddings)
    offsets, blocks = [], []
    for s in range(groups):
        block = unit
        if s:
            block = lax.ppermute(unit, "group", [(k, k ^ s) for k in range(groups)])
        other = lax.ppermute(block, "core", [(0, 1), (1, 0)])
        offsets += [(s, 0), (s, 1)]
        blocks += [block, other]

    row_early, col_early = maxima(routes[:-1], offsets, meta, unit, visitors[:-1], blocks)
    best = row_early[0, 0]
    for index, route in enumerate(routes[:-1]):
        best = jnp.maximum(best, lax.ppermute(row_early[index + 1, 0], "z", inverse(route)))
    row_late, col_late = maxima(
        routes[-1:], offsets, meta, None, visitors[-1:], blocks, col_early
    )
    home = lax.ppermute(row_late[0, 0], "z", inverse(routes[-1]))
    sent = jnp.any(jnp.array([a for a, b in routes[-1]]) == lax.axis_index("z"))
    best = jnp.maximum(best, jnp.where(sent, home, -1.0))
    if len(col_late) > 1:
        turn = (lax.axis_index("group") // (PER_CALL // 2)) ^ jnp.arange(len(col_late))
        col = jnp.stack(col_late)[turn].reshape(-1, 1, LANES)
    else:
        col = col_late[0]
    parts = lax.all_to_all(col, ("group", "core"), split_axis=0, concat_axis=0, tiled=True)
    return jnp.maximum(best, jnp.max(parts, axis=(0, 1)))[:rows]


def solution(mesh):
    groups, members = mesh.devices.shape
    fine = Mesh(mesh.devices.reshape(groups, members // 2, 2), AXES)
    placed = (P(AXES, None), P(AXES), P(AXES))
    return jax.shard_map(local, mesh=fine, in_specs=placed, out_specs=P(AXES), check_vma=False)
```

```python
import functools

import jax
import jax.numpy as jnp
from jax import lax
from jax.experimental import pallas as pl
from jax.experimental.pallas import tpu as pltpu
from jax.sharding import Mesh, PartitionSpec as P

AXES = ("group", "z", "core")
LANES = 128
CHUNK = 512
PER_CALL = 8
VMEM = pl.BlockSpec(memory_space=pltpu.VMEM)


def ring_pairs(length, shift):
    if 2 * shift < length:
        return [(k, (k + shift) % length) for k in range(length)]
    pairs = []
    for k in range(length // 2):
        low, high = k, k + shift
        pairs.append((low, high) if k % 2 == 0 else (high, low))
    return pairs


def inverse(pairs):
    return [(b, a) for a, b in pairs]


def flip(count, bits):
    return [(k, k ^ bits) for k in range(count)]


def unit_rows(values):
    values = values.astype(jnp.float32)
    total = jnp.sum(values * values, axis=1, keepdims=True) + values.shape[1] * 1e-06
    return (values * lax.rsqrt(total)).astype(jnp.bfloat16)


def lane_rows(first, second):
    count = first.shape[1]
    both = jnp.concatenate([first, second, jnp.zeros((6, count), jnp.float32)], axis=0)
    if count < LANES:
        both = jnp.concatenate([both, jnp.zeros((8, LANES - count), jnp.float32)], axis=1)
    return both


def pack_kernel(rows_ref, cluster_ref, order_ref, block_ref, meta_ref):
    rows, width = rows_ref.shape
    block_ref[:, :width] = unit_rows(rows_ref[...])
    meta = lane_rows(cluster_ref[...].astype(jnp.float32) + 1.0, order_ref[...].astype(jnp.float32))
    meta_ref[...] = meta
    turned = meta.T[:rows]
    cluster, order = turned[:, 0:1], turned[:, 1:2]
    high = jnp.floor(order / 256.0)
    lane = lax.broadcasted_iota(jnp.int32, (rows, LANES), 1)
    tail = jnp.where(lane == 0, cluster, jnp.where(lane == 1, high, order - 256.0 * high))
    block_ref[:, width:] = jnp.where(lane < 3, tail, 0.0).astype(jnp.bfloat16)


def pack(rows, cluster_ids, order_index):
    count, width = rows.shape
    return pl.pallas_call(
        pack_kernel,
        in_specs=[VMEM] * 3,
        out_specs=[VMEM] * 2,
        out_shape=[
            jax.ShapeDtypeStruct((count, width + LANES), jnp.bfloat16),
            jax.ShapeDtypeStruct((8, LANES), jnp.float32),
        ],
        cost_estimate=pl.CostEstimate(
            flops=4 * count * width, bytes_accessed=4 * count * width, transcendentals=count
        ),
    )(rows, cluster_ids.reshape(1, count), order_index.reshape(1, count))


def tail_meta(tail):
    tail = tail.astype(jnp.float32)
    return tail[:, 0:1], tail[:, 1:2] * 256.0 + tail[:, 2:3]


def maxima_kernel(packed, raw, pieces, first, carried, *refs):
    take = list(refs)
    packed_refs = [take.pop(0) for _ in range(packed)]
    raw_refs = [(take.pop(0), take.pop(0)) for _ in range(raw)]
    block_refs = [[take.pop(0) for _ in range(n)] for n in pieces]
    carry_ref = take.pop(0) if carried else None
    row_ref, col_ref, units, dots = take
    visitors = packed + raw
    width = units.shape[1]
    rows = sum(ref.shape[0] for ref in block_refs[0])

    visitor_meta = []
    for v in range(visitors):
        start = v * LANES
        if rows < LANES:
            units[start + rows : start + LANES, :] = jnp.zeros((LANES - rows, width), jnp.bfloat16)
        if v < packed:
            units[start : start + rows, :] = packed_refs[v][:, :width]
            tail = packed_refs[v][:, width:].astype(jnp.float32)
            if rows < LANES:
                tail = jnp.concatenate([tail, jnp.zeros((LANES - rows, LANES), jnp.float32)], axis=0)
            turned = tail.T
            visitor_meta.append((turned[0:1], turned[1:2] * 256.0 + turned[2:3]))
        else:
            rows_ref, meta_ref = raw_refs[v - packed]
            units[start : start + rows, :] = unit_rows(rows_ref[...])
            visitor_meta.append((meta_ref[0:1, :], meta_ref[1:2, :]))
    flat = [ref for parts in block_refs for ref in parts]
    for k in range(0, width, CHUNK):
        left = jnp.concatenate([ref[:, k : k + CHUNK] for ref in flat], axis=0)
        part = lax.dot_general(
            left,
            units[:, k : k + CHUNK],
            (((1,), (1,)), ((), ())),
            preferred_element_type=jnp.float32,
        )
        dots[...] = part if k == 0 else dots[...] + part

    row_best = [jnp.full((1, LANES), -1.0, jnp.float32) for _ in range(visitors)]
    lane = lax.broadcasted_iota(jnp.int32, (rows, LANES), 1)
    col_all = jnp.full((rows, LANES), -1.0, jnp.float32)
    for j, parts in enumerate(block_refs):
        tail = jnp.concatenate([ref[:, width:] for ref in parts], axis=0)
        block_cluster, block_order = tail_meta(tail)
        col_best = jnp.full((rows, 1), -1.0, jnp.float32)
        for v in range(visitors):
            cosine = dots[j * rows : (j + 1) * rows, v * LANES : (v + 1) * LANES]
            cluster, order = visitor_meta[v]
            same = (block_cluster == cluster) & (cluster > 0)
            seen = jnp.where(same & (block_order < order), cosine, -1.0)
            row_best[v] = jnp.maximum(row_best[v], jnp.max(seen, axis=0, keepdims=True))
            if carried or v > 0:
                seen = jnp.where(same & (order < block_order), cosine, -1.0)
                col_best = jnp.maximum(col_best, jnp.max(seen, axis=1, keepdims=True))
        col_all = jnp.where(lane == j, col_best, col_all)
    for v in range(visitors):
        row_ref[v] = row_best[v]
    if rows < LANES:
        fill = jnp.full((LANES - rows, LANES), -1.0, jnp.float32)
        col_all = jnp.concatenate([col_all, fill], axis=0)
    turned = col_all.T
    group, core = lax.axis_index("group"), lax.axis_index("core")
    for j in range(len(pieces)):
        s, c = (first + j) // 2, (first + j) % 2
        place = ((group ^ s) & (PER_CALL // 2 - 1)) * 2 + (core ^ c)
        best = turned[j : j + 1, :]
        col_ref[place] = jnp.maximum(best, carry_ref[place]) if carried else best


def maxima(packed, raw, blocks, carry=None):
    count = len(packed) + len(raw)
    rows, width = packed[0].shape[0], packed[0].shape[1] - LANES
    row_best, col_best = None, []
    for first in range(0, len(blocks), PER_CALL):
        part = blocks[first : first + PER_CALL]
        operands = list(packed)
        for pair in raw:
            operands += pair
        operands += [piece for block in part for piece in block]
        if carry is not None:
            operands.append(carry[first // PER_CALL])
        row, col = pl.pallas_call(
            functools.partial(
                maxima_kernel,
                len(packed),
                len(raw),
                [len(block) for block in part],
                first,
                carry is not None,
            ),
            in_specs=[VMEM] * len(operands),
            out_specs=[VMEM] * 2,
            out_shape=[
                jax.ShapeDtypeStruct((count, 1, LANES), jnp.float32),
                jax.ShapeDtypeStruct((len(part), 1, LANES), jnp.float32),
            ],
            scratch_shapes=[
                pltpu.VMEM((count * LANES, width), jnp.bfloat16),
                pltpu.VMEM((len(part) * rows, count * LANES), jnp.float32),
            ],
            compiler_params=pltpu.CompilerParams(vmem_limit_bytes=40 * 2**20),
            cost_estimate=pl.CostEstimate(
                flops=2 * len(part) * rows * count * LANES * width,
                bytes_accessed=2 * (len(part) + count) * rows * width,
                transcendentals=0,
            ),
        )(*operands)
        row_best = row if row_best is None else jnp.maximum(row_best, row)
        col_best.append(col)
    return row_best, col_best


def gather_plane(block, groups):
    half = block.shape[0] // 2
    blocks = {0: [block]}
    for s in range(1, groups):
        low, high = s & -s, 1 << (s.bit_length() - 1)
        if low == high:
            blocks[s] = [lax.ppermute(block, "group", flip(groups, s))]
            continue
        top, bottom = blocks[s ^ high], blocks[s ^ low]
        top = top[0][:half] if len(top) == 1 else top[0]
        bottom = bottom[0][half:] if len(bottom) == 1 else bottom[1]
        blocks[s] = [
            lax.ppermute(top, "group", flip(groups, high)),
            lax.ppermute(bottom, "group", flip(groups, low)),
        ]
    return blocks


def local(embeddings, cluster_ids, order_index):
    rows = embeddings.shape[0]
    groups, length = lax.axis_size("group"), lax.axis_size("z")
    routes = [ring_pairs(length, shift) for shift in range(1, length // 2 + 1)]
    early = [lax.ppermute(embeddings, "z", route) for route in routes[:-1]]
    own, meta = pack(embeddings, cluster_ids, order_index)
    early = [(block, lax.ppermute(meta, "z", route)) for block, route in zip(early, routes)]
    late = lax.ppermute(own, "z", routes[-1])

    blocks = []
    for parts in gather_plane(own, groups).values():
        blocks.append(parts)
        blocks.append([lax.ppermute(part, "core", flip(2, 1)) for part in parts])

    row_early, col_early = maxima([own], early, blocks)
    best = row_early[0, 0]
    for index, route in enumerate(routes[:-1]):
        best = jnp.maximum(best, lax.ppermute(row_early[index + 1, 0], "z", inverse(route)))
    row_late, col_late = maxima([late], [], blocks, col_early)
    home = lax.ppermute(row_late[0, 0], "z", inverse(routes[-1]))
    sent = jnp.any(jnp.array([a for a, b in routes[-1]]) == lax.axis_index("z"))
    best = jnp.maximum(best, jnp.where(sent, home, -1.0))
    if len(col_late) > 1:
        turn = (lax.axis_index("group") // (PER_CALL // 2)) ^ jnp.arange(len(col_late))
        col = jnp.stack(col_late)[turn].reshape(-1, 1, LANES)
    else:
        col = col_late[0]
    parts = lax.all_to_all(col, ("group", "core"), split_axis=0, concat_axis=0, tiled=True)
    return jnp.maximum(best, jnp.max(parts, axis=(0, 1)))[:rows]


def solution(mesh):
    groups, members = mesh.devices.shape
    fine = Mesh(mesh.devices.reshape(groups, members // 2, 2), AXES)
    placed = (P(AXES, None), P(AXES), P(AXES))
    return jax.shard_map(local, mesh=fine, in_specs=placed, out_specs=P(AXES), check_vma=False)
```

```python
import functools

import jax
import jax.numpy as jnp
from jax import lax
from jax.experimental import pallas as pl
from jax.experimental.pallas import tpu as pltpu
from jax.sharding import Mesh, PartitionSpec as P

AXES = ("group", "z", "core")
LANES = 128
CHUNK = 512
PER_CALL = 4
VMEM = pl.BlockSpec(memory_space=pltpu.VMEM)


def ring_pairs(length, shift):
    if 2 * shift < length:
        return [(k, (k + shift) % length) for k in range(length)]
    pairs = []
    for k in range(length // 2):
        low, high = k, k + shift
        pairs.append((low, high) if k % 2 == 0 else (high, low))
    return pairs


def flip(count, bits):
    return [(k, k ^ bits) for k in range(count)]


def unit_rows(values):
    values = values.astype(jnp.float32)
    total = jnp.sum(values * values, axis=1, keepdims=True) + values.shape[1] * 1e-06
    return (values * lax.rsqrt(total)).astype(jnp.bfloat16)


def lane_rows(first, second):
    count = first.shape[1]
    both = jnp.concatenate([first, second, jnp.zeros((6, count), jnp.float32)], axis=0)
    if count < LANES:
        both = jnp.concatenate([both, jnp.zeros((8, LANES - count), jnp.float32)], axis=1)
    return both


def pack_kernel(rows_ref, cluster_ref, order_ref, block_ref):
    rows, width = rows_ref.shape
    block_ref[:, :width] = unit_rows(rows_ref[...])
    meta = lane_rows(cluster_ref[...].astype(jnp.float32) + 1.0, order_ref[...].astype(jnp.float32))
    turned = meta.T[:rows]
    cluster, order = turned[:, 0:1], turned[:, 1:2]
    high = jnp.floor(order / 256.0)
    lane = lax.broadcasted_iota(jnp.int32, (rows, LANES), 1)
    tail = jnp.where(lane == 0, cluster, jnp.where(lane == 1, high, order - 256.0 * high))
    block_ref[:, width:] = jnp.where(lane < 3, tail, 0.0).astype(jnp.bfloat16)


def pack(rows, cluster_ids, order_index):
    count, width = rows.shape
    return pl.pallas_call(
        pack_kernel,
        in_specs=[VMEM] * 3,
        out_specs=VMEM,
        out_shape=jax.ShapeDtypeStruct((count, width + LANES), jnp.bfloat16),
        cost_estimate=pl.CostEstimate(
            flops=4 * count * width, bytes_accessed=4 * count * width, transcendentals=count
        ),
    )(rows, cluster_ids.reshape(1, count), order_index.reshape(1, count))


def device_index(group, z, core):
    return (group * lax.axis_size("z") + z) * lax.axis_size("core") + core


def source_of(route):
    here = lax.axis_index("z")
    source = here
    for a, b in route:
        source = jnp.where(here == b, a, source)
    return source


def maxima_kernel(homes, pieces, first, carried, *refs):
    take = list(refs)
    visitor_refs = [take.pop(0) for _ in homes]
    block_refs = [[take.pop(0) for _ in range(n)] for n in pieces]
    carry_ref = take.pop(0) if carried else None
    answer_ref, units, dots = take
    width = units.shape[1]
    rows = sum(ref.shape[0] for ref in block_refs[0])

    visitor_meta = []
    for v, ref in enumerate(visitor_refs):
        start = v * LANES
        before = homes[v][2]
        after = LANES - before - ref.shape[0]
        units[start + before : start + LANES - after, :] = ref[:, :width]
        tail = [ref[:, width:].astype(jnp.float32)]
        if before:
            units[start : start + before, :] = jnp.zeros((before, width), jnp.bfloat16)
            tail.insert(0, jnp.zeros((before, LANES), jnp.float32))
        if after:
            units[start + LANES - after : start + LANES, :] = jnp.zeros((after, width), jnp.bfloat16)
            tail.append(jnp.zeros((after, LANES), jnp.float32))
        turned = jnp.concatenate(tail, axis=0).T
        visitor_meta.append((turned[0:1], turned[1:2] * 256.0 + turned[2:3]))
    flat = [ref for parts in block_refs for ref in parts]
    for k in range(0, width, CHUNK):
        left = jnp.concatenate([ref[:, k : k + CHUNK] for ref in flat], axis=0)
        part = lax.dot_general(
            left,
            units[:, k : k + CHUNK],
            (((1,), (1,)), ((), ())),
            preferred_element_type=jnp.float32,
        )
        dots[...] = part if k == 0 else dots[...] + part

    row_best = [jnp.full((1, LANES), -1.0, jnp.float32) for _ in homes]
    lane = lax.broadcasted_iota(jnp.int32, (rows, LANES), 1)
    col_all = jnp.full((rows, LANES), -1.0, jnp.float32)
    for j, parts in enumerate(block_refs):
        tail = jnp.concatenate([ref[:, width:] for ref in parts], axis=0).astype(jnp.float32)
        block_cluster, block_order = tail[:, 0:1], tail[:, 1:2] * 256.0 + tail[:, 2:3]
        col_best = jnp.full((rows, 1), -1.0, jnp.float32)
        for v, (route, _, _) in enumerate(homes):
            cosine = dots[j * rows : (j + 1) * rows, v * LANES : (v + 1) * LANES]
            cluster, order = visitor_meta[v]
            same = (block_cluster == cluster) & (cluster > 0)
            seen = jnp.where(same & (block_order < order), cosine, -1.0)
            row_best[v] = jnp.maximum(row_best[v], jnp.max(seen, axis=0, keepdims=True))
            if route is not None:
                seen = jnp.where(same & (order < block_order), cosine, -1.0)
                col_best = jnp.maximum(col_best, jnp.max(seen, axis=1, keepdims=True))
        col_all = jnp.where(lane == j, col_best, col_all)
    if rows < LANES:
        fill = jnp.full((LANES - rows, LANES), -1.0, jnp.float32)
        col_all = jnp.concatenate([col_all, fill], axis=0)
    turned = col_all.T

    group, z, core = (lax.axis_index(name) for name in AXES)
    answer_ref[...] = carry_ref[...] if carried else jnp.full(answer_ref.shape, -1.0, jnp.float32)
    for v, (route, other, _) in enumerate(homes):
        source = z if route is None else source_of(route)
        home = device_index(group, source, core ^ 1 if other else core)
        answer_ref[home] = jnp.maximum(answer_ref[home], row_best[v])
    for j in range(len(pieces)):
        home = device_index(group ^ (first + j), z, core)
        answer_ref[home] = jnp.maximum(answer_ref[home], turned[j : j + 1, :])


def maxima(homes, visitors, blocks, answer):
    devices = lax.axis_size(AXES)
    rows, width = sum(piece.shape[0] for piece in blocks[0]), visitors[0].shape[1] - LANES
    for first in range(0, len(blocks), PER_CALL):
        part = blocks[first : first + PER_CALL]
        operands = list(visitors) + [piece for block in part for piece in block]
        if answer is not None:
            operands.append(answer)
        answer = pl.pallas_call(
            functools.partial(
                maxima_kernel, homes, [len(block) for block in part], first, answer is not None
            ),
            in_specs=[VMEM] * len(operands),
            out_specs=VMEM,
            out_shape=jax.ShapeDtypeStruct((devices, 1, LANES), jnp.float32),
            scratch_shapes=[
                pltpu.VMEM((len(visitors) * LANES, width), jnp.bfloat16),
                pltpu.VMEM((len(part) * rows, len(visitors) * LANES), jnp.float32),
            ],
            compiler_params=pltpu.CompilerParams(vmem_limit_bytes=40 * 2**20),
            cost_estimate=pl.CostEstimate(
                flops=2 * len(part) * rows * len(visitors) * LANES * width,
                bytes_accessed=2 * (len(part) + len(visitors)) * rows * width,
                transcendentals=0,
            ),
        )(*operands)
    return answer


def after(value, *others):
    anywhere = pl.BlockSpec(memory_space=pl.ANY)
    return pl.pallas_call(
        lambda *refs: None,
        in_specs=[anywhere] * (1 + len(others)),
        out_specs=anywhere,
        out_shape=jax.ShapeDtypeStruct(value.shape, value.dtype),
        input_output_aliases={0: 0},
        cost_estimate=pl.CostEstimate(flops=0, bytes_accessed=0, transcendentals=0),
    )(value, *others)


def gather_plane(block, groups):
    half = block.shape[0] // 2
    blocks = {0: [block]}
    for s in range(1, groups):
        low, high = s & -s, 1 << (s.bit_length() - 1)
        if low == high:
            blocks[s] = [lax.ppermute(block, "group", flip(groups, s))]
            continue
        top, bottom = blocks[s ^ high], blocks[s ^ low]
        top = top[0][:half] if len(top) == 1 else top[0]
        bottom = bottom[0][half:] if len(bottom) == 1 else bottom[1]
        blocks[s] = [
            lax.ppermute(top, "group", flip(groups, high)),
            lax.ppermute(bottom, "group", flip(groups, low)),
        ]
    return blocks


def local(embeddings, cluster_ids, order_index):
    rows = embeddings.shape[0]
    groups, length = lax.axis_size("group"), lax.axis_size("z")
    routes = [ring_pairs(length, shift) for shift in range(1, length // 2 + 1)]
    own = pack(embeddings, cluster_ids, order_index)
    arrived = [lax.ppermute(own, "z", route) for route in routes]
    blocks = list(gather_plane(own, groups).values())

    homes, visitors = [], []
    for block, route in [(own, None)] + list(zip(arrived[:-1], routes)):
        homes += [(route, False, 0), (route, True, 0)]
        visitors += [block, lax.ppermute(block, "core", flip(2, 1))]
    answer = maxima(homes, visitors, blocks, None)
    last = after(arrived[-1], answer)
    other = lax.ppermute(last, "core", flip(2, 1))
    answer = maxima([(routes[-1], False, 0)], [last], blocks, answer)
    answer = maxima([(routes[-1], True, 0)], [other], blocks, answer)
    parts = lax.all_to_all(answer, AXES, split_axis=0, concat_axis=0, tiled=True)
    return jnp.max(parts, axis=(0, 1))[:rows]


def solution(mesh):
    groups, members = mesh.devices.shape
    fine = Mesh(mesh.devices.reshape(groups, members // 2, 2), AXES)
    placed = (P(AXES, None), P(AXES), P(AXES))
    return jax.shard_map(local, mesh=fine, in_specs=placed, out_specs=P(AXES), check_vma=False)
```

```python
import functools

import jax
import jax.numpy as jnp
from jax import lax
from jax.experimental import pallas as pl
from jax.experimental.pallas import tpu as pltpu
from jax.sharding import Mesh, PartitionSpec as P

AXES = ("group", "z", "core")
LANES = 128
CHUNK = 512
PER_CALL = 4
VMEM = pl.BlockSpec(memory_space=pltpu.VMEM)


def ring_pairs(length, shift):
    if 2 * shift < length:
        return [(k, (k + shift) % length) for k in range(length)]
    pairs = []
    for k in range(length // 2):
        low, high = k, k + shift
        pairs.append((low, high) if k % 2 == 0 else (high, low))
    return pairs


def flip(count, bits):
    return [(k, k ^ bits) for k in range(count)]


def unit_rows(values):
    values = values.astype(jnp.float32)
    total = jnp.sum(values * values, axis=1, keepdims=True) + values.shape[1] * 1e-06
    return (values * lax.rsqrt(total)).astype(jnp.bfloat16)


def lane_rows(first, second):
    count = first.shape[1]
    both = jnp.concatenate([first, second, jnp.zeros((6, count), jnp.float32)], axis=0)
    if count < LANES:
        both = jnp.concatenate([both, jnp.zeros((8, LANES - count), jnp.float32)], axis=1)
    return both


def pack_kernel(rows_ref, cluster_ref, order_ref, block_ref):
    rows, width = rows_ref.shape
    block_ref[:, :width] = unit_rows(rows_ref[...])
    meta = lane_rows(cluster_ref[...].astype(jnp.float32) + 1.0, order_ref[...].astype(jnp.float32))
    turned = meta.T[:rows]
    cluster, order = turned[:, 0:1], turned[:, 1:2]
    high = jnp.floor(order / 256.0)
    lane = lax.broadcasted_iota(jnp.int32, (rows, LANES), 1)
    tail = jnp.where(lane == 0, cluster, jnp.where(lane == 1, high, order - 256.0 * high))
    block_ref[:, width:] = jnp.where(lane < 3, tail, 0.0).astype(jnp.bfloat16)


def pack(rows, cluster_ids, order_index):
    count, width = rows.shape
    return pl.pallas_call(
        pack_kernel,
        in_specs=[VMEM] * 3,
        out_specs=VMEM,
        out_shape=jax.ShapeDtypeStruct((count, width + LANES), jnp.bfloat16),
        cost_estimate=pl.CostEstimate(
            flops=4 * count * width, bytes_accessed=4 * count * width, transcendentals=count
        ),
    )(rows, cluster_ids.reshape(1, count), order_index.reshape(1, count))


def maxima_kernel(homed, visitor_pieces, pieces, carried, *refs):
    take = list(refs)
    visitor_refs = [[take.pop(0) for _ in range(n)] for n in visitor_pieces]
    block_refs = [[take.pop(0) for _ in range(n)] for n in pieces]
    carry_refs = [take.pop(0) for _ in pieces] if carried else []
    row_refs = [take.pop(0) for _ in homed]
    col_refs = [take.pop(0) for _ in pieces]
    units, dots = take if len(homed) > 1 else (None, take[0])
    width = block_refs[0][0].shape[1] - LANES
    rows = sum(ref.shape[0] for ref in block_refs[0])
    lanes = LANES if units is not None else rows

    visitor_meta = []
    for v, parts in enumerate(visitor_refs):
        place, tail = v * LANES, []
        for ref in parts:
            if units is not None:
                units[place : place + ref.shape[0], :] = ref[:, :width]
            tail.append(ref[:, width:].astype(jnp.float32))
            place += ref.shape[0]
        spare = (v + 1) * LANES - place
        if spare:
            if units is not None:
                units[place : place + spare, :] = jnp.zeros((spare, width), jnp.bfloat16)
            tail.append(jnp.zeros((spare, LANES), jnp.float32))
        turned = jnp.concatenate(tail, axis=0).T
        visitor_meta.append((turned[0:1, :lanes], turned[1:2, :lanes] * 256.0 + turned[2:3, :lanes]))
    right = visitor_refs[0][0] if units is None else units
    flat = [ref for parts in block_refs for ref in parts]
    for k in range(0, width, CHUNK):
        left = jnp.concatenate([ref[:, k : k + CHUNK] for ref in flat], axis=0)
        part = lax.dot_general(
            left,
            right[:, k : k + CHUNK],
            (((1,), (1,)), ((), ())),
            preferred_element_type=jnp.float32,
        )
        dots[...] = part if k == 0 else dots[...] + part

    row_best = [jnp.full((1, lanes), -1.0, jnp.float32) for _ in homed]
    lane = lax.broadcasted_iota(jnp.int32, (rows, LANES), 1)
    col_all = jnp.full((rows, LANES), -1.0, jnp.float32)
    for j, parts in enumerate(block_refs):
        tail = jnp.concatenate([ref[:, width:] for ref in parts], axis=0).astype(jnp.float32)
        block_cluster, block_order = tail[:, 0:1], tail[:, 1:2] * 256.0 + tail[:, 2:3]
        col_best = jnp.full((rows, 1), -1.0, jnp.float32)
        for v in range(len(homed)):
            cosine = dots[j * rows : (j + 1) * rows, v * lanes : (v + 1) * lanes]
            cluster, order = visitor_meta[v]
            same = (block_cluster == cluster) & (cluster > 0)
            seen = jnp.where(same & (block_order < order), cosine, -1.0)
            row_best[v] = jnp.maximum(row_best[v], jnp.max(seen, axis=0, keepdims=True))
            if homed[v]:
                seen = jnp.where(same & (order < block_order), cosine, -1.0)
                col_best = jnp.maximum(col_best, jnp.max(seen, axis=1, keepdims=True))
        col_all = jnp.where(lane == j, col_best, col_all)
    for v in range(len(homed)):
        row_refs[v][:, :lanes] = row_best[v]
        if lanes < LANES:
            row_refs[v][:, lanes:] = jnp.full((1, LANES - lanes), -1.0, jnp.float32)
    if rows < LANES:
        fill = jnp.full((LANES - rows, LANES), -1.0, jnp.float32)
        col_all = jnp.concatenate([col_all, fill], axis=0)
    turned = col_all.T
    for j in range(len(pieces)):
        best = turned[j : j + 1, :]
        col_refs[j][...] = jnp.maximum(best, carry_refs[j][...]) if carried else best


def maxima(homed, visitors, blocks, carry=None):
    rows, width = sum(piece.shape[0] for piece in blocks[0]), visitors[0][0].shape[1] - LANES
    count, lanes = len(visitors), LANES if len(visitors) > 1 else rows
    row_best, col_best = None, []
    for first in range(0, len(blocks), PER_CALL):
        part = blocks[first : first + PER_CALL]
        operands = [piece for block in visitors + part for piece in block]
        operands += carry[first : first + PER_CALL] if carry else []
        scratch = [pltpu.VMEM((count * LANES, width), jnp.bfloat16)] if count > 1 else []
        best = pl.pallas_call(
            functools.partial(
                maxima_kernel,
                homed,
                [len(block) for block in visitors],
                [len(block) for block in part],
                carry is not None,
            ),
            in_specs=[VMEM] * len(operands),
            out_specs=[VMEM] * (count + len(part)),
            out_shape=[jax.ShapeDtypeStruct((1, LANES), jnp.float32)] * (count + len(part)),
            scratch_shapes=scratch + [pltpu.VMEM((len(part) * rows, count * lanes), jnp.float32)],
            compiler_params=pltpu.CompilerParams(vmem_limit_bytes=40 * 2**20),
            cost_estimate=pl.CostEstimate(
                flops=2 * len(part) * rows * count * LANES * width,
                bytes_accessed=2 * (len(part) + count) * rows * width,
                transcendentals=0,
            ),
        )(*operands)
        row, col_best = best[:count], col_best + list(best[count:])
        row_best = row if row_best is None else [jnp.maximum(a, b) for a, b in zip(row_best, row)]
    return row_best, col_best


def gather_plane(block, groups):
    half = block.shape[0] // 2
    blocks = {0: [block]}
    for s in range(1, groups):
        low, high = s & -s, 1 << (s.bit_length() - 1)
        if low == high:
            blocks[s] = [lax.ppermute(block, "group", flip(groups, s))]
            continue
        top, bottom = blocks[s ^ high], blocks[s ^ low]
        top = top[0][:half] if len(top) == 1 else top[0]
        bottom = bottom[0][half:] if len(bottom) == 1 else bottom[1]
        blocks[s] = [
            lax.ppermute(top, "group", flip(groups, high)),
            lax.ppermute(bottom, "group", flip(groups, low)),
        ]
    return blocks


def copy_kernel(value_ref, other_ref, out_ref):
    out_ref[...] = value_ref[...]


def copy_behind(value, other):
    return pl.pallas_call(
        copy_kernel,
        in_specs=[VMEM, VMEM],
        out_specs=VMEM,
        out_shape=jax.ShapeDtypeStruct(value.shape, value.dtype),
    )(value, other)


def swap(block):
    return lax.ppermute(block, "core", flip(2, 1))


def send_home(best, route):
    home = lax.ppermute(best, "z", [(b, a) for a, b in route])
    if len(route) == lax.axis_size("z"):
        return home
    here = lax.axis_index("z")
    sent = functools.reduce(jnp.logical_or, [here == a for a, _ in route])
    return jnp.where(sent, home, -1.0)


def local(embeddings, cluster_ids, order_index):
    rows = embeddings.shape[0]
    groups, length = lax.axis_size("group"), lax.axis_size("z")
    routes = [ring_pairs(length, shift) for shift in range(1, length // 2 + 1)]
    own = pack(embeddings, cluster_ids, order_index)
    arrived = [lax.ppermute(own, "z", route) for route in routes]
    blocks = list(gather_plane(own, groups).values())

    cut = rows * 2 // 3 // 16 * 16
    homed, visitors = [0, 0], [[own], [swap(own)]]
    for block in arrived[:-1]:
        homed += [1, 1]
        visitors += [[block], [swap(block[:cut]), swap(block[cut:])]]
    row, col = maxima(homed, visitors, blocks)
    bests = [row[0], swap(row[1])]
    for index, route in enumerate(routes[:-1]):
        merged = jnp.maximum(row[2 * index + 2], swap(row[2 * index + 3]))
        bests.append(send_home(merged, route))

    last = copy_behind(arrived[-1], bests[-1])
    row, col = maxima([1, 1], [[last], [swap(last)]], blocks, col)
    bests.append(col[0])
    bests += [lax.ppermute(col[s], "group", flip(groups, s)) for s in range(1, groups)]
    bests.append(send_home(jnp.maximum(row[0], swap(row[1])), routes[-1]))
    return functools.reduce(jnp.maximum, bests)[0, :rows]


def solution(mesh):
    groups, members = mesh.devices.shape
    fine = Mesh(mesh.devices.reshape(groups, members // 2, 2), AXES)
    placed = (P(AXES, None), P(AXES), P(AXES))
    return jax.shard_map(local, mesh=fine, in_specs=placed, out_specs=P(AXES), check_vma=False)
```

```python
import functools

import jax
import jax.numpy as jnp
from jax import lax
from jax.experimental import pallas as pl
from jax.experimental.pallas import tpu as pltpu
from jax.sharding import Mesh, PartitionSpec as P

AXES = ("group", "z", "core")
LANES = 128
CHUNK = 512
PER_CALL = 4
VMEM = pl.BlockSpec(memory_space=pltpu.VMEM)


def flip(count, bits):
    return [(k, k ^ bits) for k in range(count)]


def unit_rows(values):
    values = values.astype(jnp.float32)
    total = jnp.sum(values * values, axis=1, keepdims=True) + values.shape[1] * 1e-06
    return (values * lax.rsqrt(total)).astype(jnp.bfloat16)


def pack_kernel(rows_ref, cluster_ref, order_ref, block_ref):
    rows, width = rows_ref.shape
    block_ref[:, :width] = unit_rows(rows_ref[...])
    meta = jnp.concatenate(
        [
            cluster_ref[...].astype(jnp.float32) + 1.0,
            order_ref[...].astype(jnp.float32),
            jnp.zeros((6, rows), jnp.float32),
        ],
        axis=0,
    )
    if rows < LANES:
        meta = jnp.concatenate([meta, jnp.zeros((8, LANES - rows), jnp.float32)], axis=1)
    turned = meta.T[:rows]
    cluster, order = turned[:, 0:1], turned[:, 1:2]
    high = jnp.floor(order / 256.0)
    lane = lax.broadcasted_iota(jnp.int32, (rows, LANES), 1)
    tail = jnp.where(lane == 0, cluster, jnp.where(lane == 1, high, order - 256.0 * high))
    block_ref[:, width:] = jnp.where(lane < 3, tail, 0.0).astype(jnp.bfloat16)


def pack(rows, cluster_ids, order_index):
    count, width = rows.shape
    return pl.pallas_call(
        pack_kernel,
        in_specs=[VMEM] * 3,
        out_specs=VMEM,
        out_shape=jax.ShapeDtypeStruct((count, width + LANES), jnp.bfloat16),
        cost_estimate=pl.CostEstimate(
            flops=4 * count * width, bytes_accessed=4 * count * width, transcendentals=count
        ),
    )(rows, cluster_ids.reshape(1, count), order_index.reshape(1, count))


def maxima_kernel(homed, visitor_pieces, pieces, carried, *refs):
    take = list(refs)
    visitor_refs = [[take.pop(0) for _ in range(n)] for n in visitor_pieces]
    block_refs = [[take.pop(0) for _ in range(n)] for n in pieces]
    carry_refs = [take.pop(0) for _ in range(2)] if carried else []
    row_refs = [take.pop(0) for _ in homed]
    col_refs = [take.pop(0) for _ in range(2)]
    units, dots = take if len(homed) > 1 else (None, take[0])
    width = block_refs[0][0].shape[1] - LANES
    rows = sum(ref.shape[0] for ref in block_refs[0])
    lanes = LANES if units is not None else rows

    visitor_meta = []
    for v, parts in enumerate(visitor_refs):
        place, tail = v * LANES, []
        for ref in parts:
            if units is not None:
                units[place : place + ref.shape[0], :] = ref[:, :width]
            tail.append(ref[:, width:].astype(jnp.float32))
            place += ref.shape[0]
        spare = (v + 1) * LANES - place
        if spare:
            if units is not None:
                units[place : place + spare, :] = jnp.zeros((spare, width), jnp.bfloat16)
            tail.append(jnp.zeros((spare, LANES), jnp.float32))
        turned = jnp.concatenate(tail, axis=0).T
        visitor_meta.append((turned[0:1, :lanes], turned[1:2, :lanes] * 256.0 + turned[2:3, :lanes]))
    right = visitor_refs[0] if units is None else [units]
    flat = [ref for parts in block_refs for ref in parts]
    for k in range(0, width, CHUNK):
        left = jnp.concatenate([ref[:, k : k + CHUNK] for ref in flat], axis=0)
        part = lax.dot_general(
            left,
            jnp.concatenate([ref[:, k : k + CHUNK] for ref in right], axis=0),
            (((1,), (1,)), ((), ())),
            preferred_element_type=jnp.float32,
        )
        dots[...] = part if k == 0 else dots[...] + part

    row_best = [jnp.full((1, lanes), -1.0, jnp.float32) for _ in homed]
    lane = lax.broadcasted_iota(jnp.int32, (rows, LANES), 1)
    col_all = jnp.full((rows, LANES), -1.0, jnp.float32)
    for j, parts in enumerate(block_refs):
        tail = jnp.concatenate([ref[:, width:] for ref in parts], axis=0).astype(jnp.float32)
        block_cluster, block_order = tail[:, 0:1], tail[:, 1:2] * 256.0 + tail[:, 2:3]
        col_best = jnp.full((rows, 1), -1.0, jnp.float32)
        for v in range(len(homed)):
            cosine = dots[j * rows : (j + 1) * rows, v * lanes : (v + 1) * lanes]
            cluster, order = visitor_meta[v]
            same = (block_cluster == cluster) & (cluster > 0)
            seen = jnp.where(same & (block_order < order), cosine, -1.0)
            row_best[v] = jnp.maximum(row_best[v], jnp.max(seen, axis=0, keepdims=True))
            if homed[v]:
                seen = jnp.where(same & (order < block_order), cosine, -1.0)
                col_best = jnp.maximum(col_best, jnp.max(seen, axis=1, keepdims=True))
        col_all = jnp.where(lane == j, col_best, col_all)
    for v in range(len(homed)):
        row_refs[v][:, :lanes] = row_best[v]
        if lanes < LANES:
            row_refs[v][:, lanes:] = jnp.full((1, LANES - lanes), -1.0, jnp.float32)
    if rows < LANES:
        fill = jnp.full((LANES - rows, LANES), -1.0, jnp.float32)
        col_all = jnp.concatenate([col_all, fill], axis=0)
    turned = col_all.T
    for c, col_ref in enumerate(col_refs):
        best = turned[c * PER_CALL : (c + 1) * PER_CALL]
        col_ref[...] = jnp.maximum(best, carry_refs[c][...]) if carried else best


def maxima(homed, visitors, mine, others, carry=None):
    rows, width = sum(piece.shape[0] for piece in mine[0]), visitors[0][0].shape[1] - LANES
    count, lanes = len(visitors), LANES if len(visitors) > 1 else rows
    row_best, col_best = None, []
    for first in range(0, len(mine), PER_CALL):
        part = mine[first : first + PER_CALL] + others[first : first + PER_CALL]
        operands = [piece for block in visitors + part for piece in block]
        operands += carry[first // PER_CALL] if carry else []
        scratch = [pltpu.VMEM((count * LANES, width), jnp.bfloat16)] if count > 1 else []
        best = pl.pallas_call(
            functools.partial(
                maxima_kernel,
                homed,
                [len(block) for block in visitors],
                [len(block) for block in part],
                carry is not None,
            ),
            in_specs=[VMEM] * len(operands),
            out_specs=[VMEM] * (count + 2),
            out_shape=[jax.ShapeDtypeStruct((1, LANES), jnp.float32)] * count
            + [jax.ShapeDtypeStruct((PER_CALL, LANES), jnp.float32)] * 2,
            scratch_shapes=scratch + [pltpu.VMEM((len(part) * rows, count * lanes), jnp.float32)],
            compiler_params=pltpu.CompilerParams(vmem_limit_bytes=40 * 2**20),
            cost_estimate=pl.CostEstimate(
                flops=2 * len(part) * rows * count * LANES * width,
                bytes_accessed=2 * (len(part) + count) * rows * width,
                transcendentals=0,
            ),
        )(*operands)
        row = best[:count]
        row_best = row if row_best is None else [jnp.maximum(a, b) for a, b in zip(row_best, row)]
        col_best.append(list(best[count:]))
    return row_best, col_best


def copy_kernel(value_ref, other_ref, out_ref):
    out_ref[...] = value_ref[...]


def copy_behind(value, other):
    return pl.pallas_call(
        copy_kernel,
        in_specs=[VMEM, pl.BlockSpec(memory_space=pl.ANY)],
        out_specs=VMEM,
        out_shape=jax.ShapeDtypeStruct(value.shape, value.dtype),
    )(value, other)


def gather_plane(block, groups, other):
    half = block.shape[0] // 2
    blocks = {0: [block]}
    halves = block[:half], block[half:]
    for s in range(1, groups):
        low, high = s & -s, 1 << (s.bit_length() - 1)
        steps = (high, low)
        ways = halves if low == high else (copy_behind(blocks[s ^ high][0], other), blocks[s ^ low][1])
        blocks[s] = [lax.ppermute(p, "group", flip(groups, step)) for p, step in zip(ways, steps)]
    return blocks


def swap(block):
    return lax.ppermute(block, "core", flip(2, 1))


def send_home(best, route):
    home = lax.ppermute(best, "z", [(b, a) for a, b in route])
    if len(route) == lax.axis_size("z"):
        return home
    here = lax.axis_index("z")
    sent = functools.reduce(jnp.logical_or, [here == a for a, _ in route])
    return jnp.where(sent, home, -1.0)


def local(embeddings, cluster_ids, order_index):
    rows = embeddings.shape[0]
    groups, length = lax.axis_size("group"), lax.axis_size("z")
    own = pack(embeddings, cluster_ids, order_index)
    pieces, routes, arrived = [own], [], []
    for shift in range(1, length // 2 + 1):
        sources = range(length if 2 * shift < length else length // 2)
        routes.append([(a, (a + shift) % length) for a in sources])
        hops = [((a + shift - 1) % length, (a + shift) % length) for a in sources]
        pieces = [lax.ppermute(piece, "z", hops) for piece in pieces]
        arrived.append(pieces)
    across = swap(own)
    mine = list(gather_plane(own, groups, across).values())
    others = [[across]] + [[swap(part) for part in parts] for parts in mine[1:]]

    homed = [0] + [1] * (len(routes) - 1)
    row, col = maxima(homed, [[own]] + arrived[:-1], mine, others)
    bests = [row[0]] + [send_home(best, route) for best, route in zip(row[1:], routes)]
    row, col = maxima([1], arrived[-1:], mine, others, col)
    bests.append(send_home(row[0], routes[-1]))
    merged = [jnp.maximum(best, swap(other)) for best, other in col]
    for s in range(groups):
        best = merged[s // PER_CALL]
        if s:
            best = lax.ppermute(best, "group", flip(groups, s))
        bests.append(best[s % PER_CALL][None])
    return functools.reduce(jnp.maximum, bests)[0, :rows]


def solution(mesh):
    groups, members = mesh.devices.shape
    fine = Mesh(mesh.devices.reshape(groups, members // 2, 2), AXES)
    placed = (P(AXES, None), P(AXES), P(AXES))
    return jax.shard_map(local, mesh=fine, in_specs=placed, out_specs=P(AXES), check_vma=False)
```

```python
import functools

import jax
import jax.numpy as jnp
from jax import lax
from jax.experimental import pallas as pl
from jax.experimental.pallas import tpu as pltpu
from jax.sharding import Mesh, PartitionSpec as P

AXES = ("group", "z", "core")
LANES = 128
CHUNK = 512
PER_CALL = 4
VMEM = pl.BlockSpec(memory_space=pltpu.VMEM)


def flip(count, bits):
    return [(k, k ^ bits) for k in range(count)]


def unit_rows(values):
    values = values.astype(jnp.float32)
    total = jnp.sum(values * values, axis=1, keepdims=True) + values.shape[1] * 1e-06
    return (values * lax.rsqrt(total)).astype(jnp.bfloat16)


def lane_rows(first, second):
    count = first.shape[1]
    both = jnp.concatenate([first, second, jnp.zeros((6, count), jnp.float32)], axis=0)
    if count < LANES:
        both = jnp.concatenate([both, jnp.zeros((8, LANES - count), jnp.float32)], axis=1)
    return both


def pack_kernel(rows_ref, cluster_ref, order_ref, block_ref):
    rows, width = rows_ref.shape
    block_ref[:, :width] = unit_rows(rows_ref[...])
    meta = lane_rows(cluster_ref[...].astype(jnp.float32) + 1.0, order_ref[...].astype(jnp.float32))
    turned = meta.T[:rows]
    cluster, order = turned[:, 0:1], turned[:, 1:2]
    high = jnp.floor(order / 256.0)
    lane = lax.broadcasted_iota(jnp.int32, (rows, LANES), 1)
    tail = jnp.where(lane == 0, cluster, jnp.where(lane == 1, high, order - 256.0 * high))
    block_ref[:, width:] = jnp.where(lane < 3, tail, 0.0).astype(jnp.bfloat16)


def pack(rows, cluster_ids, order_index):
    count, width = rows.shape
    return pl.pallas_call(
        pack_kernel,
        in_specs=[VMEM] * 3,
        out_specs=VMEM,
        out_shape=jax.ShapeDtypeStruct((count, width + LANES), jnp.bfloat16),
        cost_estimate=pl.CostEstimate(
            flops=4 * count * width, bytes_accessed=4 * count * width, transcendentals=count
        ),
    )(rows, cluster_ids.reshape(1, count), order_index.reshape(1, count))


def maxima_kernel(homed, visitor_pieces, pieces, carried, *refs):
    take = list(refs)
    visitor_refs = [[take.pop(0) for _ in range(n)] for n in visitor_pieces]
    block_refs = [[take.pop(0) for _ in range(n)] for n in pieces]
    carry_refs = [take.pop(0) for _ in pieces] if carried else []
    row_refs = [take.pop(0) for _ in homed]
    col_refs = [take.pop(0) for _ in pieces]
    units, dots = take if len(homed) > 1 else (None, take[0])
    width = block_refs[0][0].shape[1] - LANES
    rows = sum(ref.shape[0] for ref in block_refs[0])
    lanes = LANES if units is not None else rows

    visitor_meta = []
    for v, parts in enumerate(visitor_refs):
        place, tail = v * LANES, []
        for ref in parts:
            if units is not None:
                units[place : place + ref.shape[0], :] = ref[:, :width]
            tail.append(ref[:, width:].astype(jnp.float32))
            place += ref.shape[0]
        spare = (v + 1) * LANES - place
        if spare:
            if units is not None:
                units[place : place + spare, :] = jnp.zeros((spare, width), jnp.bfloat16)
            tail.append(jnp.zeros((spare, LANES), jnp.float32))
        turned = jnp.concatenate(tail, axis=0).T
        visitor_meta.append((turned[0:1, :lanes], turned[1:2, :lanes] * 256.0 + turned[2:3, :lanes]))
    right = visitor_refs[0][0] if units is None else units
    flat = [ref for parts in block_refs for ref in parts]
    for k in range(0, width, CHUNK):
        left = jnp.concatenate([ref[:, k : k + CHUNK] for ref in flat], axis=0)
        part = lax.dot_general(
            left,
            right[:, k : k + CHUNK],
            (((1,), (1,)), ((), ())),
            preferred_element_type=jnp.float32,
        )
        dots[...] = part if k == 0 else dots[...] + part

    row_best = [jnp.full((1, lanes), -1.0, jnp.float32) for _ in homed]
    lane = lax.broadcasted_iota(jnp.int32, (rows, LANES), 1)
    col_all = jnp.full((rows, LANES), -1.0, jnp.float32)
    for j, parts in enumerate(block_refs):
        tail = jnp.concatenate([ref[:, width:] for ref in parts], axis=0).astype(jnp.float32)
        block_cluster, block_order = tail[:, 0:1], tail[:, 1:2] * 256.0 + tail[:, 2:3]
        col_best = jnp.full((rows, 1), -1.0, jnp.float32)
        for v in range(len(homed)):
            cosine = dots[j * rows : (j + 1) * rows, v * lanes : (v + 1) * lanes]
            cluster, order = visitor_meta[v]
            same = (block_cluster == cluster) & (cluster > 0)
            seen = jnp.where(same & (block_order < order), cosine, -1.0)
            row_best[v] = jnp.maximum(row_best[v], jnp.max(seen, axis=0, keepdims=True))
            if homed[v]:
                seen = jnp.where(same & (order < block_order), cosine, -1.0)
                col_best = jnp.maximum(col_best, jnp.max(seen, axis=1, keepdims=True))
        col_all = jnp.where(lane == j, col_best, col_all)
    for v in range(len(homed)):
        row_refs[v][:, :lanes] = row_best[v]
        if lanes < LANES:
            row_refs[v][:, lanes:] = jnp.full((1, LANES - lanes), -1.0, jnp.float32)
    if rows < LANES:
        fill = jnp.full((LANES - rows, LANES), -1.0, jnp.float32)
        col_all = jnp.concatenate([col_all, fill], axis=0)
    turned = col_all.T
    for j in range(len(pieces)):
        best = turned[j : j + 1, :]
        col_refs[j][...] = jnp.maximum(best, carry_refs[j][...]) if carried else best


def maxima(homed, visitors, blocks, carry=None):
    rows, width = sum(piece.shape[0] for piece in blocks[0]), visitors[0][0].shape[1] - LANES
    count, lanes = len(visitors), LANES if len(visitors) > 1 else rows
    row_best, col_best = None, []
    for first in range(0, len(blocks), PER_CALL):
        part = blocks[first : first + PER_CALL]
        operands = [piece for block in visitors + part for piece in block]
        operands += carry[first : first + PER_CALL] if carry else []
        scratch = [pltpu.VMEM((count * LANES, width), jnp.bfloat16)] if count > 1 else []
        best = pl.pallas_call(
            functools.partial(
                maxima_kernel,
                homed,
                [len(block) for block in visitors],
                [len(block) for block in part],
                carry is not None,
            ),
            in_specs=[VMEM] * len(operands),
            out_specs=[VMEM] * (count + len(part)),
            out_shape=[jax.ShapeDtypeStruct((1, LANES), jnp.float32)] * (count + len(part)),
            scratch_shapes=scratch + [pltpu.VMEM((len(part) * rows, count * lanes), jnp.float32)],
            compiler_params=pltpu.CompilerParams(vmem_limit_bytes=40 * 2**20),
            cost_estimate=pl.CostEstimate(
                flops=2 * len(part) * rows * count * LANES * width,
                bytes_accessed=2 * (len(part) + count) * rows * width,
                transcendentals=0,
            ),
        )(*operands)
        row, col_best = best[:count], col_best + list(best[count:])
        row_best = row if row_best is None else [jnp.maximum(a, b) for a, b in zip(row_best, row)]
    return row_best, col_best


def gather_plane(block, groups):
    half = block.shape[0] // 2
    blocks = {0: [block]}
    for s in range(1, groups):
        low, high = s & -s, 1 << (s.bit_length() - 1)
        if low == high:
            blocks[s] = [lax.ppermute(block, "group", flip(groups, s))]
            continue
        top, bottom = blocks[s ^ high], blocks[s ^ low]
        top = top[0][:half] if len(top) == 1 else top[0]
        bottom = bottom[0][half:] if len(bottom) == 1 else bottom[1]
        blocks[s] = [
            lax.ppermute(top, "group", flip(groups, high)),
            lax.ppermute(bottom, "group", flip(groups, low)),
        ]
    return blocks


def after(value, other):
    anywhere = pl.BlockSpec(memory_space=pl.ANY)
    return pl.pallas_call(
        lambda *refs: None,
        in_specs=[anywhere] * 2,
        out_specs=anywhere,
        out_shape=jax.ShapeDtypeStruct(value.shape, value.dtype),
        input_output_aliases={0: 0},
        cost_estimate=pl.CostEstimate(flops=0, bytes_accessed=0, transcendentals=0),
    )(value, other)


def swap(block):
    return lax.ppermute(block, "core", flip(2, 1))


def send_home(best, route):
    return lax.ppermute(best, "z", [(b, a) for a, b in route])


def finish_kernel(route, *refs):
    out_ref, last_ref = refs[-1], refs[-2]
    here = lax.axis_index("z")
    sent = functools.reduce(jnp.logical_or, [here == a for a, _ in route])
    best = jnp.where(sent, last_ref[...], -1.0)
    for ref in refs[:-2]:
        best = jnp.maximum(best, ref[...])
    out_ref[...] = best[0, : out_ref.shape[0]]


def finish(bests, route, rows):
    return pl.pallas_call(
        functools.partial(finish_kernel, route),
        in_specs=[VMEM] * len(bests),
        out_specs=VMEM,
        out_shape=jax.ShapeDtypeStruct((rows,), jnp.float32),
    )(*bests)


def local(embeddings, cluster_ids, order_index):
    rows = embeddings.shape[0]
    groups, length = lax.axis_size("group"), lax.axis_size("z")
    own = pack(embeddings, cluster_ids, order_index)
    block, routes, arrived = own, [], []
    for shift in range(1, length // 2 + 1):
        sources = range(length if 2 * shift < length else length // 2)
        routes.append([(a, (a + shift) % length) for a in sources])
        hops = [((a + shift - 1) % length, (a + shift) % length) for a in sources]
        block = lax.ppermute(block, "z", hops)
        arrived.append(block)
    blocks = list(gather_plane(own, groups).values())

    homed, visitors = [0, 0], [[own], [swap(own)]]
    for block in arrived[:-1]:
        homed += [1, 1]
        visitors += [[block], [swap(block)]]
    row, col = maxima(homed, visitors, blocks)
    bests = [row[0], swap(row[1])]
    for index, route in enumerate(routes[:-1]):
        merged = jnp.maximum(row[2 * index + 2], swap(row[2 * index + 3]))
        bests.append(send_home(merged, route))

    last = after(arrived[-1], bests[-1])
    other = swap(last)
    row, col = maxima([1], [[last]], blocks, col)
    other_row, col = maxima([1], [[other]], blocks, col)
    bests.append(col[0])
    bests += [lax.ppermute(col[s], "group", flip(groups, s)) for s in range(1, groups)]
    bests.append(send_home(jnp.maximum(row[0], swap(other_row[0])), routes[-1]))
    return finish(bests, routes[-1], rows)


def solution(mesh):
    groups, members = mesh.devices.shape
    fine = Mesh(mesh.devices.reshape(groups, members // 2, 2), AXES)
    placed = (P(AXES, None), P(AXES), P(AXES))
    return jax.shard_map(local, mesh=fine, in_specs=placed, out_specs=P(AXES), check_vma=False)
```

```python
import functools

import jax
import jax.numpy as jnp
from jax import lax
from jax.experimental import pallas as pl
from jax.experimental.pallas import tpu as pltpu
from jax.sharding import Mesh, PartitionSpec as P

AXES = ("group", "z", "core")
LANES = 128
CHUNK = 512
PER_CALL = 6
VMEM = pl.BlockSpec(memory_space=pltpu.VMEM)


def flip(count, bits):
    return [(k, k ^ bits) for k in range(count)]


def unit_rows(values):
    values = values.astype(jnp.float32)
    total = jnp.sum(values * values, axis=1, keepdims=True) + values.shape[1] * 1e-06
    return (values * lax.rsqrt(total)).astype(jnp.bfloat16)


def ring_pairs(length, shift):
    if 2 * shift < length:
        return [(k, (k + shift) % length) for k in range(length)]
    pairs = [(k, k + shift) for k in range(length // 2)]
    return [pair[:: 1 - 2 * (pair[0] % 2)] for pair in pairs]


def pack_kernel(rows_ref, cluster_ref, order_ref, block_ref):
    rows, width = rows_ref.shape
    block_ref[:, :width] = unit_rows(rows_ref[...])
    meta = jnp.concatenate(
        [
            cluster_ref[...].astype(jnp.float32) + 1.0,
            order_ref[...].astype(jnp.float32),
            jnp.zeros((6, rows), jnp.float32),
        ],
        axis=0,
    )
    if rows < LANES:
        meta = jnp.concatenate([meta, jnp.zeros((8, LANES - rows), jnp.float32)], axis=1)
    turned = meta.T[:rows]
    cluster, order = turned[:, 0:1], turned[:, 1:2]
    high = jnp.floor(order / 256.0)
    lane = lax.broadcasted_iota(jnp.int32, (rows, LANES), 1)
    tail = jnp.where(lane == 0, cluster, jnp.where(lane == 1, high, order - 256.0 * high))
    block_ref[:, width:] = jnp.where(lane < 3, tail, 0.0).astype(jnp.bfloat16)


def pack(rows, cluster_ids, order_index):
    count, width = rows.shape
    return pl.pallas_call(
        pack_kernel,
        in_specs=[VMEM] * 3,
        out_specs=VMEM,
        out_shape=jax.ShapeDtypeStruct((count, width + LANES), jnp.bfloat16),
        cost_estimate=pl.CostEstimate(
            flops=4 * count * width, bytes_accessed=4 * count * width, transcendentals=count
        ),
    )(rows, cluster_ids.reshape(1, count), order_index.reshape(1, count))


def maxima_kernel(visitors, pieces, carried, *refs):
    take = list(refs)
    visitor_refs = [take.pop(0) for _ in range(visitors)]
    block_refs = [[take.pop(0) for _ in range(n)] for n in pieces]
    carry_ref = take.pop(0) if carried else None
    row_ref, col_ref, units, dots = take
    width = units.shape[1]
    rows = visitor_refs[0].shape[0]

    meta = []
    for v, ref in enumerate(visitor_refs):
        place, tail = v * LANES, ref[:, width:].astype(jnp.float32)
        units[place : place + rows, :] = ref[:, :width]
        if rows < LANES:
            units[place + rows : place + LANES, :] = jnp.zeros((LANES - rows, width), jnp.bfloat16)
            tail = jnp.concatenate([tail, jnp.zeros((LANES - rows, LANES), jnp.float32)], axis=0)
        turned = tail.T
        meta.append((turned[0:1], turned[1:2] * 256.0 + turned[2:3]))
    flat = [ref for parts in block_refs for ref in parts]
    for k in range(0, width, CHUNK):
        left = jnp.concatenate([ref[:, k : k + CHUNK] for ref in flat], axis=0)
        part = lax.dot_general(
            left,
            units[:, k : k + CHUNK],
            (((1,), (1,)), ((), ())),
            preferred_element_type=jnp.float32,
        )
        dots[...] = part if k == 0 else dots[...] + part

    row_best = [jnp.full((1, LANES), -1.0, jnp.float32) for _ in meta]
    lane = lax.broadcasted_iota(jnp.int32, (rows, LANES), 1)
    col_all = jnp.full((rows, LANES), -1.0, jnp.float32)
    for j, parts in enumerate(block_refs):
        tail = jnp.concatenate([ref[:, width:] for ref in parts], axis=0).astype(jnp.float32)
        block_cluster, block_order = tail[:, 0:1], tail[:, 1:2] * 256.0 + tail[:, 2:3]
        col_best = jnp.full((rows, 1), -1.0, jnp.float32)
        for v, (cluster, order) in enumerate(meta):
            cosine = dots[j * rows : (j + 1) * rows, v * LANES : (v + 1) * LANES]
            same = (block_cluster == cluster) & (cluster > 0)
            seen = jnp.where(same & (block_order < order), cosine, -1.0)
            row_best[v] = jnp.maximum(row_best[v], jnp.max(seen, axis=0, keepdims=True))
            if v > 0:
                seen = jnp.where(same & (order < block_order), cosine, -1.0)
                col_best = jnp.maximum(col_best, jnp.max(seen, axis=1, keepdims=True))
        col_all = jnp.where(lane == j, col_best, col_all)
    for v, best in enumerate(row_best):
        row_ref[v : v + 1, :] = jnp.maximum(best, carry_ref[v : v + 1, :]) if carried else best
    if rows < LANES:
        fill = jnp.full((LANES - rows, LANES), -1.0, jnp.float32)
        col_all = jnp.concatenate([col_all, fill], axis=0)
    col_ref[...] = col_all.T[: len(pieces)]


def maxima(visitors, blocks, carry=None):
    rows, width = visitors[0].shape[0], visitors[0].shape[1] - LANES
    count, col_best = len(visitors), []
    for first in range(0, len(blocks), PER_CALL):
        part = blocks[first : first + PER_CALL]
        operands = list(visitors) + [piece for block in part for piece in block]
        operands += [] if carry is None else [carry]
        carry, col = pl.pallas_call(
            functools.partial(
                maxima_kernel, count, [len(block) for block in part], carry is not None
            ),
            in_specs=[VMEM] * len(operands),
            out_specs=[VMEM] * 2,
            out_shape=[
                jax.ShapeDtypeStruct((count, LANES), jnp.float32),
                jax.ShapeDtypeStruct((len(part), LANES), jnp.float32),
            ],
            scratch_shapes=[
                pltpu.VMEM((count * LANES, width), jnp.bfloat16),
                pltpu.VMEM((len(part) * rows, count * LANES), jnp.float32),
            ],
            compiler_params=pltpu.CompilerParams(vmem_limit_bytes=40 * 2**20),
            cost_estimate=pl.CostEstimate(
                flops=2 * len(part) * rows * count * LANES * width,
                bytes_accessed=2 * (len(part) + count) * rows * width,
                transcendentals=0,
            ),
        )(*operands)
        col_best.append(col)
    return carry, jnp.concatenate(col_best)


def join_kernel(*refs):
    top_ref, bottom_ref, out_ref = refs[-3:]
    half = top_ref.shape[0]
    out_ref[:half] = top_ref[...]
    out_ref[half:] = bottom_ref[...]


def join(top, bottom, others):
    anywhere = pl.BlockSpec(memory_space=pl.ANY)
    rows, width = 2 * top.shape[0], top.shape[1]
    return pl.pallas_call(
        join_kernel,
        in_specs=[anywhere] * len(others) + [VMEM] * 2,
        out_specs=VMEM,
        out_shape=jax.ShapeDtypeStruct((rows, width), top.dtype),
        cost_estimate=pl.CostEstimate(flops=0, bytes_accessed=4 * rows * width, transcendentals=0),
    )(*others, top, bottom)


def cut_kernel(value_ref, other_ref, out_ref):
    out_ref[...] = value_ref[: out_ref.shape[0]]


def top_half(value, other):
    return pl.pallas_call(
        cut_kernel,
        in_specs=[VMEM, pl.BlockSpec(memory_space=pl.ANY)],
        out_specs=VMEM,
        out_shape=jax.ShapeDtypeStruct((value.shape[0] // 2, value.shape[1]), value.dtype),
    )(value, other)


def gather_plane(block, groups, other):
    half = block.shape[0] // 2
    blocks = {0: [block]}
    for s in range(1, groups):
        low, high = s & -s, 1 << (s.bit_length() - 1)
        if low == high:
            blocks[s] = [lax.ppermute(block, "group", flip(groups, s))]
            continue
        top, bottom = blocks[s ^ high], blocks[s ^ low]
        top = top_half(top[0], other) if len(top) == 1 else top[0]
        bottom = bottom[0][half:] if len(bottom) == 1 else bottom[1]
        blocks[s] = [
            lax.ppermute(top, "group", flip(groups, high)),
            lax.ppermute(bottom, "group", flip(groups, low)),
        ]
    return blocks


def swap(block):
    return lax.ppermute(block, "core", flip(2, 1))


def local(embeddings, cluster_ids, order_index):
    rows = embeddings.shape[0]
    groups, length = lax.axis_size("group"), lax.axis_size("z")
    routes = [ring_pairs(length, shift) for shift in range(1, length // 2 + 1)]
    own = pack(embeddings, cluster_ids, order_index)
    visitors = [own] + [lax.ppermute(own, "z", route) for route in routes]
    across = swap(own)
    plane = gather_plane(own, groups, across)

    last = plane.pop(groups - 1)
    blocks = [[own], [across]]
    for s in range(1, groups - 1):
        blocks += [plane[s], [swap(part) for part in plane[s]]]
    last = join(*last, visitors[1:])
    row, col = maxima(visitors, blocks)
    row, last_col = maxima(visitors, [[last], [swap(last)]], row)
    col = jnp.concatenate([col, last_col]).reshape(groups, 2, LANES)
    col = jnp.maximum(col[:, 0], swap(col[:, 1]))

    best = row[0]
    for index, route in enumerate(routes):
        home = lax.ppermute(row[index + 1], "z", [(b, a) for a, b in route])
        if len(route) < length:
            here = lax.axis_index("z")
            sent = functools.reduce(jnp.logical_or, [here == a for a, _ in route])
            home = jnp.where(sent, home, -1.0)
        best = jnp.maximum(best, home)
    for s in range(groups):
        home = lax.ppermute(col, "group", flip(groups, s)) if s else col
        best = jnp.maximum(best, home[s])
    return best[:rows]


def solution(mesh):
    groups, members = mesh.devices.shape
    fine = Mesh(mesh.devices.reshape(groups, members // 2, 2), AXES)
    placed = (P(AXES, None), P(AXES), P(AXES))
    return jax.shard_map(local, mesh=fine, in_specs=placed, out_specs=P(AXES), check_vma=False)
```

```python
import functools

import jax
import jax.numpy as jnp
from jax import lax
from jax.experimental import pallas as pl
from jax.experimental.pallas import tpu as pltpu
from jax.sharding import Mesh, PartitionSpec as P

AXES = ("group", "z", "core")
LANES = 128
CHUNK = 512
CALL = 8
VMEM = pl.BlockSpec(memory_space=pltpu.VMEM)


def flip(count, bits):
    return [(k, k ^ bits) for k in range(count)]


def unit_rows(values):
    values = values.astype(jnp.float32)
    total = jnp.sum(values * values, axis=1, keepdims=True) + values.shape[1] * 1e-06
    return (values * lax.rsqrt(total)).astype(jnp.bfloat16)


def ring_pairs(length, shift):
    if 2 * shift < length:
        return [(k, (k + shift) % length) for k in range(length)]
    pairs = [(k, k + shift) for k in range(length // 2)]
    return [pair[:: 1 - 2 * (pair[0] % 2)] for pair in pairs]


def gather_plane(block, groups):
    half = block.shape[0] // 2
    blocks = {0: [block]}
    for s in range(1, groups):
        low, high = s & -s, 1 << (s.bit_length() - 1)
        if low == high:
            blocks[s] = [lax.ppermute(block, "group", flip(groups, s))]
            continue
        top, bottom = blocks[s ^ high], blocks[s ^ low]
        top = top[0][:half] if len(top) == 1 else top[0]
        bottom = bottom[0][half:] if len(bottom) == 1 else bottom[1]
        blocks[s] = [
            lax.ppermute(top, "group", flip(groups, high)),
            lax.ppermute(bottom, "group", flip(groups, low)),
        ]
    return blocks


def swap(block):
    return lax.ppermute(block, "core", flip(2, 1))


def pack_kernel(*refs):
    both_ref, own_ref = refs[6:]
    rows, width = refs[0].shape
    core = lax.axis_index("core")
    for index, (rows_ref, cluster_ref, order_ref) in enumerate((refs[:3], refs[3:6])):
        unit = unit_rows(rows_ref[...])
        meta = jnp.concatenate(
            [
                cluster_ref[...].astype(jnp.float32) + 1.0,
                order_ref[...].astype(jnp.float32),
                jnp.zeros((6, rows), jnp.float32),
            ],
            axis=0,
        )
        if rows < LANES:
            meta = jnp.concatenate([meta, jnp.zeros((8, LANES - rows), jnp.float32)], axis=1)
        turned = meta.T[:rows]
        cluster, order = turned[:, 0:1], turned[:, 1:2]
        high = jnp.floor(order / 256.0)
        lane = lax.broadcasted_iota(jnp.int32, (rows, LANES), 1)
        tail = jnp.where(lane == 0, cluster, jnp.where(lane == 1, high, order - 256.0 * high))
        tail = jnp.where(lane < 3, tail, 0.0).astype(jnp.bfloat16)
        place = pl.ds(pl.multiple_of((core ^ index) * rows, 16), rows)
        both_ref[place, :width] = unit
        both_ref[place, width:] = tail
        if index == 0:
            own_ref[:, :width] = unit
            own_ref[:, width:] = tail


def pack(rows, cluster_ids, order_index):
    count, width = rows.shape
    operands = [rows, cluster_ids, order_index]
    operands += [swap(operand) for operand in operands]
    operands = [operand.reshape(-1, operand.shape[-1]) for operand in operands]
    return pl.pallas_call(
        pack_kernel,
        in_specs=[VMEM] * 6,
        out_specs=[VMEM] * 2,
        out_shape=[
            jax.ShapeDtypeStruct((2 * count, width + LANES), jnp.bfloat16),
            jax.ShapeDtypeStruct((count, width + LANES), jnp.bfloat16),
        ],
        compiler_params=pltpu.CompilerParams(vmem_limit_bytes=40 * 2**20),
        cost_estimate=pl.CostEstimate(
            flops=8 * count * width, bytes_accessed=10 * count * width, transcendentals=count
        ),
    )(*operands)


def own_kernel(*refs):
    both_ref, block_refs, (row_ref, *scratch) = refs[0], refs[1:-3], refs[-3:]
    (first, second), _ = best_pairs([both_ref], block_refs, False, *scratch)
    row_ref[...] = jnp.where(lax.axis_index("core") == 0, first, second)


def visit_kernel(visitors, arrays, first, *refs):
    block_refs = refs[visitors : visitors + arrays]
    row_ref, mine_ref, other_ref, *scratch = refs[visitors + arrays + 1 :]
    rows, cols = best_pairs(refs[:visitors], block_refs, True, *scratch)
    for v, best in enumerate(rows):
        row_ref[v : v + 1, :] = best
    for j, best in enumerate(cols):
        if first and j < 2:
            best = jnp.where(lax.axis_index("core") == 0, best, cols[1 - j])
        (mine_ref, other_ref)[j % 2][j // 2 : j // 2 + 1, :] = best


def best_pairs(visitor_refs, block_refs, homed, units, dots):
    width = units.shape[1]
    rows = visitor_refs[0].shape[0] // 2

    meta = []
    for v in range(2 * len(visitor_refs)):
        place, source = v * LANES, pl.ds(v % 2 * rows, rows)
        units[place : place + rows, :] = visitor_refs[v // 2][source, :width]
        tail = visitor_refs[v // 2][source, width:].astype(jnp.float32)
        if rows < LANES:
            units[place + rows : place + LANES, :] = jnp.zeros((LANES - rows, width), jnp.bfloat16)
            tail = jnp.concatenate([tail, jnp.zeros((LANES - rows, LANES), jnp.float32)], axis=0)
        turned = tail.T
        meta.append((turned[0:1], turned[1:2] * 256.0 + turned[2:3]))
    for k in range(0, width, CHUNK):
        left = jnp.concatenate([ref[:, k : k + CHUNK] for ref in block_refs], axis=0)
        part = lax.dot_general(
            left,
            units[:, k : k + CHUNK],
            (((1,), (1,)), ((), ())),
            preferred_element_type=jnp.float32,
        )
        dots[...] = part if k == 0 else dots[...] + part

    tails = jnp.concatenate([ref[:, width:] for ref in block_refs], axis=0).astype(jnp.float32)
    row_best = [jnp.full((1, LANES), -1.0, jnp.float32) for _ in meta]
    lane = lax.broadcasted_iota(jnp.int32, (rows, LANES), 1)
    col_all = jnp.full((rows, LANES), -1.0, jnp.float32)
    for j in range(dots.shape[0] // rows):
        tail = tails[j * rows : (j + 1) * rows]
        block_cluster, block_order = tail[:, 0:1], tail[:, 1:2] * 256.0 + tail[:, 2:3]
        col_best = jnp.full((rows, 1), -1.0, jnp.float32)
        for v, (cluster, order) in enumerate(meta):
            cosine = dots[j * rows : (j + 1) * rows, v * LANES : (v + 1) * LANES]
            same = (block_cluster == cluster) & (cluster > 0)
            seen = jnp.where(same & (block_order < order), cosine, -1.0)
            row_best[v] = jnp.maximum(row_best[v], jnp.max(seen, axis=0, keepdims=True))
            if homed:
                seen = jnp.where(same & (order < block_order), cosine, -1.0)
                col_best = jnp.maximum(col_best, jnp.max(seen, axis=1, keepdims=True))
        col_all = jnp.where(lane == j, col_best, col_all)
    if not homed:
        return row_best, None
    if rows < LANES:
        fill = jnp.full((LANES - rows, LANES), -1.0, jnp.float32)
        col_all = jnp.concatenate([col_all, fill], axis=0)
    turned = col_all.T
    return row_best, [turned[j : j + 1] for j in range(dots.shape[0] // rows)]


def call(kernel, operands, count, out_rows, total):
    width = operands[0].shape[1] - LANES
    return pl.pallas_call(
        kernel,
        in_specs=[VMEM] * len(operands),
        out_specs=[VMEM] * len(out_rows),
        out_shape=[jax.ShapeDtypeStruct((n, LANES), jnp.float32) for n in out_rows],
        scratch_shapes=[
            pltpu.VMEM((count * LANES, width), jnp.bfloat16),
            pltpu.VMEM((total, count * LANES), jnp.float32),
        ],
        compiler_params=pltpu.CompilerParams(vmem_limit_bytes=40 * 2**20),
        cost_estimate=pl.CostEstimate(
            flops=2 * total * count * LANES * width,
            bytes_accessed=2 * (total + count * LANES) * width,
            transcendentals=0,
        ),
    )(*operands)


def local(embeddings, cluster_ids, order_index):
    rows = embeddings.shape[0]
    groups, length = lax.axis_size("group"), lax.axis_size("z")
    z, core = lax.axis_index("z"), lax.axis_index("core")
    both, own = pack(embeddings, cluster_ids, order_index)

    routes = [ring_pairs(length, shift) for shift in range(1, length // 2 + 1)]
    trips = []
    for first in range(0, len(routes), 2):
        ways = enumerate(routes[first : first + 2])
        trips.append([(2 * a + way, 2 * b + way) for way, route in ways for a, b in route])
    visitors = [lax.ppermute(both, ("z", "core"), trip) for trip in trips]

    plane = gather_plane(own, groups)
    parts = [both]
    for s in range(1, groups):
        parts += [*plane[s], *(swap(part) for part in plane[s])]
    chunks, size = [[]], 0
    for part in parts:
        if size == CALL * rows:
            chunks, size = chunks + [[]], 0
        chunks[-1].append(part)
        size += part.shape[0]

    bests, answers = [], []
    for chunk in chunks:
        total = sum(part.shape[0] for part in chunk)
        bests += call(own_kernel, [both, *chunk], 2, [1], total)
    for index, chunk in enumerate(chunks):
        total = sum(part.shape[0] for part in chunk)
        kernel = functools.partial(visit_kernel, len(visitors), len(chunk), index == 0)
        count, half = 2 * len(visitors), total // rows // 2
        operands = [*visitors, *chunk, bests[index]]
        answers.append(call(kernel, operands, count, [count, half, half], total))
    home = functools.reduce(jnp.maximum, [answer[0] for answer in answers])
    for index, trip in enumerate(trips):
        part = home[2 * index : 2 * index + 2] if len(trips) > 1 else home
        back = lax.ppermute(part, ("z", "core"), [(b, a) for a, b in trip])
        for here, best in ((2 * z + core, back), (2 * z + (core ^ 1), swap(back))):
            sent = functools.reduce(jnp.logical_or, [here == a for a, _ in trip])
            bests.append(jnp.where(sent, jnp.where(core == 0, best[0:1], best[1:2]), -1.0))
    for index, (_, mine, other) in enumerate(answers):
        merged = jnp.maximum(mine, swap(other))
        for row in range(CALL // 2):
            s = index * CALL // 2 + row
            got = lax.ppermute(merged, "group", flip(groups, s)) if s else merged
            bests.append(got[row : row + 1])
    return functools.reduce(jnp.maximum, bests)[0, :rows]


def solution(mesh):
    groups, members = mesh.devices.shape
    fine = Mesh(mesh.devices.reshape(groups, members // 2, 2), AXES)
    placed = (P(AXES, None), P(AXES), P(AXES))
    return jax.shard_map(local, mesh=fine, in_specs=placed, out_specs=P(AXES), check_vma=False)
```

```python
import functools

import jax
import jax.numpy as jnp
from jax import lax
from jax.experimental import pallas as pl
from jax.experimental.pallas import tpu as pltpu
from jax.sharding import Mesh, PartitionSpec as P

AXES = ("group", "z", "core")
LANES = 128
CHUNK = 512
CALL = 8
PARTS = 3
VMEM = pl.BlockSpec(memory_space=pltpu.VMEM)


def flip(count, bits):
    return [(k, k ^ bits) for k in range(count)]


def unit_rows(values):
    values = values.astype(jnp.float32)
    total = jnp.sum(values * values, axis=1, keepdims=True) + values.shape[1] * 1e-06
    return (values * lax.rsqrt(total)).astype(jnp.bfloat16)


def ring_pairs(length, shift):
    if 2 * shift < length:
        return [(k, (k + shift) % length) for k in range(length)]
    pairs = [(k, k + shift) for k in range(length // 2)]
    return [pair[:: 1 - 2 * (pair[0] % 2)] for pair in pairs]


def gather_plane(block, groups):
    half = block.shape[0] // 2
    blocks = {0: [block]}
    for s in range(1, groups):
        low, high = s & -s, 1 << (s.bit_length() - 1)
        if low == high:
            blocks[s] = [lax.ppermute(block, "group", flip(groups, s))]
            continue
        top, bottom = blocks[s ^ high], blocks[s ^ low]
        top = top[0][:half] if len(top) == 1 else top[0]
        bottom = bottom[0][half:] if len(bottom) == 1 else bottom[1]
        blocks[s] = [
            lax.ppermute(top, "group", flip(groups, high)),
            lax.ppermute(bottom, "group", flip(groups, low)),
        ]
    return blocks


def swap(block):
    return lax.ppermute(block, "core", flip(2, 1))


def pack_kernel(rows_ref, cluster_ref, order_ref, block_ref, raw, ids, arrived):
    rows, width = raw.shape
    step = rows // PARTS
    parts = [pl.ds(index * step, step) for index in range(PARTS)]
    copies = [
        pltpu.make_async_copy(cluster_ref, ids.at[0], arrived.at[PARTS]),
        pltpu.make_async_copy(order_ref, ids.at[1], arrived.at[PARTS + 1]),
    ]
    for index, part in enumerate(parts):
        copies.append(
            pltpu.make_async_copy(rows_ref.at[part], raw.at[part], arrived.at[index])
        )
    for copy in copies:
        copy.start()
    for copy in copies[:2]:
        copy.wait()
    meta = jnp.concatenate(
        [
            ids[0].astype(jnp.float32) + 1.0,
            ids[1].astype(jnp.float32),
            jnp.zeros((6, rows), jnp.float32),
        ],
        axis=0,
    )
    if rows < LANES:
        meta = jnp.concatenate([meta, jnp.zeros((8, LANES - rows), jnp.float32)], axis=1)
    turned = meta.T[:rows]
    cluster, order = turned[:, 0:1], turned[:, 1:2]
    high = jnp.floor(order / 256.0)
    lane = lax.broadcasted_iota(jnp.int32, (rows, LANES), 1)
    tail = jnp.where(lane == 0, cluster, jnp.where(lane == 1, high, order - 256.0 * high))
    block_ref[:, width:] = jnp.where(lane < 3, tail, 0.0).astype(jnp.bfloat16)
    for part, copy in zip(parts, copies[2:]):
        copy.wait()
        block_ref[part, :width] = unit_rows(raw[part])


def pack(rows, cluster_ids, order_index):
    count, width = rows.shape
    return pl.pallas_call(
        pack_kernel,
        in_specs=[pl.BlockSpec(memory_space=pl.ANY)] * 3,
        out_specs=VMEM,
        out_shape=jax.ShapeDtypeStruct((count, width + LANES), jnp.bfloat16),
        scratch_shapes=[
            pltpu.VMEM((count, width), jnp.bfloat16),
            pltpu.VMEM((2, 1, count), jnp.int32),
            pltpu.SemaphoreType.DMA((PARTS + 2,)),
        ],
        cost_estimate=pl.CostEstimate(
            flops=4 * count * width, bytes_accessed=4 * count * width, transcendentals=count
        ),
    )(rows, cluster_ids.reshape(1, count), order_index.reshape(1, count))


def pair_kernel(own_ref, other_ref, both_ref):
    rows = own_ref.shape[0]
    core = lax.axis_index("core")
    both_ref[pl.ds(pl.multiple_of(core * rows, 16), rows), :] = own_ref[...]
    both_ref[pl.ds(pl.multiple_of((core ^ 1) * rows, 16), rows), :] = other_ref[...]


def pair(own, other):
    rows, width = own.shape
    return pl.pallas_call(
        pair_kernel,
        in_specs=[VMEM] * 2,
        out_specs=VMEM,
        out_shape=jax.ShapeDtypeStruct((2 * rows, width), own.dtype),
        cost_estimate=pl.CostEstimate(flops=0, bytes_accessed=8 * rows * width, transcendentals=0),
    )(own, other)


def own_kernel(*refs):
    row_ref, *scratch = refs[-3:]
    best, _ = best_of(refs[:1], refs[1:-3], refs[0].shape[0], False, *scratch)
    row_ref[...] = best[0]


def visit_kernel(visitors, arrays, *refs):
    block_refs = refs[visitors : visitors + arrays]
    row_ref, mine_ref, other_ref, *scratch = refs[visitors + arrays + 1 :]
    bests, cols = best_of(refs[:visitors], block_refs, refs[0].shape[0] // 2, True, *scratch)
    for v, best in enumerate(bests):
        row_ref[v : v + 1, :] = best
    for j, best in enumerate(cols):
        (mine_ref, other_ref)[j % 2][j // 2 : j // 2 + 1, :] = best


def best_of(visitor_refs, block_refs, rows, homed, units, dots):
    width = units.shape[1]

    meta = []
    for ref in visitor_refs:
        for source in range(0, ref.shape[0], rows):
            place, source = len(meta) * LANES, pl.ds(source, rows)
            units[place : place + rows, :] = ref[source, :width]
            tail = ref[source, width:].astype(jnp.float32)
            if rows < LANES:
                spare = LANES - rows
                units[place + rows : place + LANES, :] = jnp.zeros((spare, width), jnp.bfloat16)
                tail = jnp.concatenate([tail, jnp.zeros((spare, LANES), jnp.float32)], axis=0)
            turned = tail.T
            meta.append((turned[0:1], turned[1:2] * 256.0 + turned[2:3]))
    for k in range(0, width, CHUNK):
        left = jnp.concatenate([ref[:, k : k + CHUNK] for ref in block_refs], axis=0)
        part = lax.dot_general(
            left,
            units[:, k : k + CHUNK],
            (((1,), (1,)), ((), ())),
            preferred_element_type=jnp.float32,
        )
        dots[...] = part if k == 0 else dots[...] + part

    tails = jnp.concatenate([ref[:, width:] for ref in block_refs], axis=0).astype(jnp.float32)
    row_best = [jnp.full((1, LANES), -1.0, jnp.float32) for _ in meta]
    lane = lax.broadcasted_iota(jnp.int32, (rows, LANES), 1)
    col_all = jnp.full((rows, LANES), -1.0, jnp.float32)
    for j in range(dots.shape[0] // rows):
        tail = tails[j * rows : (j + 1) * rows]
        block_cluster, block_order = tail[:, 0:1], tail[:, 1:2] * 256.0 + tail[:, 2:3]
        col_best = jnp.full((rows, 1), -1.0, jnp.float32)
        for v, (cluster, order) in enumerate(meta):
            cosine = dots[j * rows : (j + 1) * rows, v * LANES : (v + 1) * LANES]
            same = (block_cluster == cluster) & (cluster > 0)
            seen = jnp.where(same & (block_order < order), cosine, -1.0)
            row_best[v] = jnp.maximum(row_best[v], jnp.max(seen, axis=0, keepdims=True))
            if homed:
                seen = jnp.where(same & (order < block_order), cosine, -1.0)
                col_best = jnp.maximum(col_best, jnp.max(seen, axis=1, keepdims=True))
        col_all = jnp.where(lane == j, col_best, col_all)
    if not homed:
        return row_best, None
    if rows < LANES:
        fill = jnp.full((LANES - rows, LANES), -1.0, jnp.float32)
        col_all = jnp.concatenate([col_all, fill], axis=0)
    turned = col_all.T
    return row_best, [turned[j : j + 1] for j in range(dots.shape[0] // rows)]


def call(kernel, operands, count, out_rows, total):
    width = operands[0].shape[1] - LANES
    return pl.pallas_call(
        kernel,
        in_specs=[VMEM] * len(operands),
        out_specs=[VMEM] * len(out_rows),
        out_shape=[jax.ShapeDtypeStruct((n, LANES), jnp.float32) for n in out_rows],
        scratch_shapes=[
            pltpu.VMEM((count * LANES, width), jnp.bfloat16),
            pltpu.VMEM((total, count * LANES), jnp.float32),
        ],
        compiler_params=pltpu.CompilerParams(vmem_limit_bytes=40 * 2**20),
        cost_estimate=pl.CostEstimate(
            flops=2 * total * count * LANES * width,
            bytes_accessed=2 * (total + count * LANES) * width,
            transcendentals=0,
        ),
    )(*operands)


def local(embeddings, cluster_ids, order_index):
    rows = embeddings.shape[0]
    groups, length = lax.axis_size("group"), lax.axis_size("z")
    z, core = lax.axis_index("z"), lax.axis_index("core")
    own = pack(embeddings, cluster_ids, order_index)
    other = swap(own)
    both = pair(own, other)

    routes = [ring_pairs(length, shift) for shift in range(1, length // 2 + 1)]
    trips = []
    for first in range(0, len(routes), 2):
        ways = enumerate(routes[first : first + 2])
        trips.append([(2 * a + way, 2 * b + way) for way, route in ways for a, b in route])
    visitors = [lax.ppermute(both, ("z", "core"), trip) for trip in trips]

    plane = gather_plane(own, groups)
    parts = [own, other]
    for s in range(1, groups):
        parts += [*plane[s], *(swap(part) for part in plane[s])]
    chunks, size = [[]], 0
    for part in parts:
        if size == CALL * rows:
            chunks, size = chunks + [[]], 0
        chunks[-1].append(part)
        size += part.shape[0]

    bests, answers = [], []
    for chunk in chunks:
        total = sum(part.shape[0] for part in chunk)
        bests += call(own_kernel, [own, *chunk], 1, [1], total)
    for index, chunk in enumerate(chunks):
        total = sum(part.shape[0] for part in chunk)
        kernel = functools.partial(visit_kernel, len(visitors), len(chunk))
        count, half = 2 * len(visitors), total // rows // 2
        operands = [*visitors, *chunk, bests[index]]
        answers.append(call(kernel, operands, count, [count, half, half], total))
    home = functools.reduce(jnp.maximum, [answer[0] for answer in answers])
    for index, trip in enumerate(trips):
        part = home[2 * index : 2 * index + 2] if len(trips) > 1 else home
        back = lax.ppermute(part, ("z", "core"), [(b, a) for a, b in trip])
        for here, best in ((2 * z + core, back), (2 * z + (core ^ 1), swap(back))):
            sent = functools.reduce(jnp.logical_or, [here == a for a, _ in trip])
            bests.append(jnp.where(sent, jnp.where(core == 0, best[0:1], best[1:2]), -1.0))
    for index, (_, mine, other) in enumerate(answers):
        merged = jnp.maximum(mine, swap(other))
        for row in range(CALL // 2):
            s = index * CALL // 2 + row
            got = lax.ppermute(merged, "group", flip(groups, s)) if s else merged
            bests.append(got[row : row + 1])
    return functools.reduce(jnp.maximum, bests)[0, :rows]


def solution(mesh):
    groups, members = mesh.devices.shape
    fine = Mesh(mesh.devices.reshape(groups, members // 2, 2), AXES)
    placed = (P(AXES, None), P(AXES), P(AXES))
    return jax.shard_map(local, mesh=fine, in_specs=placed, out_specs=P(AXES), check_vma=False)
```

```python
import functools

import jax
import jax.numpy as jnp
from jax import lax
from jax.experimental import pallas as pl
from jax.experimental.pallas import tpu as pltpu
from jax.sharding import Mesh, PartitionSpec as P

AXES = ("group", "z", "core")
LANES = 128
CHUNK = 512
CALL = 8
PARTS = 3
VMEM = pl.BlockSpec(memory_space=pltpu.VMEM)


def flip(count, bits):
    return [(k, k ^ bits) for k in range(count)]


def unit_rows(values):
    values = values.astype(jnp.float32)
    total = jnp.sum(values * values, axis=1, keepdims=True) + values.shape[1] * 1e-06
    return (values * lax.rsqrt(total)).astype(jnp.bfloat16)


def ring_pairs(length, shift):
    if 2 * shift < length:
        return [(k, (k + shift) % length) for k in range(length)]
    pairs = [(k, k + shift) for k in range(length // 2)]
    return [pair[:: 1 - 2 * (pair[0] % 2)] for pair in pairs]


def gather_plane(block, groups):
    half = block.shape[0] // 2
    blocks = {0: [block]}
    for s in range(1, groups):
        low, high = s & -s, 1 << (s.bit_length() - 1)
        if low == high:
            blocks[s] = [lax.ppermute(block, "group", flip(groups, s))]
            continue
        top, bottom = blocks[s ^ high], blocks[s ^ low]
        top = top[0][:half] if len(top) == 1 else top[0]
        bottom = bottom[0][half:] if len(bottom) == 1 else bottom[1]
        blocks[s] = [
            lax.ppermute(top, "group", flip(groups, high)),
            lax.ppermute(bottom, "group", flip(groups, low)),
        ]
    return blocks


def swap(block):
    return lax.ppermute(block, "core", flip(2, 1))


def pack_kernel(rows_ref, cluster_ref, order_ref, block_ref, raw, ids, arrived):
    rows, width = raw.shape
    step = rows // PARTS
    parts = [pl.ds(index * step, step) for index in range(PARTS)]
    copies = [
        pltpu.make_async_copy(cluster_ref, ids.at[0], arrived.at[PARTS]),
        pltpu.make_async_copy(order_ref, ids.at[1], arrived.at[PARTS + 1]),
    ]
    for index, part in enumerate(parts):
        copies.append(
            pltpu.make_async_copy(rows_ref.at[part], raw.at[part], arrived.at[index])
        )
    for copy in copies:
        copy.start()
    for copy in copies[:2]:
        copy.wait()
    meta = jnp.concatenate(
        [
            ids[0].astype(jnp.float32) + 1.0,
            ids[1].astype(jnp.float32),
            jnp.zeros((6, rows), jnp.float32),
        ],
        axis=0,
    )
    if rows < LANES:
        meta = jnp.concatenate([meta, jnp.zeros((8, LANES - rows), jnp.float32)], axis=1)
    turned = meta.T[:rows]
    cluster, order = turned[:, 0:1], turned[:, 1:2]
    high = jnp.floor(order / 256.0)
    lane = lax.broadcasted_iota(jnp.int32, (rows, LANES), 1)
    tail = jnp.where(lane == 0, cluster, jnp.where(lane == 1, high, order - 256.0 * high))
    block_ref[:, width:] = jnp.where(lane < 3, tail, 0.0).astype(jnp.bfloat16)
    for part, copy in zip(parts, copies[2:]):
        copy.wait()
        block_ref[part, :width] = unit_rows(raw[part])


def pack(rows, cluster_ids, order_index):
    count, width = rows.shape
    return pl.pallas_call(
        pack_kernel,
        in_specs=[pl.BlockSpec(memory_space=pl.ANY)] * 3,
        out_specs=VMEM,
        out_shape=jax.ShapeDtypeStruct((count, width + LANES), jnp.bfloat16),
        scratch_shapes=[
            pltpu.VMEM((count, width), jnp.bfloat16),
            pltpu.VMEM((2, 1, count), jnp.int32),
            pltpu.SemaphoreType.DMA((PARTS + 2,)),
        ],
        compiler_params=pltpu.CompilerParams(vmem_limit_bytes=8 * 2**20),
        cost_estimate=pl.CostEstimate(
            flops=4 * count * width, bytes_accessed=4 * count * width, transcendentals=count
        ),
    )(rows, cluster_ids.reshape(1, count), order_index.reshape(1, count))


def pair_kernel(own_ref, other_ref, both_ref):
    rows = own_ref.shape[0]
    core = lax.axis_index("core")
    both_ref[pl.ds(pl.multiple_of(core * rows, 16), rows), :] = own_ref[...]
    both_ref[pl.ds(pl.multiple_of((core ^ 1) * rows, 16), rows), :] = other_ref[...]


def pair(own, other):
    rows, width = own.shape
    return pl.pallas_call(
        pair_kernel,
        in_specs=[VMEM] * 2,
        out_specs=VMEM,
        out_shape=jax.ShapeDtypeStruct((2 * rows, width), own.dtype),
        compiler_params=pltpu.CompilerParams(vmem_limit_bytes=8 * 2**20),
        cost_estimate=pl.CostEstimate(flops=0, bytes_accessed=8 * rows * width, transcendentals=0),
    )(own, other)


def own_kernel(*refs):
    row_ref, *scratch = refs[-3:]
    best, _ = best_of(refs[:1], refs[1:-3], refs[0].shape[0], False, *scratch)
    row_ref[...] = best[0]


def visit_kernel(visitors, arrays, *refs):
    block_refs = refs[visitors : visitors + arrays]
    row_ref, mine_ref, other_ref, *scratch = refs[visitors + arrays + 1 :]
    bests, cols = best_of(refs[:visitors], block_refs, refs[0].shape[0] // 2, True, *scratch)
    for v, best in enumerate(bests):
        row_ref[v : v + 1, :] = best
    for j, best in enumerate(cols):
        (mine_ref, other_ref)[j % 2][j // 2 : j // 2 + 1, :] = best


def best_of(visitor_refs, block_refs, rows, homed, units, dots):
    width = units.shape[1]

    meta = []
    for ref in visitor_refs:
        for source in range(0, ref.shape[0], rows):
            place, source = len(meta) * LANES, pl.ds(source, rows)
            units[place : place + rows, :] = ref[source, :width]
            tail = ref[source, width:].astype(jnp.float32)
            if rows < LANES:
                spare = LANES - rows
                units[place + rows : place + LANES, :] = jnp.zeros((spare, width), jnp.bfloat16)
                tail = jnp.concatenate([tail, jnp.zeros((spare, LANES), jnp.float32)], axis=0)
            turned = tail.T
            meta.append((turned[0:1], turned[1:2] * 256.0 + turned[2:3]))
    for k in range(0, width, CHUNK):
        left = jnp.concatenate([ref[:, k : k + CHUNK] for ref in block_refs], axis=0)
        part = lax.dot_general(
            left,
            units[:, k : k + CHUNK],
            (((1,), (1,)), ((), ())),
            preferred_element_type=jnp.float32,
        )
        dots[...] = part if k == 0 else dots[...] + part

    tails = jnp.concatenate([ref[:, width:] for ref in block_refs], axis=0).astype(jnp.float32)
    row_best = [jnp.full((1, LANES), -1.0, jnp.float32) for _ in meta]
    lane = lax.broadcasted_iota(jnp.int32, (rows, LANES), 1)
    col_all = jnp.full((rows, LANES), -1.0, jnp.float32)
    for j in range(dots.shape[0] // rows):
        tail = tails[j * rows : (j + 1) * rows]
        block_cluster, block_order = tail[:, 0:1], tail[:, 1:2] * 256.0 + tail[:, 2:3]
        col_best = jnp.full((rows, 1), -1.0, jnp.float32)
        for v, (cluster, order) in enumerate(meta):
            cosine = dots[j * rows : (j + 1) * rows, v * LANES : (v + 1) * LANES]
            same = (block_cluster == cluster) & (cluster > 0)
            seen = jnp.where(same & (block_order < order), cosine, -1.0)
            row_best[v] = jnp.maximum(row_best[v], jnp.max(seen, axis=0, keepdims=True))
            if homed:
                seen = jnp.where(same & (order < block_order), cosine, -1.0)
                col_best = jnp.maximum(col_best, jnp.max(seen, axis=1, keepdims=True))
        col_all = jnp.where(lane == j, col_best, col_all)
    if not homed:
        return row_best, None
    if rows < LANES:
        fill = jnp.full((LANES - rows, LANES), -1.0, jnp.float32)
        col_all = jnp.concatenate([col_all, fill], axis=0)
    turned = col_all.T
    return row_best, [turned[j : j + 1] for j in range(dots.shape[0] // rows)]


def call(kernel, operands, count, out_rows, total):
    width = operands[0].shape[1] - LANES
    return pl.pallas_call(
        kernel,
        in_specs=[VMEM] * len(operands),
        out_specs=[VMEM] * len(out_rows),
        out_shape=[jax.ShapeDtypeStruct((n, LANES), jnp.float32) for n in out_rows],
        scratch_shapes=[
            pltpu.VMEM((count * LANES, width), jnp.bfloat16),
            pltpu.VMEM((total, count * LANES), jnp.float32),
        ],
        compiler_params=pltpu.CompilerParams(vmem_limit_bytes=24 * 2**20),
        cost_estimate=pl.CostEstimate(
            flops=2 * total * count * LANES * width,
            bytes_accessed=2 * (total + count * LANES) * width,
            transcendentals=0,
        ),
    )(*operands)


def local(embeddings, cluster_ids, order_index):
    rows = embeddings.shape[0]
    groups, length = lax.axis_size("group"), lax.axis_size("z")
    z, core = lax.axis_index("z"), lax.axis_index("core")
    own = pack(embeddings, cluster_ids, order_index)
    other = swap(own)
    both = pair(own, other)

    routes = [ring_pairs(length, shift) for shift in range(1, length // 2 + 1)]
    trips = []
    for first in range(0, len(routes), 2):
        ways = enumerate(routes[first : first + 2])
        trips.append([(2 * a + way, 2 * b + way) for way, route in ways for a, b in route])
    visitors = [lax.ppermute(both, ("z", "core"), trip) for trip in trips]

    plane = gather_plane(own, groups)
    parts = [own, other]
    for s in range(1, groups):
        parts += [*plane[s], *(swap(part) for part in plane[s])]
    chunks, size = [[]], 0
    for part in parts:
        if size == CALL * rows:
            chunks, size = chunks + [[]], 0
        chunks[-1].append(part)
        size += part.shape[0]

    bests, answers = [], []
    for chunk in chunks:
        total = sum(part.shape[0] for part in chunk)
        bests += call(own_kernel, [own, *chunk], 1, [1], total)
    for index, chunk in enumerate(chunks):
        total = sum(part.shape[0] for part in chunk)
        kernel = functools.partial(visit_kernel, len(visitors), len(chunk))
        count, half = 2 * len(visitors), total // rows // 2
        operands = [*visitors, *chunk, bests[index]]
        answers.append(call(kernel, operands, count, [count, half, half], total))
    home = functools.reduce(jnp.maximum, [answer[0] for answer in answers])
    for index, trip in enumerate(trips):
        part = home[2 * index : 2 * index + 2] if len(trips) > 1 else home
        back = lax.ppermute(part, ("z", "core"), [(b, a) for a, b in trip])
        for here, best in ((2 * z + core, back), (2 * z + (core ^ 1), swap(back))):
            sent = functools.reduce(jnp.logical_or, [here == a for a, _ in trip])
            bests.append(jnp.where(sent, jnp.where(core == 0, best[0:1], best[1:2]), -1.0))
    for index, (_, mine, other) in enumerate(answers):
        merged = jnp.maximum(mine, swap(other))
        for row in range(CALL // 2):
            s = index * CALL // 2 + row
            got = lax.ppermute(merged, "group", flip(groups, s)) if s else merged
            bests.append(got[row : row + 1])
    return functools.reduce(jnp.maximum, bests)[0, :rows]


def solution(mesh):
    groups, members = mesh.devices.shape
    fine = Mesh(mesh.devices.reshape(groups, members // 2, 2), AXES)
    placed = (P(AXES, None), P(AXES), P(AXES))
    return jax.shard_map(local, mesh=fine, in_specs=placed, out_specs=P(AXES), check_vma=False)
```

```python
import functools

import jax
import jax.numpy as jnp
from jax import lax
from jax.experimental import pallas as pl
from jax.experimental.pallas import tpu as pltpu
from jax.sharding import Mesh, PartitionSpec as P

AXES = ("group", "z", "core")
LANES = 128
CHUNK = 1024
CALL = 8
VMEM = pl.BlockSpec(memory_space=pltpu.VMEM)


def flip(count, bits):
    return [(k, k ^ bits) for k in range(count)]


def unit_rows(values):
    values = values.astype(jnp.float32)
    total = jnp.sum(values * values, axis=1, keepdims=True) + values.shape[1] * 1e-06
    return (values * lax.rsqrt(total)).astype(jnp.bfloat16)


def ring_pairs(length, shift):
    if 2 * shift < length:
        return [(k, (k + shift) % length) for k in range(length)]
    pairs = [(k, k + shift) for k in range(length // 2)]
    return [pair[:: 1 - 2 * (pair[0] % 2)] for pair in pairs]


def gather_plane(block, groups):
    half = block.shape[0] // 2
    blocks = {0: [block]}
    for s in range(1, groups):
        low, high = s & -s, 1 << (s.bit_length() - 1)
        if low == high:
            blocks[s] = [lax.ppermute(block, "group", flip(groups, s))]
            continue
        top, bottom = blocks[s ^ high], blocks[s ^ low]
        top = top[0][:half] if len(top) == 1 else top[0]
        bottom = bottom[0][half:] if len(bottom) == 1 else bottom[1]
        blocks[s] = [
            lax.ppermute(top, "group", flip(groups, high)),
            lax.ppermute(bottom, "group", flip(groups, low)),
        ]
    return blocks


def swap(block):
    return lax.ppermute(block, "core", flip(2, 1))


def pack_kernel(rows_ref, meta_ref, block_ref):
    rows, width = rows_ref.shape
    block_ref[:, :width] = unit_rows(rows_ref[...])
    turned = meta_ref[...].T[:rows]
    cluster, order = turned[:, 0:1], turned[:, 1:2]
    high = jnp.floor(order / 256.0)
    lane = lax.broadcasted_iota(jnp.int32, (rows, LANES), 1)
    tail = jnp.where(lane == 0, cluster, jnp.where(lane == 1, high, order - 256.0 * high))
    block_ref[:, width:] = jnp.where(lane < 3, tail, 0.0).astype(jnp.bfloat16)


def pack(rows, cluster_ids, order_index):
    count, width = rows.shape
    meta = jnp.stack([cluster_ids + 1, order_index]).astype(jnp.float32)
    meta = jnp.pad(meta, ((0, 6), (0, LANES - count)))
    return pl.pallas_call(
        pack_kernel,
        in_specs=[VMEM] * 2,
        out_specs=VMEM,
        out_shape=jax.ShapeDtypeStruct((count, width + LANES), jnp.bfloat16),
        compiler_params=pltpu.CompilerParams(vmem_limit_bytes=8 * 2**20),
        cost_estimate=pl.CostEstimate(
            flops=4 * count * width, bytes_accessed=4 * count * width, transcendentals=count
        ),
    )(rows, meta)


def pair_kernel(own_ref, other_ref, both_ref):
    rows = own_ref.shape[0]
    core = lax.axis_index("core")
    both_ref[pl.ds(pl.multiple_of(core * rows, 16), rows), :] = own_ref[...]
    both_ref[pl.ds(pl.multiple_of((core ^ 1) * rows, 16), rows), :] = other_ref[...]


def pair(own, other):
    rows, width = own.shape
    return pl.pallas_call(
        pair_kernel,
        in_specs=[VMEM] * 2,
        out_specs=VMEM,
        out_shape=jax.ShapeDtypeStruct((2 * rows, width), own.dtype),
        compiler_params=pltpu.CompilerParams(vmem_limit_bytes=8 * 2**20),
        cost_estimate=pl.CostEstimate(flops=0, bytes_accessed=8 * rows * width, transcendentals=0),
    )(own, other)


def own_kernel(*refs):
    row_ref, dots_ref = refs[-2:]
    row_ref[...], _ = best_of(refs[:1], refs[1:-2], refs[0].shape[0], False, [dots_ref])


def visit_kernel(visitors, arrays, *refs):
    block_refs = refs[visitors : visitors + arrays]
    out_refs = refs[visitors + arrays + 1 :]
    rows = refs[0].shape[0] // 2
    bests, col = best_of(refs[:visitors], block_refs, rows, True, out_refs[visitors + 2 :])
    for ref, best in zip(out_refs[:visitors], bests):
        ref[...] = best
    lower_ref, upper_ref = out_refs[visitors : visitors + 2]
    half = lower_ref.shape[0]
    lower_ref[...] = col[:half]
    upper_ref[...] = col[half : 2 * half]


def best_of(visitor_refs, block_refs, rows, homed, dots_refs):
    width = visitor_refs[0].shape[1] - LANES
    meta = []
    for ref in visitor_refs:
        count = ref.shape[0]
        tail = ref[:, width:].astype(jnp.float32)
        if count % LANES:
            tail = jnp.concatenate([tail, jnp.zeros((-count % LANES, LANES), jnp.float32)], axis=0)
        turned = tail.T
        meta.append((turned[0:1, :count], turned[1:2, :count] * 256.0 + turned[2:3, :count]))
    for k in range(0, width, CHUNK):
        left = jnp.concatenate([ref[:, k : k + CHUNK] for ref in block_refs], axis=0)
        for ref, dots in zip(visitor_refs, dots_refs):
            part = lax.dot_general(
                left,
                ref[:, k : k + CHUNK],
                (((1,), (1,)), ((), ())),
                preferred_element_type=jnp.float32,
            )
            dots[...] = part if k == 0 else dots[...] + part

    tails = jnp.concatenate([ref[:, width:] for ref in block_refs], axis=0).astype(jnp.float32)
    row_best = [jnp.full(cluster.shape, -1.0, jnp.float32) for cluster, _ in meta]
    lane = lax.broadcasted_iota(jnp.int32, (rows, LANES), 1)
    col_all = jnp.full((rows, LANES), -1.0, jnp.float32)
    for j in range(tails.shape[0] // rows):
        tail = tails[j * rows : (j + 1) * rows]
        block_cluster, block_order = tail[:, 0:1], tail[:, 1:2] * 256.0 + tail[:, 2:3]
        col_best = jnp.full((rows, 1), -1.0, jnp.float32)
        for v, (cluster, order) in enumerate(meta):
            cosine = dots_refs[v][j * rows : (j + 1) * rows, :]
            same = (block_cluster == cluster) & (cluster > 0)
            seen = jnp.where(same & (block_order < order), cosine, -1.0)
            row_best[v] = jnp.maximum(row_best[v], jnp.max(seen, axis=0, keepdims=True))
            if homed:
                seen = jnp.where(same & (order < block_order), cosine, -1.0)
                col_best = jnp.maximum(col_best, jnp.max(seen, axis=1, keepdims=True))
        col_all = jnp.where(lane == j, col_best, col_all)
    if not homed:
        return row_best[0], None
    if rows < LANES:
        fill = jnp.full((LANES - rows, LANES), -1.0, jnp.float32)
        col_all = jnp.concatenate([col_all, fill], axis=0)
    return row_best, col_all.T


def call(kernel, operands, counts, shapes, total):
    width = operands[0].shape[1] - LANES
    return pl.pallas_call(
        kernel,
        in_specs=[VMEM] * len(operands),
        out_specs=[VMEM] * len(shapes),
        out_shape=[jax.ShapeDtypeStruct(shape, jnp.float32) for shape in shapes],
        scratch_shapes=[pltpu.VMEM((total, count), jnp.float32) for count in counts],
        compiler_params=pltpu.CompilerParams(vmem_limit_bytes=24 * 2**20),
        cost_estimate=pl.CostEstimate(
            flops=2 * total * sum(counts) * width,
            bytes_accessed=2 * (total + sum(counts)) * width,
            transcendentals=0,
        ),
    )(*operands)


def local(embeddings, cluster_ids, order_index):
    rows = embeddings.shape[0]
    groups, length = lax.axis_size("group"), lax.axis_size("z")
    z, core = lax.axis_index("z"), lax.axis_index("core")
    own = pack(embeddings, cluster_ids, order_index)
    other = swap(own)
    both = pair(own, other)

    routes = [ring_pairs(length, shift) for shift in range(1, length // 2 + 1)]
    trips = []
    for first in range(0, len(routes), 2):
        ways = enumerate(routes[first : first + 2])
        trips.append([(2 * a + way, 2 * b + way) for way, route in ways for a, b in route])
    visitors = [lax.ppermute(both, ("z", "core"), trip) for trip in trips]

    plane = gather_plane(own, groups)
    parts = [own, other]
    for s in range(1, groups):
        parts += [*plane[s], *(swap(part) for part in plane[s])]
    chunks, size = [[]], 0
    for part in parts:
        if size == CALL * rows:
            chunks, size = chunks + [[]], 0
        chunks[-1].append(part)
        size += part.shape[0]

    bests, homes, cols = [], [], []
    for chunk in chunks:
        total = sum(part.shape[0] for part in chunk)
        bests += call(own_kernel, [own, *chunk], [rows], [(1, rows)], total)
    for index, chunk in enumerate(chunks):
        total = sum(part.shape[0] for part in chunk)
        kernel = functools.partial(visit_kernel, len(visitors), len(chunk))
        counts = [2 * rows] * len(visitors)
        shapes = [(1, count) for count in counts] + [(CALL // 2, LANES)] * 2
        answer = call(kernel, [*visitors, *chunk, bests[index]], counts, shapes, total)
        homes.append(answer[: len(visitors)])
        cols += answer[len(visitors) :]

    while len(cols) > 1:
        half = len(cols) // 2
        got = [lax.ppermute(col, "group", flip(groups, CALL // 4 * half)) for col in cols[half:]]
        cols = [jnp.maximum(a, b) for a, b in zip(cols, got)]
    (col,) = cols
    while col.shape[0] > 2:
        half = col.shape[0] // 4
        got = lax.ppermute(col, "group", flip(groups, half))
        col = jnp.maximum(col[: 2 * half], got[2 * half :])
    mine, others = [col[0:1, :rows]], [col[1:2, :rows]]
    for trip, parts in zip(trips, zip(*homes)):
        back = functools.reduce(jnp.maximum, parts)
        back = lax.ppermute(back, ("z", "core"), [(b, a) for a, b in trip])
        sent = functools.reduce(jnp.logical_or, [2 * z + core == a for a, _ in trip])
        back = jnp.where(sent, back, -1.0)
        first, second = back[:, :rows], back[:, rows:]
        mine.append(jnp.where(core == 0, first, second))
        others.append(jnp.where(core == 0, second, first))
    bests += mine + [swap(functools.reduce(jnp.maximum, others))]
    return functools.reduce(jnp.maximum, bests)[0]


def solution(mesh):
    groups, members = mesh.devices.shape
    fine = Mesh(mesh.devices.reshape(groups, members // 2, 2), AXES)
    placed = (P(AXES, None), P(AXES), P(AXES))
    return jax.shard_map(local, mesh=fine, in_specs=placed, out_specs=P(AXES), check_vma=False)
```

```python
import functools

import jax
import jax.numpy as jnp
from jax import lax
from jax.experimental import pallas as pl
from jax.experimental.pallas import tpu as pltpu
from jax.sharding import Mesh, PartitionSpec as P

AXES = ("group", "z", "core")
LANES = 128
CHUNK = 512
CALL = 8
VMEM = pl.BlockSpec(memory_space=pltpu.VMEM)


def flip(count, bits):
    return [(k, k ^ bits) for k in range(count)]


def unit_rows(values):
    values = values.astype(jnp.float32)
    total = jnp.sum(values * values, axis=1, keepdims=True) + values.shape[1] * 1e-06
    return (values * lax.rsqrt(total)).astype(jnp.bfloat16)


def ring_pairs(length, shift):
    if 2 * shift < length:
        return [(k, (k + shift) % length) for k in range(length)]
    pairs = [(k, k + shift) for k in range(length // 2)]
    return [pair[:: 1 - 2 * (pair[0] % 2)] for pair in pairs]


def gather_plane(block, groups):
    half = block.shape[0] // 2
    blocks = {0: [block]}
    for s in range(1, groups):
        low, high = s & -s, 1 << (s.bit_length() - 1)
        if low == high:
            blocks[s] = [lax.ppermute(block, "group", flip(groups, s))]
            continue
        top, bottom = blocks[s ^ high], blocks[s ^ low]
        top = top[0][:half] if len(top) == 1 else top[0]
        bottom = bottom[0][half:] if len(bottom) == 1 else bottom[1]
        blocks[s] = [
            lax.ppermute(top, "group", flip(groups, high)),
            lax.ppermute(bottom, "group", flip(groups, low)),
        ]
    return blocks


def swap(block):
    return lax.ppermute(block, "core", flip(2, 1))


def pack_kernel(rows_ref, ids_ref, block_ref):
    rows, width = rows_ref.shape
    block_ref[:, :width] = unit_rows(rows_ref[...])
    ids = ids_ref[...].astype(jnp.float32)
    meta = jnp.concatenate([ids, jnp.zeros((6, rows), jnp.float32)], axis=0)
    if rows < LANES:
        meta = jnp.concatenate([meta, jnp.zeros((8, LANES - rows), jnp.float32)], axis=1)
    turned = meta.T[:rows]
    cluster, order = turned[:, 0:1] + 1.0, turned[:, 1:2]
    high = jnp.floor(order / 256.0)
    lane = lax.broadcasted_iota(jnp.int32, (rows, LANES), 1)
    tail = jnp.where(lane == 0, cluster, jnp.where(lane == 1, high, order - 256.0 * high))
    block_ref[:, width:] = jnp.where(lane < 3, tail, 0.0).astype(jnp.bfloat16)


def pack(rows, cluster_ids, order_index):
    count, width = rows.shape
    return pl.pallas_call(
        pack_kernel,
        in_specs=[VMEM] * 2,
        out_specs=VMEM,
        out_shape=jax.ShapeDtypeStruct((count, width + LANES), jnp.bfloat16),
        compiler_params=pltpu.CompilerParams(vmem_limit_bytes=8 * 2**20),
        cost_estimate=pl.CostEstimate(
            flops=4 * count * width, bytes_accessed=4 * count * width, transcendentals=count
        ),
    )(rows, jnp.stack([cluster_ids, order_index]))


def pair_kernel(own_ref, other_ref, both_ref):
    rows = own_ref.shape[0]
    core = lax.axis_index("core")
    both_ref[pl.ds(pl.multiple_of(core * rows, 16), rows), :] = own_ref[...]
    both_ref[pl.ds(pl.multiple_of((core ^ 1) * rows, 16), rows), :] = other_ref[...]


def pair(own, other):
    rows, width = own.shape
    return pl.pallas_call(
        pair_kernel,
        in_specs=[VMEM] * 2,
        out_specs=VMEM,
        out_shape=jax.ShapeDtypeStruct((2 * rows, width), own.dtype),
        compiler_params=pltpu.CompilerParams(vmem_limit_bytes=8 * 2**20),
        cost_estimate=pl.CostEstimate(flops=0, bytes_accessed=8 * rows * width, transcendentals=0),
    )(own, other)


def own_kernel(*refs):
    row_ref, *scratch = refs[-3:]
    best, _ = best_of(refs[:1], refs[1:-3], refs[0].shape[0], False, *scratch)
    row_ref[...] = best[0]


def visit_kernel(visitors, arrays, *refs):
    block_refs = refs[visitors : visitors + arrays]
    row_ref, mine_ref, other_ref, *scratch = refs[visitors + arrays + 1 :]
    bests, cols = best_of(refs[:visitors], block_refs, refs[0].shape[0] // 2, True, *scratch)
    for v, best in enumerate(bests):
        row_ref[v : v + 1, :] = best
    for j, best in enumerate(cols):
        (mine_ref, other_ref)[j % 2][j // 2 : j // 2 + 1, :] = best


def best_of(visitor_refs, block_refs, rows, homed, units, dots):
    width = units.shape[1]

    meta = []
    for ref in visitor_refs:
        for source in range(0, ref.shape[0], rows):
            place, source = len(meta) * LANES, pl.ds(source, rows)
            units[place : place + rows, :] = ref[source, :width]
            tail = ref[source, width:].astype(jnp.float32)
            if rows < LANES:
                spare = LANES - rows
                units[place + rows : place + LANES, :] = jnp.zeros((spare, width), jnp.bfloat16)
                tail = jnp.concatenate([tail, jnp.zeros((spare, LANES), jnp.float32)], axis=0)
            turned = tail.T
            meta.append((turned[0:1], turned[1:2] * 256.0 + turned[2:3]))
    for k in range(0, width, CHUNK):
        left = jnp.concatenate([ref[:, k : k + CHUNK] for ref in block_refs], axis=0)
        part = lax.dot_general(
            left,
            units[:, k : k + CHUNK],
            (((1,), (1,)), ((), ())),
            preferred_element_type=jnp.float32,
        )
        dots[...] = part if k == 0 else dots[...] + part

    tails = jnp.concatenate([ref[:, width:] for ref in block_refs], axis=0).astype(jnp.float32)
    row_best = [jnp.full((1, LANES), -1.0, jnp.float32) for _ in meta]
    lane = lax.broadcasted_iota(jnp.int32, (rows, LANES), 1)
    col_all = jnp.full((rows, LANES), -1.0, jnp.float32)
    for j in range(dots.shape[0] // rows):
        tail = tails[j * rows : (j + 1) * rows]
        block_cluster, block_order = tail[:, 0:1], tail[:, 1:2] * 256.0 + tail[:, 2:3]
        col_best = jnp.full((rows, 1), -1.0, jnp.float32)
        for v, (cluster, order) in enumerate(meta):
            cosine = dots[j * rows : (j + 1) * rows, v * LANES : (v + 1) * LANES]
            same = (block_cluster == cluster) & (cluster > 0)
            seen = jnp.where(same & (block_order < order), cosine, -1.0)
            row_best[v] = jnp.maximum(row_best[v], jnp.max(seen, axis=0, keepdims=True))
            if homed:
                seen = jnp.where(same & (order < block_order), cosine, -1.0)
                col_best = jnp.maximum(col_best, jnp.max(seen, axis=1, keepdims=True))
        col_all = jnp.where(lane == j, col_best, col_all)
    if not homed:
        return row_best, None
    if rows < LANES:
        fill = jnp.full((LANES - rows, LANES), -1.0, jnp.float32)
        col_all = jnp.concatenate([col_all, fill], axis=0)
    turned = col_all.T
    return row_best, [turned[j : j + 1] for j in range(dots.shape[0] // rows)]


def call(kernel, operands, count, out_rows, total):
    width = operands[0].shape[1] - LANES
    return pl.pallas_call(
        kernel,
        in_specs=[VMEM] * len(operands),
        out_specs=[VMEM] * len(out_rows),
        out_shape=[jax.ShapeDtypeStruct((n, LANES), jnp.float32) for n in out_rows],
        scratch_shapes=[
            pltpu.VMEM((count * LANES, width), jnp.bfloat16),
            pltpu.VMEM((total, count * LANES), jnp.float32),
        ],
        compiler_params=pltpu.CompilerParams(vmem_limit_bytes=24 * 2**20),
        cost_estimate=pl.CostEstimate(
            flops=2 * total * count * LANES * width,
            bytes_accessed=2 * (total + count * LANES) * width,
            transcendentals=0,
        ),
    )(*operands)


def local(embeddings, cluster_ids, order_index):
    rows = embeddings.shape[0]
    groups, length = lax.axis_size("group"), lax.axis_size("z")
    z, core = lax.axis_index("z"), lax.axis_index("core")
    own = pack(embeddings, cluster_ids, order_index)
    other = swap(own)
    both = pair(own, other)

    routes = [ring_pairs(length, shift) for shift in range(1, length // 2 + 1)]
    trips = []
    for first in range(0, len(routes), 2):
        ways = enumerate(routes[first : first + 2])
        trips.append([(2 * a + way, 2 * b + way) for way, route in ways for a, b in route])
    visitors = [lax.ppermute(both, ("z", "core"), trip) for trip in trips]

    plane = gather_plane(own, groups)
    parts = [own, other]
    for s in range(1, groups):
        parts += [*plane[s], *(swap(part) for part in plane[s])]
    chunks, size = [[]], 0
    for part in parts:
        if size == CALL * rows:
            chunks, size = chunks + [[]], 0
        chunks[-1].append(part)
        size += part.shape[0]

    bests, answers = [], []
    for chunk in chunks:
        total = sum(part.shape[0] for part in chunk)
        bests += call(own_kernel, [own, *chunk], 1, [1], total)
    for index, chunk in enumerate(chunks):
        total = sum(part.shape[0] for part in chunk)
        kernel = functools.partial(visit_kernel, len(visitors), len(chunk))
        count, half = 2 * len(visitors), total // rows // 2
        operands = [*visitors, *chunk, bests[index]]
        answers.append(call(kernel, operands, count, [count, half, half], total))
    home = functools.reduce(jnp.maximum, [answer[0] for answer in answers])
    for index, trip in enumerate(trips):
        part = home[2 * index : 2 * index + 2] if len(trips) > 1 else home
        back = lax.ppermute(part, ("z", "core"), [(b, a) for a, b in trip])
        for here, best in ((2 * z + core, back), (2 * z + (core ^ 1), swap(back))):
            sent = functools.reduce(jnp.logical_or, [here == a for a, _ in trip])
            bests.append(jnp.where(sent, jnp.where(core == 0, best[0:1], best[1:2]), -1.0))
    for index, (_, mine, other) in enumerate(answers):
        merged = jnp.maximum(mine, swap(other))
        for row in range(CALL // 2):
            s = index * CALL // 2 + row
            got = lax.ppermute(merged, "group", flip(groups, s)) if s else merged
            bests.append(got[row : row + 1])
    return functools.reduce(jnp.maximum, bests)[0, :rows]


def solution(mesh):
    groups, members = mesh.devices.shape
    fine = Mesh(mesh.devices.reshape(groups, members // 2, 2), AXES)
    placed = (P(AXES, None), P(AXES), P(AXES))
    return jax.shard_map(local, mesh=fine, in_specs=placed, out_specs=P(AXES), check_vma=False)
```

```python
import functools

import jax
import jax.numpy as jnp
from jax import lax
from jax.experimental import pallas as pl
from jax.experimental.pallas import tpu as pltpu
from jax.sharding import Mesh, PartitionSpec as P

AXES = ("group", "z", "core")
LANES = 128
CHUNK = 512
CALL = 8
VMEM = pl.BlockSpec(memory_space=pltpu.VMEM)


def flip(count, bits):
    return [(k, k ^ bits) for k in range(count)]


def unit_rows(values):
    values = values.astype(jnp.float32)
    total = jnp.sum(values * values, axis=1, keepdims=True) + values.shape[1] * 1e-06
    return (values * lax.rsqrt(total)).astype(jnp.bfloat16)


def ring_pairs(length, shift):
    if 2 * shift < length:
        return [(k, (k + shift) % length) for k in range(length)]
    pairs = [(k, k + shift) for k in range(length // 2)]
    return [pair[:: 1 - 2 * (pair[0] % 2)] for pair in pairs]


def gather_plane(block, groups):
    half = block.shape[0] // 2
    blocks = {0: [block]}
    for s in range(1, groups):
        low, high = s & -s, 1 << (s.bit_length() - 1)
        if low == high:
            blocks[s] = [lax.ppermute(block, "group", flip(groups, s))]
            continue
        top, bottom = blocks[s ^ high], blocks[s ^ low]
        top = top[0][:half] if len(top) == 1 else top[0]
        bottom = bottom[0][half:] if len(bottom) == 1 else bottom[1]
        blocks[s] = [
            lax.ppermute(top, "group", flip(groups, high)),
            lax.ppermute(bottom, "group", flip(groups, low)),
        ]
    return blocks


def swap(block):
    return lax.ppermute(block, "core", flip(2, 1))


def pack_kernel(rows_ref, ids_ref, block_ref):
    rows, width = rows_ref.shape
    block_ref[:, :width] = unit_rows(rows_ref[...])
    ids = ids_ref[...].astype(jnp.float32)
    meta = jnp.concatenate([ids, jnp.zeros((6, rows), jnp.float32)], axis=0)
    if rows < LANES:
        meta = jnp.concatenate([meta, jnp.zeros((8, LANES - rows), jnp.float32)], axis=1)
    turned = meta.T[:rows]
    cluster, order = turned[:, 0:1] + 1.0, turned[:, 1:2]
    high = jnp.floor(order / 256.0)
    lane = lax.broadcasted_iota(jnp.int32, (rows, LANES), 1)
    tail = jnp.where(lane == 0, cluster, jnp.where(lane == 1, high, order - 256.0 * high))
    block_ref[:, width:] = jnp.where(lane < 3, tail, 0.0).astype(jnp.bfloat16)


def pack(rows, cluster_ids, order_index):
    count, width = rows.shape
    return pl.pallas_call(
        pack_kernel,
        in_specs=[VMEM] * 2,
        out_specs=VMEM,
        out_shape=jax.ShapeDtypeStruct((count, width + LANES), jnp.bfloat16),
        compiler_params=pltpu.CompilerParams(vmem_limit_bytes=8 * 2**20),
        cost_estimate=pl.CostEstimate(
            flops=4 * count * width, bytes_accessed=4 * count * width, transcendentals=count
        ),
    )(rows, jnp.stack([cluster_ids, order_index]))


def pair_kernel(own_ref, other_ref, both_ref):
    rows = own_ref.shape[0]
    core = lax.axis_index("core")
    both_ref[pl.ds(pl.multiple_of(core * rows, 16), rows), :] = own_ref[...]
    both_ref[pl.ds(pl.multiple_of((core ^ 1) * rows, 16), rows), :] = other_ref[...]


def pair(own, other):
    rows, width = own.shape
    return pl.pallas_call(
        pair_kernel,
        in_specs=[VMEM] * 2,
        out_specs=VMEM,
        out_shape=jax.ShapeDtypeStruct((2 * rows, width), own.dtype),
        compiler_params=pltpu.CompilerParams(vmem_limit_bytes=8 * 2**20),
        cost_estimate=pl.CostEstimate(flops=0, bytes_accessed=8 * rows * width, transcendentals=0),
    )(own, other)


def own_kernel(*refs):
    row_ref, *scratch = refs[-3:]
    best, _ = best_of(refs[:1], refs[1:-3], refs[0].shape[0], False, *scratch)
    row_ref[...] = best[0]


def visit_kernel(visitors, arrays, *refs):
    block_refs = refs[visitors : visitors + arrays]
    row_ref, mine_ref, other_ref, *scratch = refs[visitors + arrays + 1 :]
    bests, cols = best_of(refs[:visitors], block_refs, refs[0].shape[0] // 2, True, *scratch)
    for v, best in enumerate(bests):
        row_ref[v : v + 1, :] = best
    for j, best in enumerate(cols):
        place = (lax.axis_index("group") ^ (j // 2)) & (CALL // 2 - 1)
        (mine_ref, other_ref)[j % 2][place] = best


def best_of(visitor_refs, block_refs, rows, homed, units, dots):
    width = units.shape[1]

    meta = []
    for ref in visitor_refs:
        for source in range(0, ref.shape[0], rows):
            place, source = len(meta) * LANES, pl.ds(source, rows)
            units[place : place + rows, :] = ref[source, :width]
            tail = ref[source, width:].astype(jnp.float32)
            if rows < LANES:
                spare = LANES - rows
                units[place + rows : place + LANES, :] = jnp.zeros((spare, width), jnp.bfloat16)
                tail = jnp.concatenate([tail, jnp.zeros((spare, LANES), jnp.float32)], axis=0)
            turned = tail.T
            meta.append((turned[0:1], turned[1:2] * 256.0 + turned[2:3]))
    for k in range(0, width, CHUNK):
        left = jnp.concatenate([ref[:, k : k + CHUNK] for ref in block_refs], axis=0)
        part = lax.dot_general(
            left,
            units[:, k : k + CHUNK],
            (((1,), (1,)), ((), ())),
            preferred_element_type=jnp.float32,
        )
        dots[...] = part if k == 0 else dots[...] + part

    tails = jnp.concatenate([ref[:, width:] for ref in block_refs], axis=0).astype(jnp.float32)
    row_best = [jnp.full((1, LANES), -1.0, jnp.float32) for _ in meta]
    lane = lax.broadcasted_iota(jnp.int32, (rows, LANES), 1)
    col_all = jnp.full((rows, LANES), -1.0, jnp.float32)
    for j in range(dots.shape[0] // rows):
        tail = tails[j * rows : (j + 1) * rows]
        block_cluster, block_order = tail[:, 0:1], tail[:, 1:2] * 256.0 + tail[:, 2:3]
        col_best = jnp.full((rows, 1), -1.0, jnp.float32)
        for v, (cluster, order) in enumerate(meta):
            cosine = dots[j * rows : (j + 1) * rows, v * LANES : (v + 1) * LANES]
            same = (block_cluster == cluster) & (cluster > 0)
            seen = jnp.where(same & (block_order < order), cosine, -1.0)
            row_best[v] = jnp.maximum(row_best[v], jnp.max(seen, axis=0, keepdims=True))
            if homed:
                seen = jnp.where(same & (order < block_order), cosine, -1.0)
                col_best = jnp.maximum(col_best, jnp.max(seen, axis=1, keepdims=True))
        col_all = jnp.where(lane == j, col_best, col_all)
    if not homed:
        return row_best, None
    if rows < LANES:
        fill = jnp.full((LANES - rows, LANES), -1.0, jnp.float32)
        col_all = jnp.concatenate([col_all, fill], axis=0)
    turned = col_all.T
    return row_best, [turned[j : j + 1] for j in range(dots.shape[0] // rows)]


def call(kernel, operands, count, out_rows, total):
    width = operands[0].shape[1] - LANES
    return pl.pallas_call(
        kernel,
        in_specs=[VMEM] * len(operands),
        out_specs=[VMEM] * len(out_rows),
        out_shape=[jax.ShapeDtypeStruct((*n, LANES), jnp.float32) for n in out_rows],
        scratch_shapes=[
            pltpu.VMEM((count * LANES, width), jnp.bfloat16),
            pltpu.VMEM((total, count * LANES), jnp.float32),
        ],
        compiler_params=pltpu.CompilerParams(vmem_limit_bytes=24 * 2**20),
        cost_estimate=pl.CostEstimate(
            flops=2 * total * count * LANES * width,
            bytes_accessed=2 * (total + count * LANES) * width,
            transcendentals=0,
        ),
    )(*operands)


def local(embeddings, cluster_ids, order_index):
    rows = embeddings.shape[0]
    groups, length = lax.axis_size("group"), lax.axis_size("z")
    z, core = lax.axis_index("z"), lax.axis_index("core")
    own = pack(embeddings, cluster_ids, order_index)
    other = swap(own)
    both = pair(own, other)

    routes = [ring_pairs(length, shift) for shift in range(1, length // 2 + 1)]
    trips = []
    for first in range(0, len(routes), 2):
        ways = enumerate(routes[first : first + 2])
        trips.append([(2 * a + way, 2 * b + way) for way, route in ways for a, b in route])
    visitors = [lax.ppermute(both, ("z", "core"), trip) for trip in trips]

    plane = gather_plane(own, groups)
    parts = [own, other]
    for s in range(1, groups):
        parts += [*plane[s], *(swap(part) for part in plane[s])]
    chunks, size = [[]], 0
    for part in parts:
        if size == CALL * rows:
            chunks, size = chunks + [[]], 0
        chunks[-1].append(part)
        size += part.shape[0]

    bests, answers = [], []
    for chunk in chunks:
        total = sum(part.shape[0] for part in chunk)
        bests += call(own_kernel, [own, *chunk], 1, [(1,)], total)
    for index, chunk in enumerate(chunks):
        total = sum(part.shape[0] for part in chunk)
        kernel = functools.partial(visit_kernel, len(visitors), len(chunk))
        count, pairs = 2 * len(visitors), (CALL // 2, 1)
        operands = [*visitors, *chunk, bests[index]]
        answers.append(call(kernel, operands, count, [(count,), pairs, pairs], total))
    home = functools.reduce(jnp.maximum, [answer[0] for answer in answers])
    for index, trip in enumerate(trips):
        part = home[2 * index : 2 * index + 2] if len(trips) > 1 else home
        back = lax.ppermute(part, ("z", "core"), [(b, a) for a, b in trip])
        for here, best in ((2 * z + core, back), (2 * z + (core ^ 1), swap(back))):
            sent = functools.reduce(jnp.logical_or, [here == a for a, _ in trip])
            bests.append(jnp.where(sent, jnp.where(core == 0, best[0:1], best[1:2]), -1.0))
    merged = [jnp.maximum(mine, swap(other)) for _, mine, other in answers]
    if len(merged) > 1:
        turn = (lax.axis_index("group") // (CALL // 2)) ^ jnp.arange(len(merged))
        merged = [jnp.stack(merged)[turn].reshape(groups, 1, LANES)]
    parts = lax.all_to_all(merged[0], "group", split_axis=0, concat_axis=0, tiled=True)
    bests += [parts[s] for s in range(groups)]
    return functools.reduce(jnp.maximum, bests)[0, :rows]


def solution(mesh):
    groups, members = mesh.devices.shape
    fine = Mesh(mesh.devices.reshape(groups, members // 2, 2), AXES)
    placed = (P(AXES, None), P(AXES), P(AXES))
    return jax.shard_map(local, mesh=fine, in_specs=placed, out_specs=P(AXES), check_vma=False)
```

```python
import functools

import jax
import jax.numpy as jnp
from jax import lax
from jax.experimental import pallas as pl
from jax.experimental.pallas import tpu as pltpu
from jax.sharding import Mesh, PartitionSpec as P

AXES = ("group", "z", "core")
LANES = 128
CHUNK = 512
VMEM = pl.BlockSpec(memory_space=pltpu.VMEM)


def flip(count, bits):
    return [(k, k ^ bits) for k in range(count)]


def unit_rows(values):
    values = values.astype(jnp.float32)
    total = jnp.sum(values * values, axis=1, keepdims=True) + values.shape[1] * 1e-06
    return (values * lax.rsqrt(total)).astype(jnp.bfloat16)


def ring_pairs(length, shift):
    if 2 * shift < length:
        return [(k, (k + shift) % length) for k in range(length)]
    pairs = [(k, k + shift) for k in range(length // 2)]
    return [pair[:: 1 - 2 * (pair[0] % 2)] for pair in pairs]


def swap(block):
    return lax.ppermute(block, "core", flip(2, 1))


def pack_kernel(rows_ref, ids_ref, block_ref):
    rows, width = rows_ref.shape
    block_ref[:, :width] = unit_rows(rows_ref[...])
    ids = ids_ref[...].astype(jnp.float32)
    meta = jnp.concatenate([ids, jnp.zeros((6, rows), jnp.float32)], axis=0)
    if rows < LANES:
        meta = jnp.concatenate([meta, jnp.zeros((8, LANES - rows), jnp.float32)], axis=1)
    turned = meta.T[:rows]
    cluster, order = turned[:, 0:1] + 1.0, turned[:, 1:2]
    high = jnp.floor(order / 256.0)
    lane = lax.broadcasted_iota(jnp.int32, (rows, LANES), 1)
    tail = jnp.where(lane == 0, cluster, jnp.where(lane == 1, high, order - 256.0 * high))
    block_ref[:, width:] = jnp.where(lane < 3, tail, 0.0).astype(jnp.bfloat16)


def pack(rows, cluster_ids, order_index):
    count, width = rows.shape
    return pl.pallas_call(
        pack_kernel,
        in_specs=[VMEM] * 2,
        out_specs=VMEM,
        out_shape=jax.ShapeDtypeStruct((count, width + LANES), jnp.bfloat16),
        compiler_params=pltpu.CompilerParams(vmem_limit_bytes=8 * 2**20),
        cost_estimate=pl.CostEstimate(
            flops=4 * count * width, bytes_accessed=4 * count * width, transcendentals=count
        ),
    )(rows, jnp.stack([cluster_ids, order_index]))


def pair_kernel(own_ref, other_ref, both_ref):
    rows = own_ref.shape[0]
    both_ref[:rows, :] = own_ref[...]
    both_ref[rows:, :] = other_ref[...]


def pair(own, other):
    rows, width = own.shape
    return pl.pallas_call(
        pair_kernel,
        in_specs=[VMEM] * 2,
        out_specs=VMEM,
        out_shape=jax.ShapeDtypeStruct((2 * rows, width), own.dtype),
        compiler_params=pltpu.CompilerParams(vmem_limit_bytes=8 * 2**20),
        cost_estimate=pl.CostEstimate(flops=0, bytes_accessed=8 * rows * width, transcendentals=0),
    )(own, other)


def own_kernel(*refs):
    row_ref, *scratch = refs[-3:]
    best, _ = best_of(refs[:1], refs[1:-3], refs[0].shape[0], False, *scratch)
    row_ref[...] = best[0]


def visit_kernel(visitors, arrays, mine, others, *refs):
    block_refs = refs[visitors : visitors + arrays]
    row_ref, mine_ref, other_ref, *scratch = refs[visitors + arrays + 1 :]
    rows = refs[0].shape[0] // 2
    bests, cols = best_of(refs[:visitors], block_refs, rows, True, *scratch)
    for v, best in enumerate(bests):
        row_ref[v : v + 1, :] = best
    for ref, picked in ((mine_ref, mine), (other_ref, others)):
        for row, j in enumerate(picked):
            ref[row : row + 1, :] = cols[j]


def best_of(visitor_refs, block_refs, rows, homed, units, dots):
    width = units.shape[1]

    meta = []
    for ref in visitor_refs:
        for source in range(0, ref.shape[0], rows):
            place, source = len(meta) * LANES, pl.ds(source, rows)
            units[place : place + rows, :] = ref[source, :width]
            tail = ref[source, width:].astype(jnp.float32)
            if rows < LANES:
                spare = LANES - rows
                units[place + rows : place + LANES, :] = jnp.zeros((spare, width), jnp.bfloat16)
                tail = jnp.concatenate([tail, jnp.zeros((spare, LANES), jnp.float32)], axis=0)
            turned = tail.T
            meta.append((turned[0:1], turned[1:2] * 256.0 + turned[2:3]))
    for k in range(0, width, CHUNK):
        left = jnp.concatenate([ref[:, k : k + CHUNK] for ref in block_refs], axis=0)
        part = lax.dot_general(
            left,
            units[:, k : k + CHUNK],
            (((1,), (1,)), ((), ())),
            preferred_element_type=jnp.float32,
        )
        dots[...] = part if k == 0 else dots[...] + part

    tails = jnp.concatenate([ref[:, width:] for ref in block_refs], axis=0).astype(jnp.float32)
    row_best = [jnp.full((1, LANES), -1.0, jnp.float32) for _ in meta]
    lane = lax.broadcasted_iota(jnp.int32, (rows, LANES), 1)
    col_all = jnp.full((rows, LANES), -1.0, jnp.float32)
    for j in range(dots.shape[0] // rows):
        tail = tails[j * rows : (j + 1) * rows]
        block_cluster, block_order = tail[:, 0:1], tail[:, 1:2] * 256.0 + tail[:, 2:3]
        col_best = jnp.full((rows, 1), -1.0, jnp.float32)
        for v, (cluster, order) in enumerate(meta):
            cosine = dots[j * rows : (j + 1) * rows, v * LANES : (v + 1) * LANES]
            same = (block_cluster == cluster) & (cluster > 0)
            seen = jnp.where(same & (block_order < order), cosine, -1.0)
            row_best[v] = jnp.maximum(row_best[v], jnp.max(seen, axis=0, keepdims=True))
            if homed:
                seen = jnp.where(same & (order < block_order), cosine, -1.0)
                col_best = jnp.maximum(col_best, jnp.max(seen, axis=1, keepdims=True))
        col_all = jnp.where(lane == j, col_best, col_all)
    if not homed:
        return row_best, None
    if rows < LANES:
        fill = jnp.full((LANES - rows, LANES), -1.0, jnp.float32)
        col_all = jnp.concatenate([col_all, fill], axis=0)
    turned = col_all.T
    return row_best, [turned[j : j + 1] for j in range(dots.shape[0] // rows)]


def call(kernel, operands, count, out_rows, total):
    width = operands[0].shape[1] - LANES
    return pl.pallas_call(
        kernel,
        in_specs=[VMEM] * len(operands),
        out_specs=[VMEM] * len(out_rows),
        out_shape=[jax.ShapeDtypeStruct((n, LANES), jnp.float32) for n in out_rows],
        scratch_shapes=[
            pltpu.VMEM((count * LANES, width), jnp.bfloat16),
            pltpu.VMEM((total, count * LANES), jnp.float32),
        ],
        compiler_params=pltpu.CompilerParams(vmem_limit_bytes=24 * 2**20),
        cost_estimate=pl.CostEstimate(
            flops=2 * total * count * LANES * width,
            bytes_accessed=2 * (total + count * LANES) * width,
            transcendentals=0,
        ),
    )(*operands)


def group_trip(groups, first, second):
    return [(2 * k + c, 2 * (k ^ s) + c) for k in range(groups) for c, s in enumerate((first, second))]


def local(embeddings, cluster_ids, order_index):
    rows = embeddings.shape[0]
    groups, length = lax.axis_size("group"), lax.axis_size("z")
    z, core = lax.axis_index("z"), lax.axis_index("core")
    plane_axes, line_axes = ("group", "core"), ("z", "core")
    own = pack(embeddings, cluster_ids, order_index)
    both = pair(own, swap(own))

    routes = [ring_pairs(length, shift) for shift in range(1, length // 2 + 1)]
    trips = []
    for first in range(0, len(routes), 2):
        ways = enumerate(routes[first : first + 2])
        trips.append([(2 * a + way, 2 * b + way) for way, route in ways for a, b in route])
    visitors = [lax.ppermute(both, line_axes, trip) for trip in trips]

    partners = [(s, s + 1) for s in range(1, groups - 1, 2)]
    arrived = [lax.ppermute(both, plane_axes, group_trip(groups, *way)) for way in partners]
    last = groups - 1
    relay = group_trip(groups, last ^ partners[-1][0], last ^ partners[-1][1])
    half = rows // 2
    corner = [arrived[-1][first : first + half] for first in (0, half)]
    corner = [lax.ppermute(part, plane_axes, relay) for part in corner]
    sides = [(block, swap(block)) for block in arrived]
    chunks = [[both, *sides[-1], *corner, *(swap(part) for part in corner)]]
    chunks += [[*sides[k], *sides[k + 1]] for k in range(0, len(sides) - 1, 2)]

    orders = [((2, 5, 6, 0), (4, 3, 7, 1))] + [((0, 3, 4, 7), (2, 1, 6, 5))] * (len(chunks) - 1)
    bests, answers = [], []
    for chunk in chunks:
        bests += call(own_kernel, [own, *chunk], 1, [1], 8 * rows)
    for index, (chunk, order) in enumerate(zip(chunks, orders)):
        kernel = functools.partial(visit_kernel, len(visitors), len(chunk), *order)
        count = 2 * len(visitors)
        operands = [*visitors, *chunk, bests[index]]
        answers.append(call(kernel, operands, count, [count, 4, 4], 8 * rows))
    home = functools.reduce(jnp.maximum, [answer[0] for answer in answers])
    merged = [jnp.maximum(mine, swap(others)) for _, mine, others in answers]

    for index, trip in enumerate(trips):
        part = home[2 * index : 2 * index + 2] if len(trips) > 1 else home
        back = lax.ppermute(part, line_axes, [(b, a) for a, b in trip])
        for here, best in ((2 * z + core, back[0:1]), (2 * z + (core ^ 1), swap(back)[1:2])):
            sent = functools.reduce(jnp.logical_or, [here == a for a, _ in trip])
            bests.append(jnp.where(sent, best, -1.0))
    ways = [(0, 0, partners[-1])]
    ways += [(1 + k // 2, 2 * (k % 2), way) for k, way in enumerate(partners[:-1])]
    for chunk, row, (first, second) in ways:
        for order in ((first, second), (second, first)):
            got = lax.ppermute(merged[chunk], plane_axes, group_trip(groups, *order))
            bests.append(got[row : row + 1])
            row += 1
    bests.append(lax.ppermute(merged[0], "group", flip(groups, last))[2:3])
    bests.append(merged[0][3:4])
    return functools.reduce(jnp.maximum, bests)[0, :rows]


def solution(mesh):
    groups, members = mesh.devices.shape
    fine = Mesh(mesh.devices.reshape(groups, members // 2, 2), AXES)
    placed = (P(AXES, None), P(AXES), P(AXES))
    return jax.shard_map(local, mesh=fine, in_specs=placed, out_specs=P(AXES), check_vma=False)
```

```python
import functools

import jax
import jax.numpy as jnp
from jax import lax
from jax.experimental import pallas as pl
from jax.experimental.pallas import tpu as pltpu
from jax.sharding import Mesh, PartitionSpec as P

AXES = ("group", "z", "core")
LANES = 128
CHUNK = 512
VMEM = pl.BlockSpec(memory_space=pltpu.VMEM)


def flip(count, bits):
    return [(k, k ^ bits) for k in range(count)]


def unit_rows(values):
    values = values.astype(jnp.float32)
    total = jnp.sum(values * values, axis=1, keepdims=True) + values.shape[1] * 1e-06
    return (values * lax.rsqrt(total)).astype(jnp.bfloat16)


def ring_pairs(length, shift):
    if 2 * shift < length:
        return [(k, (k + shift) % length) for k in range(length)]
    pairs = [(k, k + shift) for k in range(length // 2)]
    return [pair[:: 1 - 2 * (pair[0] % 2)] for pair in pairs]


def swap(block):
    return lax.ppermute(block, "core", flip(2, 1))


def pack_into(block_ref, start, rows, ids):
    count, width = rows.shape
    place = pl.ds(start, count)
    block_ref[place, :width] = unit_rows(rows)
    meta = jnp.concatenate([ids.astype(jnp.float32), jnp.zeros((6, count), jnp.float32)], axis=0)
    if count < LANES:
        meta = jnp.concatenate([meta, jnp.zeros((8, LANES - count), jnp.float32)], axis=1)
    turned = meta.T[:count]
    cluster, order = turned[:, 0:1] + 1.0, turned[:, 1:2]
    high = jnp.floor(order / 256.0)
    lane = lax.broadcasted_iota(jnp.int32, (count, LANES), 1)
    tail = jnp.where(lane == 0, cluster, jnp.where(lane == 1, high, order - 256.0 * high))
    block_ref[place, width:] = jnp.where(lane < 3, tail, 0.0).astype(jnp.bfloat16)


def pack_kernel(rows_ref, ids_ref, block_ref):
    pack_into(block_ref, 0, rows_ref[...], ids_ref[...])


def pair_kernel(own_ref, rows_ref, ids_ref, both_ref):
    count = own_ref.shape[0]
    both_ref[:count, :] = own_ref[...]
    pack_into(both_ref, count, rows_ref[...], ids_ref[...])


def pack(kernel, operands, count):
    rows, width = operands[-2].shape
    return pl.pallas_call(
        kernel,
        in_specs=[VMEM] * len(operands),
        out_specs=VMEM,
        out_shape=jax.ShapeDtypeStruct((count * rows, width + LANES), jnp.bfloat16),
        compiler_params=pltpu.CompilerParams(vmem_limit_bytes=8 * 2**20),
        cost_estimate=pl.CostEstimate(
            flops=4 * rows * width, bytes_accessed=4 * rows * width, transcendentals=rows
        ),
    )(*operands)


def own_kernel(*refs):
    row_ref, *scratch = refs[-3:]
    best, _ = best_of(refs[:1], refs[1:-3], refs[0].shape[0], False, *scratch)
    row_ref[...] = best[0]


def visit_kernel(visitors, arrays, mine, others, *refs):
    block_refs = refs[visitors : visitors + arrays]
    row_ref, mine_ref, other_ref, *scratch = refs[visitors + arrays + 1 :]
    rows = refs[0].shape[0] // 2
    bests, cols = best_of(refs[:visitors], block_refs, rows, True, *scratch)
    for v, best in enumerate(bests):
        row_ref[v : v + 1, :] = best
    for ref, picked in ((mine_ref, mine), (other_ref, others)):
        for row, j in enumerate(picked):
            ref[row : row + 1, :] = cols[j]


def best_of(visitor_refs, block_refs, rows, homed, units, dots):
    width = units.shape[1]

    meta = []
    for ref in visitor_refs:
        for source in range(0, ref.shape[0], rows):
            place, source = len(meta) * LANES, pl.ds(source, rows)
            units[place : place + rows, :] = ref[source, :width]
            tail = ref[source, width:].astype(jnp.float32)
            if rows < LANES:
                spare = LANES - rows
                units[place + rows : place + LANES, :] = jnp.zeros((spare, width), jnp.bfloat16)
                tail = jnp.concatenate([tail, jnp.zeros((spare, LANES), jnp.float32)], axis=0)
            turned = tail.T
            meta.append((turned[0:1], turned[1:2] * 256.0 + turned[2:3]))
    for k in range(0, width, CHUNK):
        left = jnp.concatenate([ref[:, k : k + CHUNK] for ref in block_refs], axis=0)
        part = lax.dot_general(
            left,
            units[:, k : k + CHUNK],
            (((1,), (1,)), ((), ())),
            preferred_element_type=jnp.float32,
        )
        dots[...] = part if k == 0 else dots[...] + part

    tails = jnp.concatenate([ref[:, width:] for ref in block_refs], axis=0).astype(jnp.float32)
    row_best = [jnp.full((1, LANES), -1.0, jnp.float32) for _ in meta]
    lane = lax.broadcasted_iota(jnp.int32, (rows, LANES), 1)
    col_all = jnp.full((rows, LANES), -1.0, jnp.float32)
    for j in range(dots.shape[0] // rows):
        tail = tails[j * rows : (j + 1) * rows]
        block_cluster, block_order = tail[:, 0:1], tail[:, 1:2] * 256.0 + tail[:, 2:3]
        col_best = jnp.full((rows, 1), -1.0, jnp.float32)
        for v, (cluster, order) in enumerate(meta):
            cosine = dots[j * rows : (j + 1) * rows, v * LANES : (v + 1) * LANES]
            same = (block_cluster == cluster) & (cluster > 0)
            seen = jnp.where(same & (block_order < order), cosine, -1.0)
            row_best[v] = jnp.maximum(row_best[v], jnp.max(seen, axis=0, keepdims=True))
            if homed:
                seen = jnp.where(same & (order < block_order), cosine, -1.0)
                col_best = jnp.maximum(col_best, jnp.max(seen, axis=1, keepdims=True))
        col_all = jnp.where(lane == j, col_best, col_all)
    if not homed:
        return row_best, None
    if rows < LANES:
        fill = jnp.full((LANES - rows, LANES), -1.0, jnp.float32)
        col_all = jnp.concatenate([col_all, fill], axis=0)
    turned = col_all.T
    return row_best, [turned[j : j + 1] for j in range(dots.shape[0] // rows)]


def call(kernel, operands, count, out_rows, total):
    width = operands[0].shape[1] - LANES
    return pl.pallas_call(
        kernel,
        in_specs=[VMEM] * len(operands),
        out_specs=[VMEM] * len(out_rows),
        out_shape=[jax.ShapeDtypeStruct((n, LANES), jnp.float32) for n in out_rows],
        scratch_shapes=[
            pltpu.VMEM((count * LANES, width), jnp.bfloat16),
            pltpu.VMEM((total, count * LANES), jnp.float32),
        ],
        compiler_params=pltpu.CompilerParams(vmem_limit_bytes=24 * 2**20),
        cost_estimate=pl.CostEstimate(
            flops=2 * total * count * LANES * width,
            bytes_accessed=2 * (total + count * LANES) * width,
            transcendentals=0,
        ),
    )(*operands)


def group_trip(groups, first, second):
    return [(2 * k + c, 2 * (k ^ s) + c) for k in range(groups) for c, s in enumerate((first, second))]


def local(embeddings, cluster_ids, order_index):
    rows = embeddings.shape[0]
    groups, length = lax.axis_size("group"), lax.axis_size("z")
    z, core = lax.axis_index("z"), lax.axis_index("core")
    plane_axes, line_axes = ("group", "core"), ("z", "core")
    ids = jnp.stack([cluster_ids, order_index])
    own = pack(pack_kernel, [embeddings, ids], 1)
    both = pack(pair_kernel, [own, swap(embeddings), swap(ids)], 2)

    routes = [ring_pairs(length, shift) for shift in range(1, length // 2 + 1)]
    trips = []
    for first in range(0, len(routes), 2):
        ways = enumerate(routes[first : first + 2])
        trips.append([(2 * a + way, 2 * b + way) for way, route in ways for a, b in route])
    visitors = [lax.ppermute(both, line_axes, trip) for trip in trips]

    partners = [(s, s + 1) for s in range(1, groups - 1, 2)]
    arrived = [lax.ppermute(both, plane_axes, group_trip(groups, *way)) for way in partners]
    last = groups - 1
    relay = group_trip(groups, last ^ partners[-1][0], last ^ partners[-1][1])
    half = rows // 2
    corner = [arrived[-1][first : first + half] for first in (0, half)]
    corner = [lax.ppermute(part, plane_axes, relay) for part in corner]
    sides = [(block, swap(block)) for block in arrived]
    chunks = [[both, *sides[-1], *corner, *(swap(part) for part in corner)]]
    chunks += [[*sides[k], *sides[k + 1]] for k in range(0, len(sides) - 1, 2)]

    orders = [((2, 5, 6, 0), (4, 3, 7, 1))] + [((0, 3, 4, 7), (2, 1, 6, 5))] * (len(chunks) - 1)
    bests, answers = [], []
    for chunk in chunks:
        bests += call(own_kernel, [own, *chunk], 1, [1], 8 * rows)
    for index, (chunk, order) in enumerate(zip(chunks, orders)):
        kernel = functools.partial(visit_kernel, len(visitors), len(chunk), *order)
        count = 2 * len(visitors)
        operands = [*visitors, *chunk, bests[index]]
        answers.append(call(kernel, operands, count, [count, 4, 4], 8 * rows))
    home = functools.reduce(jnp.maximum, [answer[0] for answer in answers])
    merged = [jnp.maximum(mine, swap(others)) for _, mine, others in answers]

    for index, trip in enumerate(trips):
        part = home[2 * index : 2 * index + 2] if len(trips) > 1 else home
        back = lax.ppermute(part, line_axes, [(b, a) for a, b in trip])
        for here, best in ((2 * z + core, back[0:1]), (2 * z + (core ^ 1), swap(back)[1:2])):
            sent = functools.reduce(jnp.logical_or, [here == a for a, _ in trip])
            bests.append(jnp.where(sent, best, -1.0))
    bests.append(lax.ppermute(merged[0], "group", flip(groups, last))[2:3])
    ways = [(0, 0, partners[-1])]
    ways += [(1 + k // 2, 2 * (k % 2), way) for k, way in enumerate(partners[:-1])]
    for chunk, row, (first, second) in ways:
        for order in ((first, second), (second, first)):
            got = lax.ppermute(merged[chunk], plane_axes, group_trip(groups, *order))
            bests.append(got[row : row + 1])
            row += 1
    bests.append(merged[0][3:4])
    return functools.reduce(jnp.maximum, bests)[0, :rows]


def solution(mesh):
    groups, members = mesh.devices.shape
    fine = Mesh(mesh.devices.reshape(groups, members // 2, 2), AXES)
    placed = (P(AXES, None), P(AXES), P(AXES))
    return jax.shard_map(local, mesh=fine, in_specs=placed, out_specs=P(AXES), check_vma=False)
```

```python
import functools

import jax
import jax.numpy as jnp
from jax import lax
from jax.experimental import pallas as pl
from jax.experimental.pallas import tpu as pltpu
from jax.sharding import Mesh, PartitionSpec as P

AXES = ("group", "z", "core")
LANES = 128
CHUNK = 512
VMEM = pl.BlockSpec(memory_space=pltpu.VMEM)


def flip(count, bits):
    return [(k, k ^ bits) for k in range(count)]


def unit_rows(values):
    values = values.astype(jnp.float32)
    total = jnp.sum(values * values, axis=1, keepdims=True) + values.shape[1] * 1e-06
    return (values * lax.rsqrt(total)).astype(jnp.bfloat16)


def line_trips(length):
    if length == 4:
        ways = [[(0, 1), (2, 3), (3, 0)], [(0, 2), (2, 1), (1, 3)]]
    else:
        ways = [[(k, (k + shift) % length) for k in range(length)] for shift in range(1, (length + 1) // 2)]
        if length % 2 == 0:
            pairs = [(k, k + length // 2) for k in range(length // 2)]
            ways.append([pair[:: 1 - 2 * (pair[0] % 2)] for pair in pairs])
    return [
        [(2 * a + core, 2 * b + core) for core, way in enumerate(ways[first : first + 2]) for a, b in way]
        for first in range(0, len(ways), 2)
    ]


def swap(block):
    return lax.ppermute(block, "core", flip(2, 1))


def pack_into(block_ref, start, rows, ids):
    count, width = rows.shape
    place = pl.ds(start, count)
    block_ref[place, :width] = unit_rows(rows)
    meta = jnp.concatenate([ids.astype(jnp.float32), jnp.zeros((6, count), jnp.float32)], axis=0)
    if count < LANES:
        meta = jnp.concatenate([meta, jnp.zeros((8, LANES - count), jnp.float32)], axis=1)
    turned = meta.T[:count]
    cluster, order = turned[:, 0:1] + 1.0, turned[:, 1:2]
    high = jnp.floor(order / 256.0)
    lane = lax.broadcasted_iota(jnp.int32, (count, LANES), 1)
    tail = jnp.where(lane == 0, cluster, jnp.where(lane == 1, high, order - 256.0 * high))
    block_ref[place, width:] = jnp.where(lane < 3, tail, 0.0).astype(jnp.bfloat16)


def pack_kernel(rows_ref, ids_ref, block_ref):
    pack_into(block_ref, 0, rows_ref[...], ids_ref[...])


def pair_kernel(own_ref, rows_ref, ids_ref, both_ref):
    count = own_ref.shape[0]
    both_ref[:count, :] = own_ref[...]
    pack_into(both_ref, count, rows_ref[...], ids_ref[...])


def pack(kernel, operands, count):
    rows, width = operands[-2].shape
    return pl.pallas_call(
        kernel,
        in_specs=[VMEM] * len(operands),
        out_specs=VMEM,
        out_shape=jax.ShapeDtypeStruct((count * rows, width + LANES), jnp.bfloat16),
        compiler_params=pltpu.CompilerParams(vmem_limit_bytes=8 * 2**20),
        cost_estimate=pl.CostEstimate(
            flops=4 * rows * width, bytes_accessed=4 * rows * width, transcendentals=rows
        ),
    )(*operands)


def own_kernel(*refs):
    row_ref, *scratch = refs[-3:]
    best, _ = best_of(refs[:1], refs[1:-3], refs[0].shape[0], False, *scratch)
    row_ref[...] = best[0]


def visit_kernel(visitors, arrays, mine, others, *refs):
    block_refs = refs[visitors : visitors + arrays]
    row_ref, mine_ref, other_ref, *scratch = refs[visitors + arrays + 1 :]
    rows = refs[0].shape[0] // 2
    bests, cols = best_of(refs[:visitors], block_refs, rows, True, *scratch)
    for v, best in enumerate(bests):
        row_ref[v : v + 1, :] = best
    for ref, picked in ((mine_ref, mine), (other_ref, others)):
        for row, j in enumerate(picked):
            ref[row : row + 1, :] = cols[j]


def best_of(visitor_refs, block_refs, rows, homed, units, dots):
    width = units.shape[1]

    meta = []
    for ref in visitor_refs:
        for source in range(0, ref.shape[0], rows):
            place, source = len(meta) * LANES, pl.ds(source, rows)
            units[place : place + rows, :] = ref[source, :width]
            tail = ref[source, width:].astype(jnp.float32)
            if rows < LANES:
                spare = LANES - rows
                units[place + rows : place + LANES, :] = jnp.zeros((spare, width), jnp.bfloat16)
                tail = jnp.concatenate([tail, jnp.zeros((spare, LANES), jnp.float32)], axis=0)
            turned = tail.T
            meta.append((turned[0:1], turned[1:2] * 256.0 + turned[2:3]))
    for k in range(0, width, CHUNK):
        left = jnp.concatenate([ref[:, k : k + CHUNK] for ref in block_refs], axis=0)
        part = lax.dot_general(
            left,
            units[:, k : k + CHUNK],
            (((1,), (1,)), ((), ())),
            preferred_element_type=jnp.float32,
        )
        dots[...] = part if k == 0 else dots[...] + part

    tails = jnp.concatenate([ref[:, width:] for ref in block_refs], axis=0).astype(jnp.float32)
    row_best = [jnp.full((1, LANES), -1.0, jnp.float32) for _ in meta]
    lane = lax.broadcasted_iota(jnp.int32, (rows, LANES), 1)
    col_all = jnp.full((rows, LANES), -1.0, jnp.float32)
    for j in range(dots.shape[0] // rows):
        tail = tails[j * rows : (j + 1) * rows]
        block_cluster, block_order = tail[:, 0:1], tail[:, 1:2] * 256.0 + tail[:, 2:3]
        col_best = jnp.full((rows, 1), -1.0, jnp.float32)
        for v, (cluster, order) in enumerate(meta):
            cosine = dots[j * rows : (j + 1) * rows, v * LANES : (v + 1) * LANES]
            same = (block_cluster == cluster) & (cluster > 0)
            seen = jnp.where(same & (block_order < order), cosine, -1.0)
            row_best[v] = jnp.maximum(row_best[v], jnp.max(seen, axis=0, keepdims=True))
            if homed:
                seen = jnp.where(same & (order < block_order), cosine, -1.0)
                col_best = jnp.maximum(col_best, jnp.max(seen, axis=1, keepdims=True))
        col_all = jnp.where(lane == j, col_best, col_all)
    if not homed:
        return row_best, None
    if rows < LANES:
        fill = jnp.full((LANES - rows, LANES), -1.0, jnp.float32)
        col_all = jnp.concatenate([col_all, fill], axis=0)
    turned = col_all.T
    return row_best, [turned[j : j + 1] for j in range(dots.shape[0] // rows)]


def call(kernel, operands, count, out_rows, total):
    width = operands[0].shape[1] - LANES
    return pl.pallas_call(
        kernel,
        in_specs=[VMEM] * len(operands),
        out_specs=[VMEM] * len(out_rows),
        out_shape=[jax.ShapeDtypeStruct((n, LANES), jnp.float32) for n in out_rows],
        scratch_shapes=[
            pltpu.VMEM((count * LANES, width), jnp.bfloat16),
            pltpu.VMEM((total, count * LANES), jnp.float32),
        ],
        compiler_params=pltpu.CompilerParams(vmem_limit_bytes=24 * 2**20),
        cost_estimate=pl.CostEstimate(
            flops=2 * total * count * LANES * width,
            bytes_accessed=2 * (total + count * LANES) * width,
            transcendentals=0,
        ),
    )(*operands)


def group_trip(groups, first, second):
    return [(2 * k + c, 2 * (k ^ s) + c) for k in range(groups) for c, s in enumerate((first, second))]


def local(embeddings, cluster_ids, order_index):
    rows = embeddings.shape[0]
    groups, length = lax.axis_size("group"), lax.axis_size("z")
    z, core = lax.axis_index("z"), lax.axis_index("core")
    plane_axes, line_axes = ("group", "core"), ("z", "core")
    ids = jnp.stack([cluster_ids, order_index])
    own = pack(pack_kernel, [embeddings, ids], 1)
    both = pack(pair_kernel, [own, swap(embeddings), swap(ids)], 2)

    trips = line_trips(length)
    visitors = [lax.ppermute(both, line_axes, trip) for trip in trips]

    partners = [(s, s + 1) for s in range(1, groups - 1, 2)]
    arrived = [lax.ppermute(both, plane_axes, group_trip(groups, *way)) for way in partners]
    last = groups - 1
    relay = group_trip(groups, last ^ partners[-1][0], last ^ partners[-1][1])
    half = rows // 2
    corner = [arrived[-1][first : first + half] for first in (0, half)]
    corner = [lax.ppermute(part, plane_axes, relay) for part in corner]
    sides = [(block, swap(block)) for block in arrived]
    chunks = [[both, *sides[-1], *corner, *(swap(part) for part in corner)]]
    chunks += [[*sides[k], *sides[k + 1]] for k in range(0, len(sides) - 1, 2)]

    orders = [((2, 5, 6, 0), (4, 3, 7, 1))] + [((0, 3, 4, 7), (2, 1, 6, 5))] * (len(chunks) - 1)
    bests, answers = [], []
    for chunk in chunks:
        bests += call(own_kernel, [own, *chunk], 1, [1], 8 * rows)
    for index, (chunk, order) in enumerate(zip(chunks, orders)):
        kernel = functools.partial(visit_kernel, len(visitors), len(chunk), *order)
        count = 2 * len(visitors)
        operands = [*visitors, *chunk, bests[index]]
        answers.append(call(kernel, operands, count, [count, 4, 4], 8 * rows))
    home = functools.reduce(jnp.maximum, [answer[0] for answer in answers])
    merged = [jnp.maximum(mine, swap(others)) for _, mine, others in answers]

    for index, trip in enumerate(trips):
        part = home[2 * index : 2 * index + 2] if len(trips) > 1 else home
        back = lax.ppermute(part, line_axes, [(b, a) for a, b in trip])
        for here, best in ((2 * z + core, back[0:1]), (2 * z + (core ^ 1), swap(back)[1:2])):
            sent = functools.reduce(jnp.logical_or, [here == a for a, _ in trip])
            bests.append(jnp.where(sent, best, -1.0))
    bests.append(lax.ppermute(merged[0], "group", flip(groups, last))[2:3])
    ways = [(0, 0, partners[-1])]
    ways += [(1 + k // 2, 2 * (k % 2), way) for k, way in enumerate(partners[:-1])]
    for chunk, row, (first, second) in ways:
        for order in ((first, second), (second, first)):
            got = lax.ppermute(merged[chunk], plane_axes, group_trip(groups, *order))
            bests.append(got[row : row + 1])
            row += 1
    bests.append(merged[0][3:4])
    return functools.reduce(jnp.maximum, bests)[0, :rows]


def solution(mesh):
    groups, members = mesh.devices.shape
    fine = Mesh(mesh.devices.reshape(groups, members // 2, 2), AXES)
    placed = (P(AXES, None), P(AXES), P(AXES))
    return jax.shard_map(local, mesh=fine, in_specs=placed, out_specs=P(AXES), check_vma=False)
```

```python
import functools

import jax
import jax.numpy as jnp
from jax import lax
from jax.experimental import pallas as pl
from jax.experimental.pallas import tpu as pltpu
from jax.sharding import Mesh, PartitionSpec as P

AXES = ("group", "z", "core")
LANES = 128
CHUNK = 512
VMEM = pl.BlockSpec(memory_space=pltpu.VMEM)


def flip(count, bits):
    return [(k, k ^ bits) for k in range(count)]


def unit_rows(values):
    values = values.astype(jnp.float32)
    total = jnp.sum(values * values, axis=1, keepdims=True) + values.shape[1] * 1e-06
    return (values * lax.rsqrt(total)).astype(jnp.bfloat16)


def line_trips(length):
    if length == 4:
        ways = [[(0, 1), (1, 3), (3, 2), (2, 0)], [(3, 0), (1, 2)]]
    else:
        ways = [[(k, (k + shift) % length) for k in range(length)] for shift in range(1, (length + 1) // 2)]
        if length % 2 == 0:
            pairs = [(k, k + length // 2) for k in range(length // 2)]
            ways.append([pair[:: 1 - 2 * (pair[0] % 2)] for pair in pairs])
    return [
        [(2 * a + core, 2 * b + core) for core, way in enumerate(ways[first : first + 2]) for a, b in way]
        for first in range(0, len(ways), 2)
    ]


def swap(block):
    return lax.ppermute(block, "core", flip(2, 1))


def pack_into(block_ref, start, rows, ids):
    count, width = rows.shape
    place = pl.ds(start, count)
    block_ref[place, :width] = unit_rows(rows)
    meta = jnp.concatenate([ids.astype(jnp.float32), jnp.zeros((6, count), jnp.float32)], axis=0)
    if count < LANES:
        meta = jnp.concatenate([meta, jnp.zeros((8, LANES - count), jnp.float32)], axis=1)
    turned = meta.T[:count]
    cluster, order = turned[:, 0:1] + 1.0, turned[:, 1:2]
    high = jnp.floor(order / 256.0)
    lane = lax.broadcasted_iota(jnp.int32, (count, LANES), 1)
    tail = jnp.where(lane == 0, cluster, jnp.where(lane == 1, high, order - 256.0 * high))
    block_ref[place, width:] = jnp.where(lane < 3, tail, 0.0).astype(jnp.bfloat16)


def pack_kernel(rows_ref, ids_ref, block_ref):
    pack_into(block_ref, 0, rows_ref[...], ids_ref[...])


def pair_kernel(own_ref, rows_ref, ids_ref, both_ref):
    count = own_ref.shape[0]
    both_ref[:count, :] = own_ref[...]
    pack_into(both_ref, count, rows_ref[...], ids_ref[...])


def pack(kernel, operands, count):
    rows, width = operands[-2].shape
    return pl.pallas_call(
        kernel,
        in_specs=[VMEM] * len(operands),
        out_specs=VMEM,
        out_shape=jax.ShapeDtypeStruct((count * rows, width + LANES), jnp.bfloat16),
        compiler_params=pltpu.CompilerParams(vmem_limit_bytes=8 * 2**20),
        cost_estimate=pl.CostEstimate(
            flops=4 * rows * width, bytes_accessed=4 * rows * width, transcendentals=rows
        ),
    )(*operands)


def own_kernel(*refs):
    row_ref, *scratch = refs[-3:]
    best, _ = best_of(refs[:1], refs[1:-3], refs[0].shape[0], False, *scratch)
    row_ref[...] = best[0]


def visit_kernel(visitors, arrays, mine, others, *refs):
    block_refs = refs[visitors : visitors + arrays]
    row_ref, mine_ref, other_ref, *scratch = refs[visitors + arrays + 1 :]
    rows = refs[0].shape[0] // 2
    bests, cols = best_of(refs[:visitors], block_refs, rows, True, *scratch)
    for v, best in enumerate(bests):
        row_ref[v : v + 1, :] = best
    for ref, picked in ((mine_ref, mine), (other_ref, others)):
        for row, j in enumerate(picked):
            ref[row : row + 1, :] = cols[j]


def best_of(visitor_refs, block_refs, rows, homed, units, dots):
    width = units.shape[1]

    meta = []
    for ref in visitor_refs:
        for source in range(0, ref.shape[0], rows):
            place, source = len(meta) * LANES, pl.ds(source, rows)
            units[place : place + rows, :] = ref[source, :width]
            tail = ref[source, width:].astype(jnp.float32)
            if rows < LANES:
                spare = LANES - rows
                units[place + rows : place + LANES, :] = jnp.zeros((spare, width), jnp.bfloat16)
                tail = jnp.concatenate([tail, jnp.zeros((spare, LANES), jnp.float32)], axis=0)
            turned = tail.T
            meta.append((turned[0:1], turned[1:2] * 256.0 + turned[2:3]))
    for k in range(0, width, CHUNK):
        left = jnp.concatenate([ref[:, k : k + CHUNK] for ref in block_refs], axis=0)
        part = lax.dot_general(
            left,
            units[:, k : k + CHUNK],
            (((1,), (1,)), ((), ())),
            preferred_element_type=jnp.float32,
        )
        dots[...] = part if k == 0 else dots[...] + part

    tails = jnp.concatenate([ref[:, width:] for ref in block_refs], axis=0).astype(jnp.float32)
    row_best = [jnp.full((1, LANES), -1.0, jnp.float32) for _ in meta]
    lane = lax.broadcasted_iota(jnp.int32, (rows, LANES), 1)
    col_all = jnp.full((rows, LANES), -1.0, jnp.float32)
    for j in range(dots.shape[0] // rows):
        tail = tails[j * rows : (j + 1) * rows]
        block_cluster, block_order = tail[:, 0:1], tail[:, 1:2] * 256.0 + tail[:, 2:3]
        col_best = jnp.full((rows, 1), -1.0, jnp.float32)
        for v, (cluster, order) in enumerate(meta):
            cosine = dots[j * rows : (j + 1) * rows, v * LANES : (v + 1) * LANES]
            same = (block_cluster == cluster) & (cluster > 0)
            seen = jnp.where(same & (block_order < order), cosine, -1.0)
            row_best[v] = jnp.maximum(row_best[v], jnp.max(seen, axis=0, keepdims=True))
            if homed:
                seen = jnp.where(same & (order < block_order), cosine, -1.0)
                col_best = jnp.maximum(col_best, jnp.max(seen, axis=1, keepdims=True))
        col_all = jnp.where(lane == j, col_best, col_all)
    if not homed:
        return row_best, None
    if rows < LANES:
        fill = jnp.full((LANES - rows, LANES), -1.0, jnp.float32)
        col_all = jnp.concatenate([col_all, fill], axis=0)
    turned = col_all.T
    return row_best, [turned[j : j + 1] for j in range(dots.shape[0] // rows)]


def call(kernel, operands, count, out_rows, total):
    width = operands[0].shape[1] - LANES
    return pl.pallas_call(
        kernel,
        in_specs=[VMEM] * len(operands),
        out_specs=[VMEM] * len(out_rows),
        out_shape=[jax.ShapeDtypeStruct((n, LANES), jnp.float32) for n in out_rows],
        scratch_shapes=[
            pltpu.VMEM((count * LANES, width), jnp.bfloat16),
            pltpu.VMEM((total, count * LANES), jnp.float32),
        ],
        compiler_params=pltpu.CompilerParams(vmem_limit_bytes=24 * 2**20),
        cost_estimate=pl.CostEstimate(
            flops=2 * total * count * LANES * width,
            bytes_accessed=2 * (total + count * LANES) * width,
            transcendentals=0,
        ),
    )(*operands)


def group_trip(groups, first, second):
    return [(2 * k + c, 2 * (k ^ s) + c) for k in range(groups) for c, s in enumerate((first, second))]


def local(embeddings, cluster_ids, order_index):
    rows = embeddings.shape[0]
    groups, length = lax.axis_size("group"), lax.axis_size("z")
    z, core = lax.axis_index("z"), lax.axis_index("core")
    plane_axes, line_axes = ("group", "core"), ("z", "core")
    ids = jnp.stack([cluster_ids, order_index])
    own = pack(pack_kernel, [embeddings, ids], 1)
    both = pack(pair_kernel, [own, swap(embeddings), swap(ids)], 2)

    trips = line_trips(length)
    visitors = [lax.ppermute(both, line_axes, trip) for trip in trips]

    partners = [(s, s + 1) for s in range(1, groups - 1, 2)]
    arrived = [lax.ppermute(both, plane_axes, group_trip(groups, *way)) for way in partners]
    last = groups - 1
    relay = group_trip(groups, last ^ partners[-1][0], last ^ partners[-1][1])
    half = rows // 2
    corner = [arrived[-1][first : first + half] for first in (0, half)]
    corner = [lax.ppermute(part, plane_axes, relay) for part in corner]
    sides = [(block, swap(block)) for block in arrived]
    chunks = [[both, *sides[-1], *corner, *(swap(part) for part in corner)]]
    chunks += [[*sides[k], *sides[k + 1]] for k in range(0, len(sides) - 1, 2)]

    orders = [((2, 5, 6, 0), (4, 3, 7, 1))] + [((0, 3, 4, 7), (2, 1, 6, 5))] * (len(chunks) - 1)
    bests, answers = [], []
    for chunk in chunks:
        bests += call(own_kernel, [own, *chunk], 1, [1], 8 * rows)
    for index, (chunk, order) in enumerate(zip(chunks, orders)):
        kernel = functools.partial(visit_kernel, len(visitors), len(chunk), *order)
        count = 2 * len(visitors)
        operands = [*visitors, *chunk, bests[index]]
        answers.append(call(kernel, operands, count, [count, 4, 4], 8 * rows))
    home = functools.reduce(jnp.maximum, [answer[0] for answer in answers])
    merged = [jnp.maximum(mine, swap(others)) for _, mine, others in answers]

    for index, trip in enumerate(trips):
        part = home[2 * index : 2 * index + 2] if len(trips) > 1 else home
        back = lax.ppermute(part, line_axes, [(b, a) for a, b in trip])
        for here, best in ((2 * z + core, back[0:1]), (2 * z + (core ^ 1), swap(back)[1:2])):
            sent = functools.reduce(jnp.logical_or, [here == a for a, _ in trip])
            bests.append(jnp.where(sent, best, -1.0))
    bests.append(lax.ppermute(merged[0], "group", flip(groups, last))[2:3])
    ways = [(0, 0, partners[-1])]
    ways += [(1 + k // 2, 2 * (k % 2), way) for k, way in enumerate(partners[:-1])]
    for chunk, row, (first, second) in ways:
        for order in ((first, second), (second, first)):
            got = lax.ppermute(merged[chunk], plane_axes, group_trip(groups, *order))
            bests.append(got[row : row + 1])
            row += 1
    bests.append(merged[0][3:4])
    return functools.reduce(jnp.maximum, bests)[0, :rows]


def solution(mesh):
    groups, members = mesh.devices.shape
    fine = Mesh(mesh.devices.reshape(groups, members // 2, 2), AXES)
    placed = (P(AXES, None), P(AXES), P(AXES))
    return jax.shard_map(local, mesh=fine, in_specs=placed, out_specs=P(AXES), check_vma=False)
```

```python
import functools

import jax
import jax.numpy as jnp
from jax import lax
from jax.experimental import pallas as pl
from jax.experimental.pallas import tpu as pltpu
from jax.sharding import Mesh, PartitionSpec as P

AXES = ("group", "z", "core")
LANES = 128
CHUNK = 512
TAIL = 16
VMEM = pl.BlockSpec(memory_space=pltpu.VMEM)


def flip(count, bits):
    return [(k, k ^ bits) for k in range(count)]


def unit_rows(values):
    values = values.astype(jnp.float32)
    total = jnp.sum(values * values, axis=1, keepdims=True) + values.shape[1] * 1e-06
    return (values * lax.rsqrt(total)).astype(jnp.bfloat16)


def ring_pairs(length, shift):
    if 2 * shift < length:
        return [(k, (k + shift) % length) for k in range(length)]
    pairs = [(k, k + shift) for k in range(length // 2)]
    return [pair[:: 1 - 2 * (pair[0] % 2)] for pair in pairs]


def swap(block):
    return lax.ppermute(block, "core", flip(2, 1))


def pack_into(block_ref, start, rows, ids):
    count, width = rows.shape
    place = pl.ds(start, count)
    block_ref[place, :width] = unit_rows(rows)
    meta = jnp.concatenate([ids.astype(jnp.float32), jnp.zeros((6, count), jnp.float32)], axis=0)
    if count < LANES:
        meta = jnp.concatenate([meta, jnp.zeros((8, LANES - count), jnp.float32)], axis=1)
    turned = meta.T[:count]
    cluster, order = turned[:, 0:1] + 1.0, turned[:, 1:2]
    high = jnp.floor(order / 256.0)
    lane = lax.broadcasted_iota(jnp.int32, (count, LANES), 1)
    tail = jnp.where(lane == 0, cluster, jnp.where(lane == 1, high, order - 256.0 * high))
    block_ref[place, width:] = jnp.where(lane < 3, tail, 0.0).astype(jnp.bfloat16)


def pack_kernel(rows_ref, ids_ref, block_ref):
    pack_into(block_ref, 0, rows_ref[...], ids_ref[...])


def pair_kernel(own_ref, own_ids_ref, rows_ref, ids_ref, both_ref, line_ref):
    count, width = rows_ref.shape
    both_ref[:count, :] = own_ref[...]
    pack_into(both_ref, count, rows_ref[...], ids_ref[...])
    for k in range(width // LANES):
        columns = both_ref[:, k * LANES : (k + 1) * LANES]
        line_ref[2 * count * k : 2 * count * (k + 1), :] = columns
    lines = []
    for ref in (own_ids_ref, ids_ref):
        ids = ref[...].astype(jnp.float32)
        high = jnp.floor(ids[1:2] / 256.0)
        lines += [ids[0:1] + 1.0, high, ids[1:2] - 256.0 * high]
    tail = jnp.concatenate(lines + [jnp.zeros((TAIL - 6, count), jnp.float32)], axis=0)
    if count < LANES:
        tail = jnp.concatenate([tail, jnp.zeros((TAIL, LANES - count), jnp.float32)], axis=1)
    line_ref[2 * count * (width // LANES) :, :] = tail.astype(jnp.bfloat16)


def pack(kernel, operands, shapes):
    rows, width = operands[-2].shape
    return pl.pallas_call(
        kernel,
        in_specs=[VMEM] * len(operands),
        out_specs=[VMEM] * len(shapes),
        out_shape=[jax.ShapeDtypeStruct(shape, jnp.bfloat16) for shape in shapes],
        compiler_params=pltpu.CompilerParams(vmem_limit_bytes=8 * 2**20),
        cost_estimate=pl.CostEstimate(
            flops=4 * rows * width, bytes_accessed=4 * rows * width, transcendentals=rows
        ),
    )(*operands)


def padded(rows):
    spare = -rows.shape[0] % LANES
    if not spare:
        return rows
    return jnp.concatenate([rows, jnp.zeros((spare, rows.shape[1]), rows.dtype)], axis=0)


def own_kernel(*refs):
    own_ref, row_ref, dots = refs[0], *refs[-2:]
    rows, width = own_ref.shape[0], own_ref.shape[1] - LANES
    turned = padded(own_ref[:, width:].astype(jnp.float32)).T
    meta = [(turned[0:1], turned[1:2] * 256.0 + turned[2:3])]

    def visitors_at(k):
        return padded(own_ref[:, k : k + CHUNK])

    bests, _ = best_of(visitors_at, meta, refs[1:-2], rows, False, dots)
    row_ref[...] = bests[0]


def visit_kernel(visitors, arrays, mine, others, *refs):
    line_refs, block_refs = refs[:visitors], refs[visitors : visitors + arrays]
    row_ref, mine_ref, other_ref, dots = refs[visitors + arrays + 1 :]
    width = block_refs[0].shape[1] - LANES
    rows = (line_refs[0].shape[0] - TAIL) // (2 * width // LANES)
    meta = []
    for ref in line_refs:
        tail = ref[2 * rows * (width // LANES) :, :].astype(jnp.float32)
        for row in (0, 3):
            order = tail[row + 1 : row + 2] * 256.0 + tail[row + 2 : row + 3]
            meta.append((tail[row : row + 1], order))

    def visitors_at(k):
        parts = []
        for ref in line_refs:
            for core in range(2):
                starts = [rows * (2 * block + core) for block in range(k // LANES, (k + CHUNK) // LANES)]
                columns = [ref[start : start + rows, :] for start in starts]
                parts.append(padded(jnp.concatenate(columns, axis=1)))
        return jnp.concatenate(parts, axis=0)

    bests, cols = best_of(visitors_at, meta, block_refs, rows, True, dots)
    for v, best in enumerate(bests):
        row_ref[v : v + 1, :] = best
    for ref, picked in ((mine_ref, mine), (other_ref, others)):
        for row, j in enumerate(picked):
            ref[row : row + 1, :] = cols[j]


def best_of(visitors_at, meta, block_refs, rows, homed, dots):
    width = block_refs[0].shape[1] - LANES
    for k in range(0, width, CHUNK):
        left = jnp.concatenate([ref[:, k : k + CHUNK] for ref in block_refs], axis=0)
        part = lax.dot_general(
            left,
            visitors_at(k),
            (((1,), (1,)), ((), ())),
            preferred_element_type=jnp.float32,
        )
        dots[...] = part if k == 0 else dots[...] + part

    tails = jnp.concatenate([ref[:, width:] for ref in block_refs], axis=0).astype(jnp.float32)
    row_best = [jnp.full((1, LANES), -1.0, jnp.float32) for _ in meta]
    lane = lax.broadcasted_iota(jnp.int32, (rows, LANES), 1)
    col_all = jnp.full((rows, LANES), -1.0, jnp.float32)
    for j in range(dots.shape[0] // rows):
        tail = tails[j * rows : (j + 1) * rows]
        block_cluster, block_order = tail[:, 0:1], tail[:, 1:2] * 256.0 + tail[:, 2:3]
        col_best = jnp.full((rows, 1), -1.0, jnp.float32)
        for v, (cluster, order) in enumerate(meta):
            cosine = dots[j * rows : (j + 1) * rows, v * LANES : (v + 1) * LANES]
            same = (block_cluster == cluster) & (cluster > 0)
            seen = jnp.where(same & (block_order < order), cosine, -1.0)
            row_best[v] = jnp.maximum(row_best[v], jnp.max(seen, axis=0, keepdims=True))
            if homed:
                seen = jnp.where(same & (order < block_order), cosine, -1.0)
                col_best = jnp.maximum(col_best, jnp.max(seen, axis=1, keepdims=True))
        col_all = jnp.where(lane == j, col_best, col_all)
    if not homed:
        return row_best, None
    if rows < LANES:
        fill = jnp.full((LANES - rows, LANES), -1.0, jnp.float32)
        col_all = jnp.concatenate([col_all, fill], axis=0)
    turned = col_all.T
    return row_best, [turned[j : j + 1] for j in range(dots.shape[0] // rows)]


def call(kernel, operands, count, out_rows, total, width):
    return pl.pallas_call(
        kernel,
        in_specs=[VMEM] * len(operands),
        out_specs=[VMEM] * len(out_rows),
        out_shape=[jax.ShapeDtypeStruct((n, LANES), jnp.float32) for n in out_rows],
        scratch_shapes=[pltpu.VMEM((total, count * LANES), jnp.float32)],
        compiler_params=pltpu.CompilerParams(vmem_limit_bytes=24 * 2**20),
        cost_estimate=pl.CostEstimate(
            flops=2 * total * count * LANES * width,
            bytes_accessed=2 * (total + count * LANES) * width,
            transcendentals=0,
        ),
    )(*operands)


def group_trip(groups, first, second):
    return [(2 * k + c, 2 * (k ^ s) + c) for k in range(groups) for c, s in enumerate((first, second))]


def local(embeddings, cluster_ids, order_index):
    rows, width = embeddings.shape
    groups, length = lax.axis_size("group"), lax.axis_size("z")
    z, core = lax.axis_index("z"), lax.axis_index("core")
    plane_axes, line_axes = ("group", "core"), ("z", "core")
    ids = jnp.stack([cluster_ids, order_index])
    (own,) = pack(pack_kernel, [embeddings, ids], [(rows, width + LANES)])
    shapes = [(2 * rows, width + LANES), (2 * rows * width // LANES + TAIL, LANES)]
    both, line = pack(pair_kernel, [own, ids, swap(embeddings), swap(ids)], shapes)

    routes = [ring_pairs(length, shift) for shift in range(1, length // 2 + 1)]
    trips = []
    for first in range(0, len(routes), 2):
        ways = enumerate(routes[first : first + 2])
        trips.append([(2 * a + way, 2 * b + way) for way, route in ways for a, b in route])
    visitors = [lax.ppermute(line, line_axes, trip) for trip in trips]

    partners = [(s, s + 1) for s in range(1, groups - 1, 2)]
    arrived = [lax.ppermute(both, plane_axes, group_trip(groups, *way)) for way in partners]
    last = groups - 1
    relay = group_trip(groups, last ^ partners[-1][0], last ^ partners[-1][1])
    half = rows // 2
    corner = [arrived[-1][first : first + half] for first in (0, half)]
    corner = [lax.ppermute(part, plane_axes, relay) for part in corner]
    sides = [(block, swap(block)) for block in arrived]
    chunks = [[both, *sides[-1], *corner, *(swap(part) for part in corner)]]
    chunks += [[*sides[k], *sides[k + 1]] for k in range(0, len(sides) - 1, 2)]

    orders = [((2, 5, 6, 0), (4, 3, 7, 1))] + [((0, 3, 4, 7), (2, 1, 6, 5))] * (len(chunks) - 1)
    bests, answers = [], []
    for chunk in chunks:
        bests += call(own_kernel, [own, *chunk], 1, [1], 8 * rows, width)
    for index, (chunk, order) in enumerate(zip(chunks, orders)):
        kernel = functools.partial(visit_kernel, len(visitors), len(chunk), *order)
        count = 2 * len(visitors)
        operands = [*visitors, *chunk, bests[index]]
        answers.append(call(kernel, operands, count, [count, 4, 4], 8 * rows, width))
    home = functools.reduce(jnp.maximum, [answer[0] for answer in answers])
    merged = [jnp.maximum(mine, swap(others)) for _, mine, others in answers]

    for index, trip in enumerate(trips):
        part = home[2 * index : 2 * index + 2] if len(trips) > 1 else home
        back = lax.ppermute(part, line_axes, [(b, a) for a, b in trip])
        for here, best in ((2 * z + core, back[0:1]), (2 * z + (core ^ 1), swap(back)[1:2])):
            sent = functools.reduce(jnp.logical_or, [here == a for a, _ in trip])
            bests.append(jnp.where(sent, best, -1.0))
    ways = [(0, 0, partners[-1])]
    ways += [(1 + k // 2, 2 * (k % 2), way) for k, way in enumerate(partners[:-1])]
    for chunk, row, (first, second) in ways:
        for order in ((first, second), (second, first)):
            got = lax.ppermute(merged[chunk], plane_axes, group_trip(groups, *order))
            bests.append(got[row : row + 1])
            row += 1
    bests.append(lax.ppermute(merged[0], "group", flip(groups, last))[2:3])
    bests.append(merged[0][3:4])
    return functools.reduce(jnp.maximum, bests)[0, :rows]


def solution(mesh):
    groups, members = mesh.devices.shape
    fine = Mesh(mesh.devices.reshape(groups, members // 2, 2), AXES)
    placed = (P(AXES, None), P(AXES), P(AXES))
    return jax.shard_map(local, mesh=fine, in_specs=placed, out_specs=P(AXES), check_vma=False)
```

```python
import functools

import jax
import jax.numpy as jnp
from jax import lax
from jax.experimental import pallas as pl
from jax.experimental.pallas import tpu as pltpu
from jax.sharding import Mesh, PartitionSpec as P

AXES = ("group", "z", "core")
LANES = 128
CHUNK = 512
TAIL = 16
VMEM = pl.BlockSpec(memory_space=pltpu.VMEM)


def flip(count, bits):
    return [(k, k ^ bits) for k in range(count)]


def unit_rows(values):
    values = values.astype(jnp.float32)
    total = jnp.sum(values * values, axis=1, keepdims=True) + values.shape[1] * 1e-06
    return (values * lax.rsqrt(total)).astype(jnp.bfloat16)


def ring_pairs(length, shift):
    if 2 * shift < length:
        return [(k, (k + shift) % length) for k in range(length)]
    pairs = [(k, k + shift) for k in range(length // 2)]
    return [pair[:: 1 - 2 * (pair[0] % 2)] for pair in pairs]


def swap(block):
    return lax.ppermute(block, "core", flip(2, 1))


def pack_into(block_ref, start, rows, ids):
    count, width = rows.shape
    place = pl.ds(start, count)
    block_ref[place, :width] = unit_rows(rows)
    meta = jnp.concatenate([ids.astype(jnp.float32), jnp.zeros((6, count), jnp.float32)], axis=0)
    if count < LANES:
        meta = jnp.concatenate([meta, jnp.zeros((8, LANES - count), jnp.float32)], axis=1)
    turned = meta.T[:count]
    cluster, order = turned[:, 0:1] + 1.0, turned[:, 1:2]
    high = jnp.floor(order / 256.0)
    lane = lax.broadcasted_iota(jnp.int32, (count, LANES), 1)
    tail = jnp.where(lane == 0, cluster, jnp.where(lane == 1, high, order - 256.0 * high))
    block_ref[place, width:] = jnp.where(lane < 3, tail, 0.0).astype(jnp.bfloat16)


def pack_kernel(rows_ref, ids_ref, block_ref):
    pack_into(block_ref, 0, rows_ref[...], ids_ref[...])


def pair_kernel(own_ref, own_ids_ref, rows_ref, ids_ref, both_ref, line_ref):
    count, width = rows_ref.shape
    both_ref[:count, :] = own_ref[...]
    pack_into(both_ref, count, rows_ref[...], ids_ref[...])
    for k in range(width // LANES):
        columns = both_ref[:, k * LANES : (k + 1) * LANES]
        line_ref[2 * count * k : 2 * count * (k + 1), :] = columns
    lines = []
    for ref in (own_ids_ref, ids_ref):
        ids = ref[...].astype(jnp.float32)
        high = jnp.floor(ids[1:2] / 256.0)
        lines += [ids[0:1] + 1.0, high, ids[1:2] - 256.0 * high]
    tail = jnp.concatenate(lines + [jnp.zeros((TAIL - 6, count), jnp.float32)], axis=0)
    if count < LANES:
        tail = jnp.concatenate([tail, jnp.zeros((TAIL, LANES - count), jnp.float32)], axis=1)
    line_ref[2 * count * (width // LANES) :, :] = tail.astype(jnp.bfloat16)


def pack(kernel, operands, shapes):
    rows, width = operands[-2].shape
    return pl.pallas_call(
        kernel,
        in_specs=[VMEM] * len(operands),
        out_specs=[VMEM] * len(shapes),
        out_shape=[jax.ShapeDtypeStruct(shape, jnp.bfloat16) for shape in shapes],
        compiler_params=pltpu.CompilerParams(vmem_limit_bytes=8 * 2**20),
        cost_estimate=pl.CostEstimate(
            flops=4 * rows * width, bytes_accessed=4 * rows * width, transcendentals=rows
        ),
    )(*operands)


def padded(rows):
    spare = -rows.shape[0] % LANES
    if not spare:
        return rows
    return jnp.concatenate([rows, jnp.zeros((spare, rows.shape[1]), rows.dtype)], axis=0)


def own_kernel(*refs):
    own_ref, row_ref, dots = refs[0], *refs[-2:]
    rows, width = own_ref.shape[0], own_ref.shape[1] - LANES
    turned = padded(own_ref[:, width:].astype(jnp.float32)).T
    meta = [(turned[0:1], turned[1:2] * 256.0 + turned[2:3])]

    def visitors_at(k):
        return padded(own_ref[:, k : k + CHUNK])

    bests, _ = best_of(visitors_at, meta, refs[1:-2], rows, False, dots)
    row_ref[...] = bests[0]


def visit_kernel(visitors, arrays, mine, others, *refs):
    line_refs, block_refs = refs[:visitors], refs[visitors : visitors + arrays]
    row_ref, mine_ref, other_ref, dots = refs[visitors + arrays + 1 :]
    width = block_refs[0].shape[1] - LANES
    rows = (line_refs[0].shape[0] - TAIL) // (2 * width // LANES)
    meta = []
    for ref in line_refs:
        tail = ref[2 * rows * (width // LANES) :, :].astype(jnp.float32)
        for row in (0, 3):
            order = tail[row + 1 : row + 2] * 256.0 + tail[row + 2 : row + 3]
            meta.append((tail[row : row + 1], order))

    def visitors_at(k):
        parts = []
        for ref in line_refs:
            for core in range(2):
                starts = [rows * (2 * block + core) for block in range(k // LANES, (k + CHUNK) // LANES)]
                columns = [ref[start : start + rows, :] for start in starts]
                parts.append(padded(jnp.concatenate(columns, axis=1)))
        return jnp.concatenate(parts, axis=0)

    bests, cols = best_of(visitors_at, meta, block_refs, rows, True, dots)
    for v, best in enumerate(bests):
        row_ref[v : v + 1, :] = best
    for ref, picked in ((mine_ref, mine), (other_ref, others)):
        for row, j in enumerate(picked):
            ref[row : row + 1, :] = cols[j]


def best_of(visitors_at, meta, block_refs, rows, homed, dots):
    width = block_refs[0].shape[1] - LANES
    for k in range(0, width, CHUNK):
        left = jnp.concatenate([ref[:, k : k + CHUNK] for ref in block_refs], axis=0)
        part = lax.dot_general(
            left,
            visitors_at(k),
            (((1,), (1,)), ((), ())),
            preferred_element_type=jnp.float32,
        )
        dots[...] = part if k == 0 else dots[...] + part

    tails = jnp.concatenate([ref[:, width:] for ref in block_refs], axis=0).astype(jnp.float32)
    row_best = [jnp.full((1, LANES), -1.0, jnp.float32) for _ in meta]
    lane = lax.broadcasted_iota(jnp.int32, (rows, LANES), 1)
    col_all = jnp.full((rows, LANES), -1.0, jnp.float32)
    for j in range(dots.shape[0] // rows):
        tail = tails[j * rows : (j + 1) * rows]
        block_cluster, block_order = tail[:, 0:1], tail[:, 1:2] * 256.0 + tail[:, 2:3]
        col_best = jnp.full((rows, 1), -1.0, jnp.float32)
        for v, (cluster, order) in enumerate(meta):
            cosine = dots[j * rows : (j + 1) * rows, v * LANES : (v + 1) * LANES]
            same = (block_cluster == cluster) & (cluster > 0)
            seen = jnp.where(same & (block_order < order), cosine, -1.0)
            row_best[v] = jnp.maximum(row_best[v], jnp.max(seen, axis=0, keepdims=True))
            if homed:
                seen = jnp.where(same & (order < block_order), cosine, -1.0)
                col_best = jnp.maximum(col_best, jnp.max(seen, axis=1, keepdims=True))
        col_all = jnp.where(lane == j, col_best, col_all)
    if not homed:
        return row_best, None
    if rows < LANES:
        fill = jnp.full((LANES - rows, LANES), -1.0, jnp.float32)
        col_all = jnp.concatenate([col_all, fill], axis=0)
    turned = col_all.T
    return row_best, [turned[j : j + 1] for j in range(dots.shape[0] // rows)]


def call(kernel, operands, count, out_rows, total, width):
    return pl.pallas_call(
        kernel,
        in_specs=[VMEM] * len(operands),
        out_specs=[VMEM] * len(out_rows),
        out_shape=[jax.ShapeDtypeStruct((n, LANES), jnp.float32) for n in out_rows],
        scratch_shapes=[pltpu.VMEM((total, count * LANES), jnp.float32)],
        compiler_params=pltpu.CompilerParams(vmem_limit_bytes=24 * 2**20),
        cost_estimate=pl.CostEstimate(
            flops=2 * total * count * LANES * width,
            bytes_accessed=2 * (total + count * LANES) * width,
            transcendentals=0,
        ),
    )(*operands)


def group_trip(groups, first, second):
    return [(2 * k + c, 2 * (k ^ s) + c) for k in range(groups) for c, s in enumerate((first, second))]


def local(embeddings, cluster_ids, order_index):
    rows, width = embeddings.shape
    groups, length = lax.axis_size("group"), lax.axis_size("z")
    z, core = lax.axis_index("z"), lax.axis_index("core")
    plane_axes, line_axes = ("group", "core"), ("z", "core")
    ids = jnp.stack([cluster_ids, order_index])
    (own,) = pack(pack_kernel, [embeddings, ids], [(rows, width + LANES)])
    shapes = [(2 * rows, width + LANES), (2 * rows * width // LANES + TAIL, LANES)]
    both, line = pack(pair_kernel, [own, ids, swap(embeddings), swap(ids)], shapes)

    routes = [ring_pairs(length, shift) for shift in range(1, length // 2 + 1)]
    trips = []
    for first in range(0, len(routes), 2):
        ways = enumerate(routes[first : first + 2][::-1])
        trips.append([(2 * a + way, 2 * b + way) for way, route in ways for a, b in route])
    visitors = [lax.ppermute(line, line_axes, trip) for trip in trips]

    partners = [(s, s + 1) for s in range(1, groups - 1, 2)]
    arrived = [lax.ppermute(both, plane_axes, group_trip(groups, *way)) for way in partners]
    last = groups - 1
    relay = group_trip(groups, last ^ partners[-1][0], last ^ partners[-1][1])
    half = rows // 2
    corner = [arrived[-1][first : first + half] for first in (0, half)]
    corner = [lax.ppermute(part, plane_axes, relay) for part in corner]
    sides = [(block, swap(block)) for block in arrived]
    chunks = [[both, *sides[-1], *corner, *(swap(part) for part in corner)]]
    chunks += [[*sides[k], *sides[k + 1]] for k in range(0, len(sides) - 1, 2)]

    orders = [((2, 5, 6, 0), (4, 3, 7, 1))] + [((0, 3, 4, 7), (2, 1, 6, 5))] * (len(chunks) - 1)
    bests, answers = [], []
    for chunk in chunks:
        bests += call(own_kernel, [own, *chunk], 1, [1], 8 * rows, width)
    for index, (chunk, order) in enumerate(zip(chunks, orders)):
        kernel = functools.partial(visit_kernel, len(visitors), len(chunk), *order)
        count = 2 * len(visitors)
        operands = [*visitors, *chunk, bests[index]]
        answers.append(call(kernel, operands, count, [count, 4, 4], 8 * rows, width))
    home = functools.reduce(jnp.maximum, [answer[0] for answer in answers])
    merged = [jnp.maximum(mine, swap(others)) for _, mine, others in answers]

    for index, trip in enumerate(trips):
        part = home[2 * index : 2 * index + 2] if len(trips) > 1 else home
        back = lax.ppermute(part, line_axes, [(b, a) for a, b in trip])
        for here, best in ((2 * z + core, back[0:1]), (2 * z + (core ^ 1), swap(back)[1:2])):
            sent = functools.reduce(jnp.logical_or, [here == a for a, _ in trip])
            bests.append(jnp.where(sent, best, -1.0))
    ways = [(0, 0, partners[-1])]
    ways += [(1 + k // 2, 2 * (k % 2), way) for k, way in enumerate(partners[:-1])]
    for chunk, row, (first, second) in ways:
        for offset, order in ((1, (second, first)), (0, (first, second))):
            got = lax.ppermute(merged[chunk], plane_axes, group_trip(groups, *order))
            bests.append(got[row + offset : row + offset + 1])
    bests.append(lax.ppermute(merged[0], "group", flip(groups, last))[2:3])
    bests.append(merged[0][3:4])
    return functools.reduce(jnp.maximum, bests)[0, :rows]


def solution(mesh):
    groups, members = mesh.devices.shape
    fine = Mesh(mesh.devices.reshape(groups, members // 2, 2), AXES)
    placed = (P(AXES, None), P(AXES), P(AXES))
    return jax.shard_map(local, mesh=fine, in_specs=placed, out_specs=P(AXES), check_vma=False)
```

```python
import functools

import jax
import jax.numpy as jnp
from jax import lax
from jax.experimental import pallas as pl
from jax.experimental.pallas import tpu as pltpu
from jax.sharding import Mesh, PartitionSpec as P

AXES = ("group", "z", "core")
LANES = 128
CHUNK = 1024
TAIL = 16
VMEM = pl.BlockSpec(memory_space=pltpu.VMEM)


def flip(count, bits):
    return [(k, k ^ bits) for k in range(count)]


def unit_rows(values):
    values = values.astype(jnp.float32)
    total = jnp.sum(values * values, axis=1, keepdims=True) + values.shape[1] * 1e-06
    return (values * lax.rsqrt(total)).astype(jnp.bfloat16)


def ring_pairs(length, shift):
    if 2 * shift < length:
        return [(k, (k + shift) % length) for k in range(length)]
    pairs = [(k, k + shift) for k in range(length // 2)]
    return [pair[:: 1 - 2 * (pair[0] % 2)] for pair in pairs]


def swap(block):
    return lax.ppermute(block, "core", flip(2, 1))


def pack_into(block_ref, start, rows, ids):
    count, width = rows.shape
    place = pl.ds(start, count)
    block_ref[place, :width] = unit_rows(rows)
    meta = jnp.concatenate([ids.astype(jnp.float32), jnp.zeros((6, count), jnp.float32)], axis=0)
    if count < LANES:
        meta = jnp.concatenate([meta, jnp.zeros((8, LANES - count), jnp.float32)], axis=1)
    turned = meta.T[:count]
    cluster, order = turned[:, 0:1] + 1.0, turned[:, 1:2]
    high = jnp.floor(order / 256.0)
    lane = lax.broadcasted_iota(jnp.int32, (count, LANES), 1)
    tail = jnp.where(lane == 0, cluster, jnp.where(lane == 1, high, order - 256.0 * high))
    block_ref[place, width:] = jnp.where(lane < 3, tail, 0.0).astype(jnp.bfloat16)


def pack_kernel(rows_ref, ids_ref, block_ref):
    pack_into(block_ref, 0, rows_ref[...], ids_ref[...])


def pair_kernel(own_ref, own_ids_ref, rows_ref, ids_ref, both_ref, line_ref):
    count, width = rows_ref.shape
    both_ref[:count, :] = own_ref[...]
    pack_into(both_ref, count, rows_ref[...], ids_ref[...])
    for k in range(width // LANES):
        columns, start = pl.ds(k * LANES, LANES), 2 * count * k
        line_ref[start : start + count, :] = own_ref[:, columns]
        line_ref[start + count : start + 2 * count, :] = both_ref[count:, columns]
    lines = []
    for ref in (own_ids_ref, ids_ref):
        ids = ref[...].astype(jnp.float32)
        high = jnp.floor(ids[1:2] / 256.0)
        lines += [ids[0:1] + 1.0, high, ids[1:2] - 256.0 * high]
    tail = jnp.concatenate(lines + [jnp.zeros((TAIL - 6, count), jnp.float32)], axis=0)
    if count < LANES:
        tail = jnp.concatenate([tail, jnp.zeros((TAIL, LANES - count), jnp.float32)], axis=1)
    line_ref[2 * count * (width // LANES) :, :] = tail.astype(jnp.bfloat16)


def pack(kernel, operands, shapes):
    rows, width = operands[-2].shape
    return pl.pallas_call(
        kernel,
        in_specs=[VMEM] * len(operands),
        out_specs=[VMEM] * len(shapes),
        out_shape=[jax.ShapeDtypeStruct(shape, jnp.bfloat16) for shape in shapes],
        compiler_params=pltpu.CompilerParams(vmem_limit_bytes=8 * 2**20),
        cost_estimate=pl.CostEstimate(
            flops=4 * rows * width, bytes_accessed=4 * rows * width, transcendentals=rows
        ),
    )(*operands)


def padded(rows):
    spare = -rows.shape[0] % LANES
    if not spare:
        return rows
    return jnp.concatenate([rows, jnp.zeros((spare, rows.shape[1]), rows.dtype)], axis=0)


def own_kernel(*refs):
    own_ref, row_ref, dots = refs[0], *refs[-2:]
    rows, width = own_ref.shape[0], own_ref.shape[1] - LANES
    turned = padded(own_ref[:, width:].astype(jnp.float32)).T
    meta = [(turned[0:1], turned[1:2] * 256.0 + turned[2:3])]

    def visitors_at(k):
        return padded(own_ref[:, k : k + CHUNK])

    bests, _ = best_of(visitors_at, meta, refs[1:-2], rows, False, dots)
    row_ref[...] = bests[0]


def visit_kernel(visitors, arrays, mine, others, *refs):
    line_refs, block_refs = refs[:visitors], refs[visitors : visitors + arrays]
    row_ref, mine_ref, other_ref, dots = refs[visitors + arrays + 1 :]
    width = block_refs[0].shape[1] - LANES
    rows = (line_refs[0].shape[0] - TAIL) // (2 * width // LANES)
    meta = []
    for ref in line_refs:
        tail = ref[2 * rows * (width // LANES) :, :].astype(jnp.float32)
        for row in (0, 3):
            order = tail[row + 1 : row + 2] * 256.0 + tail[row + 2 : row + 3]
            meta.append((tail[row : row + 1], order))

    def visitors_at(k):
        parts = []
        for ref in line_refs:
            for core in range(2):
                starts = [rows * (2 * block + core) for block in range(k // LANES, (k + CHUNK) // LANES)]
                columns = [ref[start : start + rows, :] for start in starts]
                parts.append(padded(jnp.concatenate(columns, axis=1)))
        return jnp.concatenate(parts, axis=0)

    bests, cols = best_of(visitors_at, meta, block_refs, rows, True, dots)
    for v, best in enumerate(bests):
        row_ref[v : v + 1, :] = best
    for ref, picked in ((mine_ref, mine), (other_ref, others)):
        for row, j in enumerate(picked):
            ref[row : row + 1, :] = cols[j]


def best_of(visitors_at, meta, block_refs, rows, homed, dots):
    width = block_refs[0].shape[1] - LANES
    for k in range(0, width, CHUNK):
        left = jnp.concatenate([ref[:, k : k + CHUNK] for ref in block_refs], axis=0)
        part = lax.dot_general(
            left,
            visitors_at(k),
            (((1,), (1,)), ((), ())),
            preferred_element_type=jnp.float32,
        )
        dots[...] = part if k == 0 else dots[...] + part

    tails = jnp.concatenate([ref[:, width:] for ref in block_refs], axis=0).astype(jnp.float32)
    row_best = [jnp.full((1, LANES), -1.0, jnp.float32) for _ in meta]
    lane = lax.broadcasted_iota(jnp.int32, (rows, LANES), 1)
    col_all = jnp.full((rows, LANES), -1.0, jnp.float32)
    for j in range(dots.shape[0] // rows):
        tail = tails[j * rows : (j + 1) * rows]
        block_cluster, block_order = tail[:, 0:1], tail[:, 1:2] * 256.0 + tail[:, 2:3]
        col_best = jnp.full((rows, 1), -1.0, jnp.float32)
        for v, (cluster, order) in enumerate(meta):
            cosine = dots[j * rows : (j + 1) * rows, v * LANES : (v + 1) * LANES]
            same = (block_cluster == cluster) & (cluster > 0)
            seen = jnp.where(same & (block_order < order), cosine, -1.0)
            row_best[v] = jnp.maximum(row_best[v], jnp.max(seen, axis=0, keepdims=True))
            if homed:
                seen = jnp.where(same & (order < block_order), cosine, -1.0)
                col_best = jnp.maximum(col_best, jnp.max(seen, axis=1, keepdims=True))
        col_all = jnp.where(lane == j, col_best, col_all)
    if not homed:
        return row_best, None
    if rows < LANES:
        fill = jnp.full((LANES - rows, LANES), -1.0, jnp.float32)
        col_all = jnp.concatenate([col_all, fill], axis=0)
    turned = col_all.T
    return row_best, [turned[j : j + 1] for j in range(dots.shape[0] // rows)]


def call(kernel, operands, count, out_rows, total, width):
    return pl.pallas_call(
        kernel,
        in_specs=[VMEM] * len(operands),
        out_specs=[VMEM] * len(out_rows),
        out_shape=[jax.ShapeDtypeStruct((n, LANES), jnp.float32) for n in out_rows],
        scratch_shapes=[pltpu.VMEM((total, count * LANES), jnp.float32)],
        compiler_params=pltpu.CompilerParams(vmem_limit_bytes=24 * 2**20),
        cost_estimate=pl.CostEstimate(
            flops=2 * total * count * LANES * width,
            bytes_accessed=2 * (total + count * LANES) * width,
            transcendentals=0,
        ),
    )(*operands)


def group_trip(groups, first, second):
    return [(2 * k + c, 2 * (k ^ s) + c) for k in range(groups) for c, s in enumerate((first, second))]


def local(embeddings, cluster_ids, order_index):
    rows, width = embeddings.shape
    groups, length = lax.axis_size("group"), lax.axis_size("z")
    z, core = lax.axis_index("z"), lax.axis_index("core")
    plane_axes, line_axes = ("group", "core"), ("z", "core")
    ids = jnp.stack([cluster_ids, order_index])
    (own,) = pack(pack_kernel, [embeddings, ids], [(rows, width + LANES)])
    shapes = [(2 * rows, width + LANES), (2 * rows * width // LANES + TAIL, LANES)]
    both, line = pack(pair_kernel, [own, ids, swap(embeddings), swap(ids)], shapes)

    routes = [ring_pairs(length, shift) for shift in range(1, length // 2 + 1)]
    trips = []
    for first in range(0, len(routes), 2):
        ways = enumerate(routes[first : first + 2][::-1])
        trips.append([(2 * a + way, 2 * b + way) for way, route in ways for a, b in route])
    visitors = [lax.ppermute(line, line_axes, trip) for trip in trips]

    partners = [(s, s + 1) for s in range(1, groups - 1, 2)]
    arrived = [lax.ppermute(both, plane_axes, group_trip(groups, *way)) for way in partners]
    last = groups - 1
    relay = group_trip(groups, last ^ partners[-1][0], last ^ partners[-1][1])
    half = rows // 2
    corner = [arrived[-1][first : first + half] for first in (0, half)]
    corner = [lax.ppermute(part, plane_axes, relay) for part in corner]
    sides = [(block, swap(block)) for block in arrived]
    chunks = [[both, *sides[-1], *corner, *(swap(part) for part in corner)]]
    chunks += [[*sides[k], *sides[k + 1]] for k in range(0, len(sides) - 1, 2)]

    orders = [((2, 5, 6, 0), (4, 3, 7, 1))] + [((0, 3, 4, 7), (2, 1, 6, 5))] * (len(chunks) - 1)
    bests, answers = [], []
    for chunk in chunks:
        bests += call(own_kernel, [own, *chunk], 1, [1], 8 * rows, width)
    for index, (chunk, order) in enumerate(zip(chunks, orders)):
        kernel = functools.partial(visit_kernel, len(visitors), len(chunk), *order)
        count = 2 * len(visitors)
        operands = [*visitors, *chunk, bests[index]]
        answers.append(call(kernel, operands, count, [count, 4, 4], 8 * rows, width))
    home = functools.reduce(jnp.maximum, [answer[0] for answer in answers])
    merged = [jnp.maximum(mine, swap(others)) for _, mine, others in answers]

    for index, trip in enumerate(trips):
        part = home[2 * index : 2 * index + 2] if len(trips) > 1 else home
        back = lax.ppermute(part, line_axes, [(b, a) for a, b in trip])
        for here, best in ((2 * z + core, back[0:1]), (2 * z + (core ^ 1), swap(back)[1:2])):
            sent = functools.reduce(jnp.logical_or, [here == a for a, _ in trip])
            bests.append(jnp.where(sent, best, -1.0))
    ways = [(0, 0, partners[-1])]
    ways += [(1 + k // 2, 2 * (k % 2), way) for k, way in enumerate(partners[:-1])]
    for chunk, row, (first, second) in ways:
        for offset, order in ((1, (second, first)), (0, (first, second))):
            got = lax.ppermute(merged[chunk], plane_axes, group_trip(groups, *order))
            bests.append(got[row + offset : row + offset + 1])
    bests.append(lax.ppermute(merged[0], "group", flip(groups, last))[2:3])
    bests.append(merged[0][3:4])
    return functools.reduce(jnp.maximum, bests)[0, :rows]


def solution(mesh):
    groups, members = mesh.devices.shape
    fine = Mesh(mesh.devices.reshape(groups, members // 2, 2), AXES)
    placed = (P(AXES, None), P(AXES), P(AXES))
    return jax.shard_map(local, mesh=fine, in_specs=placed, out_specs=P(AXES), check_vma=False)
```

```python
import functools

import jax
import jax.numpy as jnp
from jax import lax
from jax.experimental import pallas as pl
from jax.experimental.pallas import tpu as pltpu
from jax.sharding import Mesh, PartitionSpec as P

AXES = ("group", "z", "core")
LANES = 128
CHUNK = 512
TAIL = 16
VMEM = pl.BlockSpec(memory_space=pltpu.VMEM)


def flip(count, bits):
    return [(k, k ^ bits) for k in range(count)]


def unit_rows(values):
    values = values.astype(jnp.float32)
    total = jnp.sum(values * values, axis=1, keepdims=True) + values.shape[1] * 1e-06
    return (values * lax.rsqrt(total)).astype(jnp.bfloat16)


def swap(block):
    return lax.ppermute(block, "core", flip(2, 1))


def line_trips(length):
    if length == 4:
        ways = [[(0, 1), (1, 2), (2, 3)], [(2, 0), (3, 1), (0, 3)]]
    else:
        ways = [[(k, (k + shift) % length) for k in range(length)] for shift in range(1, (length + 1) // 2)]
        if length % 2 == 0:
            pairs = [(k, k + length // 2) for k in range(length // 2)]
            ways.append([pair[:: 1 - 2 * (pair[0] % 2)] for pair in pairs])
    return [
        [(2 * a + core, 2 * b + core) for core, way in enumerate(ways[first : first + 2]) for a, b in way]
        for first in range(0, len(ways), 2)
    ]


def pack_into(block_ref, start, rows, ids):
    count, width = rows.shape
    place = pl.ds(start, count)
    block_ref[place, :width] = unit_rows(rows)
    meta = jnp.concatenate([ids.astype(jnp.float32), jnp.zeros((6, count), jnp.float32)], axis=0)
    if count < LANES:
        meta = jnp.concatenate([meta, jnp.zeros((8, LANES - count), jnp.float32)], axis=1)
    turned = meta.T[:count]
    cluster, order = turned[:, 0:1] + 1.0, turned[:, 1:2]
    high = jnp.floor(order / 256.0)
    lane = lax.broadcasted_iota(jnp.int32, (count, LANES), 1)
    tail = jnp.where(lane == 0, cluster, jnp.where(lane == 1, high, order - 256.0 * high))
    block_ref[place, width:] = jnp.where(lane < 3, tail, 0.0).astype(jnp.bfloat16)


def pack_kernel(rows_ref, ids_ref, block_ref):
    pack_into(block_ref, 0, rows_ref[...], ids_ref[...])


def pair_kernel(own_ref, own_ids_ref, rows_ref, ids_ref, both_ref, line_ref):
    count, width = rows_ref.shape
    both_ref[:count, :] = own_ref[...]
    pack_into(both_ref, count, rows_ref[...], ids_ref[...])
    for k in range(width // LANES):
        columns = both_ref[:, k * LANES : (k + 1) * LANES]
        line_ref[2 * count * k : 2 * count * (k + 1), :] = columns
    lines = []
    for ref in (own_ids_ref, ids_ref):
        ids = ref[...].astype(jnp.float32)
        high = jnp.floor(ids[1:2] / 256.0)
        lines += [ids[0:1] + 1.0, high, ids[1:2] - 256.0 * high]
    tail = jnp.concatenate(lines + [jnp.zeros((TAIL - 6, count), jnp.float32)], axis=0)
    if count < LANES:
        tail = jnp.concatenate([tail, jnp.zeros((TAIL, LANES - count), jnp.float32)], axis=1)
    line_ref[2 * count * (width // LANES) :, :] = tail.astype(jnp.bfloat16)


def pack(kernel, operands, shapes):
    rows, width = operands[-2].shape
    return pl.pallas_call(
        kernel,
        in_specs=[VMEM] * len(operands),
        out_specs=[VMEM] * len(shapes),
        out_shape=[jax.ShapeDtypeStruct(shape, jnp.bfloat16) for shape in shapes],
        compiler_params=pltpu.CompilerParams(vmem_limit_bytes=8 * 2**20),
        cost_estimate=pl.CostEstimate(
            flops=4 * rows * width, bytes_accessed=4 * rows * width, transcendentals=rows
        ),
    )(*operands)


def padded(rows):
    spare = -rows.shape[0] % LANES
    if not spare:
        return rows
    return jnp.concatenate([rows, jnp.zeros((spare, rows.shape[1]), rows.dtype)], axis=0)


def own_kernel(*refs):
    own_ref, row_ref, dots = refs[0], *refs[-2:]
    rows, width = own_ref.shape[0], own_ref.shape[1] - LANES
    turned = padded(own_ref[:, width:].astype(jnp.float32)).T
    meta = [(turned[0:1], turned[1:2] * 256.0 + turned[2:3])]

    def visitors_at(k):
        return padded(own_ref[:, k : k + CHUNK])

    bests, _ = best_of(visitors_at, meta, refs[1:-2], rows, False, dots)
    row_ref[...] = bests[0]


def visit_kernel(visitors, arrays, mine, others, *refs):
    line_refs, block_refs = refs[:visitors], refs[visitors : visitors + arrays]
    row_ref, mine_ref, other_ref, dots = refs[visitors + arrays + 1 :]
    width = block_refs[0].shape[1] - LANES
    rows = (line_refs[0].shape[0] - TAIL) // (2 * width // LANES)
    meta = []
    for ref in line_refs:
        tail = ref[2 * rows * (width // LANES) :, :].astype(jnp.float32)
        for row in (0, 3):
            order = tail[row + 1 : row + 2] * 256.0 + tail[row + 2 : row + 3]
            meta.append((tail[row : row + 1], order))

    def visitors_at(k):
        parts = []
        for ref in line_refs:
            for core in range(2):
                starts = [rows * (2 * block + core) for block in range(k // LANES, (k + CHUNK) // LANES)]
                columns = [ref[start : start + rows, :] for start in starts]
                parts.append(padded(jnp.concatenate(columns, axis=1)))
        return jnp.concatenate(parts, axis=0)

    bests, cols = best_of(visitors_at, meta, block_refs, rows, True, dots)
    for v, best in enumerate(bests):
        row_ref[v : v + 1, :] = best
    for ref, picked in ((mine_ref, mine), (other_ref, others)):
        for row, j in enumerate(picked):
            ref[row : row + 1, :] = cols[j]


def best_of(visitors_at, meta, block_refs, rows, homed, dots):
    width = block_refs[0].shape[1] - LANES
    for k in range(0, width, CHUNK):
        left = jnp.concatenate([ref[:, k : k + CHUNK] for ref in block_refs], axis=0)
        part = lax.dot_general(
            left,
            visitors_at(k),
            (((1,), (1,)), ((), ())),
            preferred_element_type=jnp.float32,
        )
        dots[...] = part if k == 0 else dots[...] + part

    tails = jnp.concatenate([ref[:, width:] for ref in block_refs], axis=0).astype(jnp.float32)
    row_best = [jnp.full((1, LANES), -1.0, jnp.float32) for _ in meta]
    lane = lax.broadcasted_iota(jnp.int32, (rows, LANES), 1)
    col_all = jnp.full((rows, LANES), -1.0, jnp.float32)
    for j in range(dots.shape[0] // rows):
        tail = tails[j * rows : (j + 1) * rows]
        block_cluster, block_order = tail[:, 0:1], tail[:, 1:2] * 256.0 + tail[:, 2:3]
        col_best = jnp.full((rows, 1), -1.0, jnp.float32)
        for v, (cluster, order) in enumerate(meta):
            cosine = dots[j * rows : (j + 1) * rows, v * LANES : (v + 1) * LANES]
            same = (block_cluster == cluster) & (cluster > 0)
            seen = jnp.where(same & (block_order < order), cosine, -1.0)
            row_best[v] = jnp.maximum(row_best[v], jnp.max(seen, axis=0, keepdims=True))
            if homed:
                seen = jnp.where(same & (order < block_order), cosine, -1.0)
                col_best = jnp.maximum(col_best, jnp.max(seen, axis=1, keepdims=True))
        col_all = jnp.where(lane == j, col_best, col_all)
    if not homed:
        return row_best, None
    if rows < LANES:
        fill = jnp.full((LANES - rows, LANES), -1.0, jnp.float32)
        col_all = jnp.concatenate([col_all, fill], axis=0)
    turned = col_all.T
    return row_best, [turned[j : j + 1] for j in range(dots.shape[0] // rows)]


def call(kernel, operands, count, out_rows, total, width):
    return pl.pallas_call(
        kernel,
        in_specs=[VMEM] * len(operands),
        out_specs=[VMEM] * len(out_rows),
        out_shape=[jax.ShapeDtypeStruct((n, LANES), jnp.float32) for n in out_rows],
        scratch_shapes=[pltpu.VMEM((total, count * LANES), jnp.float32)],
        compiler_params=pltpu.CompilerParams(vmem_limit_bytes=24 * 2**20),
        cost_estimate=pl.CostEstimate(
            flops=2 * total * count * LANES * width,
            bytes_accessed=2 * (total + count * LANES) * width,
            transcendentals=0,
        ),
    )(*operands)


def group_trip(groups, first, second):
    return [(2 * k + c, 2 * (k ^ s) + c) for k in range(groups) for c, s in enumerate((first, second))]


def local(embeddings, cluster_ids, order_index):
    rows, width = embeddings.shape
    groups, length = lax.axis_size("group"), lax.axis_size("z")
    z, core = lax.axis_index("z"), lax.axis_index("core")
    plane_axes, line_axes = ("group", "core"), ("z", "core")
    ids = jnp.stack([cluster_ids, order_index])
    (own,) = pack(pack_kernel, [embeddings, ids], [(rows, width + LANES)])
    shapes = [(2 * rows, width + LANES), (2 * rows * width // LANES + TAIL, LANES)]
    both, line = pack(pair_kernel, [own, ids, swap(embeddings), swap(ids)], shapes)

    trips = line_trips(length)
    visitors = [lax.ppermute(line, line_axes, trip) for trip in trips]

    partners = [(s, s + 1) for s in range(1, groups - 1, 2)]
    arrived = [lax.ppermute(both, plane_axes, group_trip(groups, *way)) for way in partners]
    last = groups - 1
    relay = group_trip(groups, last ^ partners[-1][0], last ^ partners[-1][1])
    half = rows // 2
    corner = [arrived[-1][first : first + half] for first in (0, half)]
    corner = [lax.ppermute(part, plane_axes, relay) for part in corner]
    sides = [(block, swap(block)) for block in arrived]
    chunks = [[both, *sides[-1], *corner, *(swap(part) for part in corner)]]
    chunks += [[*sides[k], *sides[k + 1]] for k in range(0, len(sides) - 1, 2)]

    orders = [((2, 5, 6, 0), (4, 3, 7, 1))] + [((0, 3, 4, 7), (2, 1, 6, 5))] * (len(chunks) - 1)
    bests, answers = [], []
    for chunk in chunks:
        bests += call(own_kernel, [own, *chunk], 1, [1], 8 * rows, width)
    for index, (chunk, order) in enumerate(zip(chunks, orders)):
        kernel = functools.partial(visit_kernel, len(visitors), len(chunk), *order)
        count = 2 * len(visitors)
        operands = [*visitors, *chunk, bests[index]]
        answers.append(call(kernel, operands, count, [count, 4, 4], 8 * rows, width))
    home = functools.reduce(jnp.maximum, [answer[0] for answer in answers])
    merged = [jnp.maximum(mine, swap(others)) for _, mine, others in answers]

    for index, trip in enumerate(trips):
        part = home[2 * index : 2 * index + 2] if len(trips) > 1 else home
        back = lax.ppermute(part, line_axes, [(b, a) for a, b in trip])
        for here, best in ((2 * z + core, back[0:1]), (2 * z + (core ^ 1), swap(back)[1:2])):
            sent = functools.reduce(jnp.logical_or, [here == a for a, _ in trip])
            bests.append(jnp.where(sent, best, -1.0))
    ways = [(0, 0, partners[-1])]
    ways += [(1 + k // 2, 2 * (k % 2), way) for k, way in enumerate(partners[:-1])]
    for chunk, row, (first, second) in ways:
        for offset, order in ((1, (second, first)), (0, (first, second))):
            got = lax.ppermute(merged[chunk], plane_axes, group_trip(groups, *order))
            bests.append(got[row + offset : row + offset + 1])
    bests.append(lax.ppermute(merged[0], "group", flip(groups, last))[2:3])
    bests.append(merged[0][3:4])
    return functools.reduce(jnp.maximum, bests)[0, :rows]


def solution(mesh):
    groups, members = mesh.devices.shape
    fine = Mesh(mesh.devices.reshape(groups, members // 2, 2), AXES)
    placed = (P(AXES, None), P(AXES), P(AXES))
    return jax.shard_map(local, mesh=fine, in_specs=placed, out_specs=P(AXES), check_vma=False)
```

```python
import functools

import jax
import jax.numpy as jnp
from jax import lax
from jax.experimental import pallas as pl
from jax.experimental.pallas import tpu as pltpu
from jax.sharding import Mesh, PartitionSpec as P

AXES = ("group", "z", "core")
LANES = 128
CHUNK = 512
TAIL = 16
VMEM = pl.BlockSpec(memory_space=pltpu.VMEM)


def flip(count, bits):
    return [(k, k ^ bits) for k in range(count)]


def unit_rows(values):
    values = values.astype(jnp.float32)
    total = jnp.sum(values * values, axis=1, keepdims=True) + values.shape[1] * 1e-06
    return (values * lax.rsqrt(total)).astype(jnp.bfloat16)


def ring_pairs(length, shift):
    if 2 * shift < length:
        return [((k + shift) % length, k) for k in range(length)]
    pairs = [(k, k + shift) for k in range(length // 2)]
    return [pair[:: 1 - 2 * (pair[0] % 2)] for pair in pairs]


def swap(block):
    return lax.ppermute(block, "core", flip(2, 1))


def pack_into(block_ref, start, rows, ids):
    count, width = rows.shape
    place = pl.ds(start, count)
    block_ref[place, :width] = unit_rows(rows)
    meta = jnp.concatenate([ids.astype(jnp.float32), jnp.zeros((6, count), jnp.float32)], axis=0)
    if count < LANES:
        meta = jnp.concatenate([meta, jnp.zeros((8, LANES - count), jnp.float32)], axis=1)
    turned = meta.T[:count]
    cluster, order = turned[:, 0:1] + 1.0, turned[:, 1:2]
    high = jnp.floor(order / 256.0)
    lane = lax.broadcasted_iota(jnp.int32, (count, LANES), 1)
    tail = jnp.where(lane == 0, cluster, jnp.where(lane == 1, high, order - 256.0 * high))
    block_ref[place, width:] = jnp.where(lane < 3, tail, 0.0).astype(jnp.bfloat16)


def pack_kernel(rows_ref, ids_ref, block_ref):
    pack_into(block_ref, 0, rows_ref[...], ids_ref[...])


def pair_kernel(own_ref, own_ids_ref, rows_ref, ids_ref, both_ref, line_ref):
    count, width = rows_ref.shape
    both_ref[:count, :] = own_ref[...]
    pack_into(both_ref, count, rows_ref[...], ids_ref[...])
    for k in range(width // LANES):
        columns = both_ref[:, k * LANES : (k + 1) * LANES]
        line_ref[2 * count * k : 2 * count * (k + 1), :] = columns
    lines = []
    for ref in (own_ids_ref, ids_ref):
        ids = ref[...].astype(jnp.float32)
        high = jnp.floor(ids[1:2] / 256.0)
        lines += [ids[0:1] + 1.0, high, ids[1:2] - 256.0 * high]
    tail = jnp.concatenate(lines + [jnp.zeros((TAIL - 6, count), jnp.float32)], axis=0)
    if count < LANES:
        tail = jnp.concatenate([tail, jnp.zeros((TAIL, LANES - count), jnp.float32)], axis=1)
    line_ref[2 * count * (width // LANES) :, :] = tail.astype(jnp.bfloat16)


def pack(kernel, operands, shapes):
    rows, width = operands[-2].shape
    return pl.pallas_call(
        kernel,
        in_specs=[VMEM] * len(operands),
        out_specs=[VMEM] * len(shapes),
        out_shape=[jax.ShapeDtypeStruct(shape, jnp.bfloat16) for shape in shapes],
        compiler_params=pltpu.CompilerParams(vmem_limit_bytes=8 * 2**20),
        cost_estimate=pl.CostEstimate(
            flops=4 * rows * width, bytes_accessed=4 * rows * width, transcendentals=rows
        ),
    )(*operands)


def padded(rows):
    spare = -rows.shape[0] % LANES
    if not spare:
        return rows
    return jnp.concatenate([rows, jnp.zeros((spare, rows.shape[1]), rows.dtype)], axis=0)


def own_kernel(*refs):
    own_ref, row_ref, dots = refs[0], *refs[-2:]
    rows, width = own_ref.shape[0], own_ref.shape[1] - LANES
    turned = padded(own_ref[:, width:].astype(jnp.float32)).T
    meta = [(turned[0:1], turned[1:2] * 256.0 + turned[2:3])]

    def visitors_at(k):
        return padded(own_ref[:, k : k + CHUNK])

    bests, _ = best_of(visitors_at, meta, refs[1:-2], rows, False, dots)
    row_ref[...] = bests[0]


def visit_kernel(visitors, arrays, mine, others, *refs):
    line_refs, block_refs = refs[:visitors], refs[visitors : visitors + arrays]
    row_ref, mine_ref, other_ref, dots = refs[visitors + arrays + 1 :]
    width = block_refs[0].shape[1] - LANES
    rows = (line_refs[0].shape[0] - TAIL) // (2 * width // LANES)
    meta = []
    for ref in line_refs:
        tail = ref[2 * rows * (width // LANES) :, :].astype(jnp.float32)
        for row in (0, 3):
            order = tail[row + 1 : row + 2] * 256.0 + tail[row + 2 : row + 3]
            meta.append((tail[row : row + 1], order))

    def visitors_at(k):
        parts = []
        for ref in line_refs:
            for core in range(2):
                starts = [rows * (2 * block + core) for block in range(k // LANES, (k + CHUNK) // LANES)]
                columns = [ref[start : start + rows, :] for start in starts]
                parts.append(padded(jnp.concatenate(columns, axis=1)))
        return jnp.concatenate(parts, axis=0)

    bests, cols = best_of(visitors_at, meta, block_refs, rows, True, dots)
    for v, best in enumerate(bests):
        row_ref[v : v + 1, :] = best
    for ref, picked in ((mine_ref, mine), (other_ref, others)):
        for row, j in enumerate(picked):
            ref[row : row + 1, :] = cols[j]


def best_of(visitors_at, meta, block_refs, rows, homed, dots):
    width = block_refs[0].shape[1] - LANES
    for k in range(0, width, CHUNK):
        left = jnp.concatenate([ref[:, k : k + CHUNK] for ref in block_refs], axis=0)
        part = lax.dot_general(
            left,
            visitors_at(k),
            (((1,), (1,)), ((), ())),
            preferred_element_type=jnp.float32,
        )
        dots[...] = part if k == 0 else dots[...] + part

    tails = jnp.concatenate([ref[:, width:] for ref in block_refs], axis=0).astype(jnp.float32)
    row_best = [jnp.full((1, LANES), -1.0, jnp.float32) for _ in meta]
    lane = lax.broadcasted_iota(jnp.int32, (rows, LANES), 1)
    col_all = jnp.full((rows, LANES), -1.0, jnp.float32)
    for j in range(dots.shape[0] // rows):
        tail = tails[j * rows : (j + 1) * rows]
        block_cluster, block_order = tail[:, 0:1], tail[:, 1:2] * 256.0 + tail[:, 2:3]
        col_best = jnp.full((rows, 1), -1.0, jnp.float32)
        for v, (cluster, order) in enumerate(meta):
            cosine = dots[j * rows : (j + 1) * rows, v * LANES : (v + 1) * LANES]
            same = (block_cluster == cluster) & (cluster > 0)
            seen = jnp.where(same & (block_order < order), cosine, -1.0)
            row_best[v] = jnp.maximum(row_best[v], jnp.max(seen, axis=0, keepdims=True))
            if homed:
                seen = jnp.where(same & (order < block_order), cosine, -1.0)
                col_best = jnp.maximum(col_best, jnp.max(seen, axis=1, keepdims=True))
        col_all = jnp.where(lane == j, col_best, col_all)
    if not homed:
        return row_best, None
    if rows < LANES:
        fill = jnp.full((LANES - rows, LANES), -1.0, jnp.float32)
        col_all = jnp.concatenate([col_all, fill], axis=0)
    turned = col_all.T
    return row_best, [turned[j : j + 1] for j in range(dots.shape[0] // rows)]


def call(kernel, operands, count, out_rows, total, width):
    return pl.pallas_call(
        kernel,
        in_specs=[VMEM] * len(operands),
        out_specs=[VMEM] * len(out_rows),
        out_shape=[jax.ShapeDtypeStruct((n, LANES), jnp.float32) for n in out_rows],
        scratch_shapes=[pltpu.VMEM((total, count * LANES), jnp.float32)],
        compiler_params=pltpu.CompilerParams(vmem_limit_bytes=24 * 2**20),
        cost_estimate=pl.CostEstimate(
            flops=2 * total * count * LANES * width,
            bytes_accessed=2 * (total + count * LANES) * width,
            transcendentals=0,
        ),
    )(*operands)


def group_trip(groups, first, second):
    return [(2 * k + c, 2 * (k ^ s) + c) for k in range(groups) for c, s in enumerate((first, second))]


def local(embeddings, cluster_ids, order_index):
    rows, width = embeddings.shape
    groups, length = lax.axis_size("group"), lax.axis_size("z")
    z, core = lax.axis_index("z"), lax.axis_index("core")
    plane_axes, line_axes = ("group", "core"), ("z", "core")
    ids = jnp.stack([cluster_ids, order_index])
    (own,) = pack(pack_kernel, [embeddings, ids], [(rows, width + LANES)])
    shapes = [(2 * rows, width + LANES), (2 * rows * width // LANES + TAIL, LANES)]
    both, line = pack(pair_kernel, [own, ids, swap(embeddings), swap(ids)], shapes)

    routes = [ring_pairs(length, shift) for shift in range(1, length // 2 + 1)]
    trips = []
    for first in range(0, len(routes), 2):
        ways = enumerate(routes[first : first + 2][::-1])
        trips.append([(2 * a + way, 2 * b + way) for way, route in ways for a, b in route])
    visitors = [lax.ppermute(line, line_axes, trip) for trip in trips]

    partners = [(s, s + 1) for s in range(1, groups - 1, 2)]
    arrived = [lax.ppermute(both, plane_axes, group_trip(groups, *way)) for way in partners]
    last = groups - 1
    relay = group_trip(groups, last ^ partners[-1][0], last ^ partners[-1][1])
    half = rows // 2
    corner = [arrived[-1][first : first + half] for first in (0, half)]
    corner = [lax.ppermute(part, plane_axes, relay) for part in corner]
    sides = [(block, swap(block)) for block in arrived]
    chunks = [[both, *sides[-1], *corner, *(swap(part) for part in corner)]]
    chunks += [[*sides[k], *sides[k + 1]] for k in range(0, len(sides) - 1, 2)]

    orders = [((2, 5, 6, 0), (4, 3, 7, 1))] + [((0, 3, 4, 7), (2, 1, 6, 5))] * (len(chunks) - 1)
    bests, answers = [], []
    for chunk in chunks:
        bests += call(own_kernel, [own, *chunk], 1, [1], 8 * rows, width)
    for index, (chunk, order) in enumerate(zip(chunks, orders)):
        kernel = functools.partial(visit_kernel, len(visitors), len(chunk), *order)
        count = 2 * len(visitors)
        operands = [*visitors, *chunk, bests[index]]
        answers.append(call(kernel, operands, count, [count, 4, 4], 8 * rows, width))
    home = functools.reduce(jnp.maximum, [answer[0] for answer in answers])
    merged = [jnp.maximum(mine, swap(others)) for _, mine, others in answers]

    for index, trip in enumerate(trips):
        part = home[2 * index : 2 * index + 2] if len(trips) > 1 else home
        back = lax.ppermute(part, line_axes, [(b, a) for a, b in trip])
        for here, best in ((2 * z + core, back[0:1]), (2 * z + (core ^ 1), swap(back)[1:2])):
            sent = functools.reduce(jnp.logical_or, [here == a for a, _ in trip])
            bests.append(jnp.where(sent, best, -1.0))
    ways = [(0, 0, partners[-1])]
    ways += [(1 + k // 2, 2 * (k % 2), way) for k, way in enumerate(partners[:-1])]
    for chunk, row, (first, second) in ways:
        for offset, order in ((1, (second, first)), (0, (first, second))):
            got = lax.ppermute(merged[chunk], plane_axes, group_trip(groups, *order))
            bests.append(got[row + offset : row + offset + 1])
    bests.append(lax.ppermute(merged[0], "group", flip(groups, last))[2:3])
    bests.append(merged[0][3:4])
    return functools.reduce(jnp.maximum, bests)[0, :rows]


def solution(mesh):
    groups, members = mesh.devices.shape
    fine = Mesh(mesh.devices.reshape(groups, members // 2, 2), AXES)
    placed = (P(AXES, None), P(AXES), P(AXES))
    return jax.shard_map(local, mesh=fine, in_specs=placed, out_specs=P(AXES), check_vma=False)
```

```python
import functools

import jax
import jax.numpy as jnp
from jax import lax
from jax.experimental import pallas as pl
from jax.experimental.pallas import tpu as pltpu
from jax.sharding import Mesh, PartitionSpec as P

AXES = ("group", "z", "core")
LANES = 128
CHUNK = 512
TAIL = 16
VMEM = pl.BlockSpec(memory_space=pltpu.VMEM)


def flip(count, bits):
    return [(k, k ^ bits) for k in range(count)]


def unit_rows(values):
    values = values.astype(jnp.float32)
    total = jnp.sum(values * values, axis=1, keepdims=True) + values.shape[1] * 1e-06
    return (values * lax.rsqrt(total)).astype(jnp.bfloat16)


def ring_pairs(length, shift):
    if 2 * shift < length:
        return [(k, (k + shift) % length) for k in range(length)]
    pairs = [(k, k + shift) for k in range(length // 2)]
    return [pair[:: 1 - 2 * (pair[0] % 2)] for pair in pairs]


def swap(block):
    return lax.ppermute(block, "core", flip(2, 1))


def pack_into(block_ref, start, rows, ids):
    count, width = rows.shape
    place = pl.ds(start, count)
    block_ref[place, :width] = unit_rows(rows)
    meta = jnp.concatenate([ids.astype(jnp.float32), jnp.zeros((6, count), jnp.float32)], axis=0)
    if count < LANES:
        meta = jnp.concatenate([meta, jnp.zeros((8, LANES - count), jnp.float32)], axis=1)
    turned = meta.T[:count]
    cluster, order = turned[:, 0:1] + 1.0, turned[:, 1:2]
    high = jnp.floor(order / 256.0)
    lane = lax.broadcasted_iota(jnp.int32, (count, LANES), 1)
    tail = jnp.where(lane == 0, cluster, jnp.where(lane == 1, high, order - 256.0 * high))
    block_ref[place, width:] = jnp.where(lane < 3, tail, 0.0).astype(jnp.bfloat16)


def pack_kernel(rows_ref, ids_ref, block_ref):
    pack_into(block_ref, 0, rows_ref[...], ids_ref[...])


def pair_kernel(own_ref, own_ids_ref, rows_ref, ids_ref, both_ref, line_ref):
    count, width = rows_ref.shape
    both_ref[:count, :] = own_ref[...]
    pack_into(both_ref, count, rows_ref[...], ids_ref[...])
    for k in range(width // LANES):
        columns = both_ref[:, k * LANES : (k + 1) * LANES]
        line_ref[2 * count * k : 2 * count * (k + 1), :] = columns
    lines = []
    for ref in (own_ids_ref, ids_ref):
        ids = ref[...].astype(jnp.float32)
        high = jnp.floor(ids[1:2] / 256.0)
        lines += [ids[0:1] + 1.0, high, ids[1:2] - 256.0 * high]
    tail = jnp.concatenate(lines + [jnp.zeros((TAIL - 6, count), jnp.float32)], axis=0)
    if count < LANES:
        tail = jnp.concatenate([tail, jnp.zeros((TAIL, LANES - count), jnp.float32)], axis=1)
    line_ref[2 * count * (width // LANES) :, :] = tail.astype(jnp.bfloat16)


def pack(kernel, operands, shapes):
    rows, width = operands[-2].shape
    return pl.pallas_call(
        kernel,
        in_specs=[VMEM] * len(operands),
        out_specs=[VMEM] * len(shapes),
        out_shape=[jax.ShapeDtypeStruct(shape, jnp.bfloat16) for shape in shapes],
        compiler_params=pltpu.CompilerParams(vmem_limit_bytes=8 * 2**20),
        cost_estimate=pl.CostEstimate(
            flops=4 * rows * width, bytes_accessed=4 * rows * width, transcendentals=rows
        ),
    )(*operands)


def padded(rows):
    spare = -rows.shape[0] % LANES
    if not spare:
        return rows
    return jnp.concatenate([rows, jnp.zeros((spare, rows.shape[1]), rows.dtype)], axis=0)


def own_kernel(*refs):
    own_ref, row_ref, dots = refs[0], *refs[-2:]
    rows, width = own_ref.shape[0], own_ref.shape[1] - LANES
    turned = padded(own_ref[:, width:].astype(jnp.float32)).T
    meta = [(turned[0:1], turned[1:2] * 256.0 + turned[2:3])]

    def visitors_at(k):
        return padded(own_ref[:, k : k + CHUNK])

    bests, _ = best_of(visitors_at, meta, refs[1:-2], rows, False, dots)
    row_ref[...] = bests[0]


def visit_kernel(visitors, arrays, mine, others, *refs):
    line_refs, block_refs = refs[:visitors], refs[visitors : visitors + arrays]
    row_ref, mine_ref, other_ref, dots = refs[visitors + arrays + 1 :]
    width = block_refs[0].shape[1] - LANES
    rows = (line_refs[0].shape[0] - TAIL) // (2 * width // LANES)
    meta = []
    for ref in line_refs:
        tail = ref[2 * rows * (width // LANES) :, :].astype(jnp.float32)
        for row in (0, 3):
            order = tail[row + 1 : row + 2] * 256.0 + tail[row + 2 : row + 3]
            meta.append((tail[row : row + 1], order))

    def visitors_at(k):
        parts = []
        for ref in line_refs:
            for core in range(2):
                starts = [rows * (2 * block + core) for block in range(k // LANES, (k + CHUNK) // LANES)]
                columns = [ref[start : start + rows, :] for start in starts]
                parts.append(padded(jnp.concatenate(columns, axis=1)))
        return jnp.concatenate(parts, axis=0)

    bests, cols = best_of(visitors_at, meta, block_refs, rows, True, dots)
    for v, best in enumerate(bests):
        row_ref[v : v + 1, :] = best
    for ref, picked in ((mine_ref, mine), (other_ref, others)):
        for row, j in enumerate(picked):
            ref[row : row + 1, :] = cols[j]


def best_of(visitors_at, meta, block_refs, rows, homed, dots):
    width = block_refs[0].shape[1] - LANES
    for k in range(0, width, CHUNK):
        left = jnp.concatenate([ref[:, k : k + CHUNK] for ref in block_refs], axis=0)
        part = lax.dot_general(
            left,
            visitors_at(k),
            (((1,), (1,)), ((), ())),
            preferred_element_type=jnp.float32,
        )
        dots[...] = part if k == 0 else dots[...] + part

    tails = jnp.concatenate([ref[:, width:] for ref in block_refs], axis=0).astype(jnp.float32)
    row_best = [jnp.full((1, LANES), -1.0, jnp.float32) for _ in meta]
    lane = lax.broadcasted_iota(jnp.int32, (rows, LANES), 1)
    col_all = jnp.full((rows, LANES), -1.0, jnp.float32)
    for j in range(dots.shape[0] // rows):
        tail = tails[j * rows : (j + 1) * rows]
        block_cluster, block_order = tail[:, 0:1], tail[:, 1:2] * 256.0 + tail[:, 2:3]
        col_best = jnp.full((rows, 1), -1.0, jnp.float32)
        for v, (cluster, order) in enumerate(meta):
            cosine = dots[j * rows : (j + 1) * rows, v * LANES : (v + 1) * LANES]
            same = (block_cluster == cluster) & (cluster > 0)
            seen = jnp.where(same & (block_order < order), cosine, -1.0)
            row_best[v] = jnp.maximum(row_best[v], jnp.max(seen, axis=0, keepdims=True))
            if homed:
                seen = jnp.where(same & (order < block_order), cosine, -1.0)
                col_best = jnp.maximum(col_best, jnp.max(seen, axis=1, keepdims=True))
        col_all = jnp.where(lane == j, col_best, col_all)
    if not homed:
        return row_best, None
    if rows < LANES:
        fill = jnp.full((LANES - rows, LANES), -1.0, jnp.float32)
        col_all = jnp.concatenate([col_all, fill], axis=0)
    turned = col_all.T
    return row_best, [turned[j : j + 1] for j in range(dots.shape[0] // rows)]


def call(kernel, operands, count, out_rows, total, width):
    return pl.pallas_call(
        kernel,
        in_specs=[VMEM] * len(operands),
        out_specs=[VMEM] * len(out_rows),
        out_shape=[jax.ShapeDtypeStruct((n, LANES), jnp.float32) for n in out_rows],
        scratch_shapes=[pltpu.VMEM((total, count * LANES), jnp.float32)],
        compiler_params=pltpu.CompilerParams(vmem_limit_bytes=24 * 2**20),
        cost_estimate=pl.CostEstimate(
            flops=2 * total * count * LANES * width,
            bytes_accessed=2 * (total + count * LANES) * width,
            transcendentals=0,
        ),
    )(*operands)


def group_trip(groups, first, second):
    return [(2 * k + c, 2 * (k ^ s) + c) for k in range(groups) for c, s in enumerate((first, second))]


def local(embeddings, cluster_ids, order_index):
    rows, width = embeddings.shape
    groups, length = lax.axis_size("group"), lax.axis_size("z")
    z, core = lax.axis_index("z"), lax.axis_index("core")
    plane_axes, line_axes = ("group", "core"), ("z", "core")
    ids = jnp.stack([cluster_ids, order_index])
    (own,) = pack(pack_kernel, [embeddings, ids], [(rows, width + LANES)])
    shapes = [(2 * rows, width + LANES), (2 * rows * width // LANES + TAIL, LANES)]
    both, line = pack(pair_kernel, [own, ids, swap(embeddings), swap(ids)], shapes)

    routes = [ring_pairs(length, shift) for shift in range(1, length // 2 + 1)]
    trips = []
    for first in range(0, len(routes), 2):
        ways = enumerate(routes[first : first + 2][::-1])
        trips.append([(2 * a + way, 2 * b + way) for way, route in ways for a, b in route])
    visitors = [lax.ppermute(line, line_axes, trip) for trip in trips]

    partners = [(s, s + 1) for s in range(1, groups - 1, 2)]
    arrived = [lax.ppermute(both, plane_axes, group_trip(groups, *way)) for way in partners]
    last = groups - 1
    relay = group_trip(groups, last ^ partners[-1][0], last ^ partners[-1][1])
    half = rows // 2
    corner = [arrived[-1][first : first + half] for first in (0, half)]
    corner = [lax.ppermute(part, plane_axes, relay) for part in corner]
    sides = [(block, swap(block)) for block in arrived]
    chunks = [[both, *sides[-1], *corner, *(swap(part) for part in corner)]]
    chunks += [[*sides[k], *sides[k + 1]] for k in range(0, len(sides) - 1, 2)]

    orders = [((2, 5, 6, 0), (4, 3, 7, 1))] + [((0, 3, 4, 7), (2, 1, 6, 5))] * (len(chunks) - 1)
    bests, answers = [], []
    for chunk in chunks:
        bests += call(own_kernel, [own, *chunk], 1, [1], 8 * rows, width)
    for index, (chunk, order) in enumerate(zip(chunks, orders)):
        kernel = functools.partial(visit_kernel, len(visitors), len(chunk), *order)
        count = 2 * len(visitors)
        operands = [*visitors, *chunk, bests[index]]
        answers.append(call(kernel, operands, count, [count, 4, 4], 8 * rows, width))
    home = functools.reduce(jnp.maximum, [answer[0] for answer in answers])
    merged = [jnp.maximum(mine, swap(others)) for _, mine, others in answers]

    for index, trip in enumerate(trips):
        part = home[2 * index : 2 * index + 2] if len(trips) > 1 else home
        back = lax.ppermute(part, line_axes, [(b, a) for a, b in trip])
        for here, best in ((2 * z + core, back[0:1]), (2 * z + (core ^ 1), swap(back)[1:2])):
            sent = functools.reduce(jnp.logical_or, [here == a for a, _ in trip])
            bests.append(jnp.where(sent, best, -1.0))
    ways = [(0, 0, partners[-1])]
    ways += [(1 + k // 2, 2 * (k % 2), way) for k, way in enumerate(partners[:-1])]
    for chunk, row, (first, second) in ways:
        got = lax.ppermute(merged[chunk], plane_axes, group_trip(groups, second, first))
        bests.append(got[row + 1 : row + 2])
    bests.append(lax.ppermute(merged[0], "group", flip(groups, last))[2:3])
    for chunk, row, (first, second) in ways:
        got = lax.ppermute(merged[chunk], plane_axes, group_trip(groups, first, second))
        bests.append(got[row : row + 1])
    bests.append(merged[0][3:4])
    return functools.reduce(jnp.maximum, bests)[0, :rows]


def solution(mesh):
    groups, members = mesh.devices.shape
    fine = Mesh(mesh.devices.reshape(groups, members // 2, 2), AXES)
    placed = (P(AXES, None), P(AXES), P(AXES))
    return jax.shard_map(local, mesh=fine, in_specs=placed, out_specs=P(AXES), check_vma=False)
```

```python
import functools

import jax
import jax.numpy as jnp
from jax import lax
from jax.experimental import pallas as pl
from jax.experimental.pallas import tpu as pltpu
from jax.sharding import Mesh, PartitionSpec as P

AXES = ("group", "z", "core")
LANES = 128
CHUNK = 512
TAIL = 16
VMEM = pl.BlockSpec(memory_space=pltpu.VMEM)


def flip(count, bits):
    return [(k, k ^ bits) for k in range(count)]


def unit_rows(values):
    values = values.astype(jnp.float32)
    total = jnp.sum(values * values, axis=1, keepdims=True) + values.shape[1] * 1e-06
    return (values * lax.rsqrt(total)).astype(jnp.bfloat16)


def ring_pairs(length, shift):
    if 2 * shift < length:
        return [(k, (k + shift) % length) for k in range(length)]
    pairs = [(k, k + shift) for k in range(length // 2)]
    return [pair[:: 1 - 2 * (pair[0] % 2)] for pair in pairs]


def swap(block):
    return lax.ppermute(block, "core", flip(2, 1))


def pack_into(block_ref, start, rows, ids):
    count, width = rows.shape
    place = pl.ds(start, count)
    block_ref[place, :width] = unit_rows(rows)
    meta = jnp.concatenate([ids.astype(jnp.float32), jnp.zeros((6, count), jnp.float32)], axis=0)
    if count < LANES:
        meta = jnp.concatenate([meta, jnp.zeros((8, LANES - count), jnp.float32)], axis=1)
    turned = meta.T[:count]
    cluster, order = turned[:, 0:1] + 1.0, turned[:, 1:2]
    high = jnp.floor(order / 256.0)
    lane = lax.broadcasted_iota(jnp.int32, (count, LANES), 1)
    tail = jnp.where(lane == 0, cluster, jnp.where(lane == 1, high, order - 256.0 * high))
    block_ref[place, width:] = jnp.where(lane < 3, tail, 0.0).astype(jnp.bfloat16)


def pack_kernel(rows_ref, ids_ref, block_ref):
    pack_into(block_ref, 0, rows_ref[...], ids_ref[...])


def pair_kernel(own_ref, own_ids_ref, rows_ref, ids_ref, both_ref, line_ref):
    count, width = rows_ref.shape
    both_ref[:count, :] = own_ref[...]
    pack_into(both_ref, count, rows_ref[...], ids_ref[...])
    for k in range(width // LANES):
        columns = both_ref[:, k * LANES : (k + 1) * LANES]
        line_ref[2 * count * k : 2 * count * (k + 1), :] = columns
    lines = []
    for ref in (own_ids_ref, ids_ref):
        ids = ref[...].astype(jnp.float32)
        high = jnp.floor(ids[1:2] / 256.0)
        lines += [ids[0:1] + 1.0, high, ids[1:2] - 256.0 * high]
    tail = jnp.concatenate(lines + [jnp.zeros((TAIL - 6, count), jnp.float32)], axis=0)
    if count < LANES:
        tail = jnp.concatenate([tail, jnp.zeros((TAIL, LANES - count), jnp.float32)], axis=1)
    line_ref[2 * count * (width // LANES) :, :] = tail.astype(jnp.bfloat16)


def pack(kernel, operands, shapes):
    rows, width = operands[-2].shape
    return pl.pallas_call(
        kernel,
        in_specs=[VMEM] * len(operands),
        out_specs=[VMEM] * len(shapes),
        out_shape=[jax.ShapeDtypeStruct(shape, jnp.bfloat16) for shape in shapes],
        compiler_params=pltpu.CompilerParams(vmem_limit_bytes=8 * 2**20),
        cost_estimate=pl.CostEstimate(
            flops=4 * rows * width, bytes_accessed=4 * rows * width, transcendentals=rows
        ),
    )(*operands)


def padded(rows):
    spare = -rows.shape[0] % LANES
    if not spare:
        return rows
    return jnp.concatenate([rows, jnp.zeros((spare, rows.shape[1]), rows.dtype)], axis=0)


def own_kernel(*refs):
    own_ref, row_ref, dots = refs[0], *refs[-2:]
    rows, width = own_ref.shape[0], own_ref.shape[1] - LANES
    turned = padded(own_ref[:, width:].astype(jnp.float32)).T
    meta = [(turned[0:1], turned[1:2] * 256.0 + turned[2:3])]

    def visitors_at(k):
        return padded(own_ref[:, k : k + CHUNK])

    bests, _ = best_of(visitors_at, meta, refs[1:-2], rows, False, dots)
    row_ref[...] = bests[0]


def visit_kernel(visitors, arrays, mine, others, *refs):
    line_refs, block_refs = refs[:visitors], refs[visitors : visitors + arrays]
    row_ref, mine_ref, other_ref, dots = refs[visitors + arrays + 1 :]
    width = block_refs[0].shape[1] - LANES
    rows = (line_refs[0].shape[0] - TAIL) // (2 * width // LANES)
    meta = []
    for ref in line_refs:
        tail = ref[2 * rows * (width // LANES) :, :].astype(jnp.float32)
        for row in (0, 3):
            order = tail[row + 1 : row + 2] * 256.0 + tail[row + 2 : row + 3]
            meta.append((tail[row : row + 1], order))

    def visitors_at(k):
        parts = []
        for ref in line_refs:
            for core in range(2):
                starts = [rows * (2 * block + core) for block in range(k // LANES, (k + CHUNK) // LANES)]
                columns = [ref[start : start + rows, :] for start in starts]
                parts.append(padded(jnp.concatenate(columns, axis=1)))
        return jnp.concatenate(parts, axis=0)

    bests, cols = best_of(visitors_at, meta, block_refs, rows, True, dots)
    for v, best in enumerate(bests):
        row_ref[v : v + 1, :] = best
    for ref, picked in ((mine_ref, mine), (other_ref, others)):
        for row, j in enumerate(picked):
            ref[row : row + 1, :] = cols[j]


def best_of(visitors_at, meta, block_refs, rows, homed, dots):
    width = block_refs[0].shape[1] - LANES
    for k in range(0, width, CHUNK):
        left = jnp.concatenate([ref[:, k : k + CHUNK] for ref in block_refs], axis=0)
        part = lax.dot_general(
            left,
            visitors_at(k),
            (((1,), (1,)), ((), ())),
            preferred_element_type=jnp.float32,
        )
        dots[...] = part if k == 0 else dots[...] + part

    tails = jnp.concatenate([ref[:, width:] for ref in block_refs], axis=0).astype(jnp.float32)
    row_best = [jnp.full((1, LANES), -1.0, jnp.float32) for _ in meta]
    lane = lax.broadcasted_iota(jnp.int32, (rows, LANES), 1)
    col_all = jnp.full((rows, LANES), -1.0, jnp.float32)
    for j in range(dots.shape[0] // rows):
        tail = tails[j * rows : (j + 1) * rows]
        block_cluster, block_order = tail[:, 0:1], tail[:, 1:2] * 256.0 + tail[:, 2:3]
        col_best = jnp.full((rows, 1), -1.0, jnp.float32)
        for v, (cluster, order) in enumerate(meta):
            cosine = dots[j * rows : (j + 1) * rows, v * LANES : (v + 1) * LANES]
            same = (block_cluster == cluster) & (cluster > 0)
            seen = jnp.where(same & (block_order < order), cosine, -1.0)
            row_best[v] = jnp.maximum(row_best[v], jnp.max(seen, axis=0, keepdims=True))
            if homed:
                seen = jnp.where(same & (order < block_order), cosine, -1.0)
                col_best = jnp.maximum(col_best, jnp.max(seen, axis=1, keepdims=True))
        col_all = jnp.where(lane == j, col_best, col_all)
    if not homed:
        return row_best, None
    if rows < LANES:
        fill = jnp.full((LANES - rows, LANES), -1.0, jnp.float32)
        col_all = jnp.concatenate([col_all, fill], axis=0)
    turned = col_all.T
    return row_best, [turned[j : j + 1] for j in range(dots.shape[0] // rows)]


def call(kernel, operands, count, out_rows, total, width):
    return pl.pallas_call(
        kernel,
        in_specs=[VMEM] * len(operands),
        out_specs=[VMEM] * len(out_rows),
        out_shape=[jax.ShapeDtypeStruct((n, LANES), jnp.float32) for n in out_rows],
        scratch_shapes=[pltpu.VMEM((total, count * LANES), jnp.float32)],
        compiler_params=pltpu.CompilerParams(vmem_limit_bytes=24 * 2**20),
        cost_estimate=pl.CostEstimate(
            flops=2 * total * count * LANES * width,
            bytes_accessed=2 * (total + count * LANES) * width,
            transcendentals=0,
        ),
    )(*operands)


def group_trip(groups, first, second):
    return [(2 * k + c, 2 * (k ^ s) + c) for k in range(groups) for c, s in enumerate((first, second))]


def local(embeddings, cluster_ids, order_index):
    rows, width = embeddings.shape
    groups, length = lax.axis_size("group"), lax.axis_size("z")
    z, core = lax.axis_index("z"), lax.axis_index("core")
    plane_axes, line_axes = ("group", "core"), ("z", "core")
    ids = jnp.stack([cluster_ids, order_index])
    (own,) = pack(pack_kernel, [embeddings, ids], [(rows, width + LANES)])
    shapes = [(2 * rows, width + LANES), (2 * rows * width // LANES + TAIL, LANES)]
    both, line = pack(pair_kernel, [own, ids, swap(embeddings), swap(ids)], shapes)

    routes = [ring_pairs(length, shift) for shift in range(1, length // 2 + 1)]
    trips = []
    for first in range(0, len(routes), 2):
        ways = enumerate(routes[first : first + 2][::-1])
        trips.append([(2 * a + way, 2 * b + way) for way, route in ways for a, b in route])
    visitors = [lax.ppermute(line, line_axes, trip) for trip in trips]

    partners = [(s, s + 1) for s in range(1, groups - 1, 2)]
    arrived = [lax.ppermute(both, plane_axes, group_trip(groups, *way)) for way in partners]
    last = groups - 1
    relay = group_trip(groups, last ^ partners[-1][0], last ^ partners[-1][1])
    half = rows // 2
    corner = [arrived[-1][first : first + half] for first in (0, half)]
    corner = [lax.ppermute(part, plane_axes, relay) for part in corner]
    sides = [(block, swap(block)) for block in arrived]
    chunks = [[both, *sides[-1], *corner, *(swap(part) for part in corner)]]
    chunks += [[*sides[k], *sides[k + 1]] for k in range(0, len(sides) - 1, 2)]

    orders = [((2, 5, 6, 0), (4, 3, 7, 1))] + [((0, 3, 4, 7), (2, 1, 6, 5))] * (len(chunks) - 1)
    bests, answers = [], []
    for chunk in chunks:
        bests += call(own_kernel, [own, *chunk], 1, [1], 8 * rows, width)
    for index, (chunk, order) in enumerate(zip(chunks, orders)):
        kernel = functools.partial(visit_kernel, len(visitors), len(chunk), *order)
        count = 2 * len(visitors)
        operands = [*visitors, *chunk, bests[index]]
        answers.append(call(kernel, operands, count, [count, 4, 4], 8 * rows, width))
    bests = [best[0, :rows] for best in bests]
    home = functools.reduce(jnp.maximum, [answer[0] for answer in answers])
    merged = [jnp.maximum(mine, swap(others)) for _, mine, others in answers]

    for index, trip in enumerate(trips):
        part = home[2 * index : 2 * index + 2] if len(trips) > 1 else home
        back = lax.ppermute(part, line_axes, [(b, a) for a, b in trip])
        for here, best in ((2 * z + core, back[0:1]), (2 * z + (core ^ 1), swap(back)[1:2])):
            sent = functools.reduce(jnp.logical_or, [here == a for a, _ in trip])
            bests.append(jnp.where(sent, best[0, :rows], -1.0))
    ways = [(0, 0, partners[-1])]
    ways += [(1 + k // 2, 2 * (k % 2), way) for k, way in enumerate(partners[:-1])]
    for chunk, row, (first, second) in ways:
        for offset, order in ((1, (second, first)), (0, (first, second))):
            got = lax.ppermute(merged[chunk], plane_axes, group_trip(groups, *order))
            bests.append(got[row + offset, :rows])
    bests.append(lax.ppermute(merged[0], "group", flip(groups, last))[2, :rows])
    bests.append(merged[0][3, :rows])
    return functools.reduce(jnp.maximum, bests)


def solution(mesh):
    groups, members = mesh.devices.shape
    fine = Mesh(mesh.devices.reshape(groups, members // 2, 2), AXES)
    placed = (P(AXES, None), P(AXES), P(AXES))
    return jax.shard_map(local, mesh=fine, in_specs=placed, out_specs=P(AXES), check_vma=False)
```

```python
import functools

import jax
import jax.numpy as jnp
from jax import lax
from jax.experimental import pallas as pl
from jax.experimental.pallas import tpu as pltpu
from jax.sharding import Mesh, PartitionSpec as P

AXES = ("group", "z", "core")
LANES = 128
CHUNK = 512
TAIL = 16
VMEM = pl.BlockSpec(memory_space=pltpu.VMEM)


def flip(count, bits):
    return [(k, k ^ bits) for k in range(count)]


def unit_rows(values):
    values = values.astype(jnp.float32)
    total = jnp.sum(values * values, axis=1, keepdims=True) + values.shape[1] * 1e-06
    return (values * lax.rsqrt(total)).astype(jnp.bfloat16)


def ring_pairs(length, shift):
    if 2 * shift < length:
        return [(k, (k + shift) % length) for k in range(length)]
    pairs = [(k, k + shift) for k in range(length // 2)]
    return [pair[:: 1 - 2 * (pair[0] % 2)] for pair in pairs]


def swap(block):
    return lax.ppermute(block, "core", flip(2, 1))


def pack_into(block_ref, start, rows, ids):
    count, width = rows.shape
    place = pl.ds(start, count)
    block_ref[place, :width] = unit_rows(rows)
    meta = jnp.concatenate([ids.astype(jnp.float32), jnp.zeros((6, count), jnp.float32)], axis=0)
    if count < LANES:
        meta = jnp.concatenate([meta, jnp.zeros((8, LANES - count), jnp.float32)], axis=1)
    turned = meta.T[:count]
    cluster, order = turned[:, 0:1] + 1.0, turned[:, 1:2]
    high = jnp.floor(order / 256.0)
    lane = lax.broadcasted_iota(jnp.int32, (count, LANES), 1)
    tail = jnp.where(lane == 0, cluster, jnp.where(lane == 1, high, order - 256.0 * high))
    block_ref[place, width:] = jnp.where(lane < 3, tail, 0.0).astype(jnp.bfloat16)


def pack_kernel(rows_ref, ids_ref, block_ref):
    pack_into(block_ref, 0, rows_ref[...], ids_ref[...])


def pair_kernel(own_ref, own_ids_ref, rows_ref, ids_ref, both_ref, line_ref):
    count, width = rows_ref.shape
    both_ref[:count, :] = own_ref[...]
    pack_into(both_ref, count, rows_ref[...], ids_ref[...])
    for k in range(width // LANES):
        columns = both_ref[:, k * LANES : (k + 1) * LANES]
        line_ref[2 * count * k : 2 * count * (k + 1), :] = columns
    lines = []
    for ref in (own_ids_ref, ids_ref):
        ids = ref[...].astype(jnp.float32)
        high = jnp.floor(ids[1:2] / 256.0)
        lines += [ids[0:1] + 1.0, high, ids[1:2] - 256.0 * high]
    tail = jnp.concatenate(lines + [jnp.zeros((TAIL - 6, count), jnp.float32)], axis=0)
    if count < LANES:
        tail = jnp.concatenate([tail, jnp.zeros((TAIL, LANES - count), jnp.float32)], axis=1)
    line_ref[2 * count * (width // LANES) :, :] = tail.astype(jnp.bfloat16)


def pack(kernel, operands, shapes):
    rows, width = operands[-2].shape
    return pl.pallas_call(
        kernel,
        in_specs=[VMEM] * len(operands),
        out_specs=[VMEM] * len(shapes),
        out_shape=[jax.ShapeDtypeStruct(shape, jnp.bfloat16) for shape in shapes],
        compiler_params=pltpu.CompilerParams(vmem_limit_bytes=8 * 2**20),
        cost_estimate=pl.CostEstimate(
            flops=4 * rows * width, bytes_accessed=4 * rows * width, transcendentals=rows
        ),
    )(*operands)


def padded(rows):
    spare = -rows.shape[0] % LANES
    if not spare:
        return rows
    return jnp.concatenate([rows, jnp.zeros((spare, rows.shape[1]), rows.dtype)], axis=0)


def own_kernel(*refs):
    own_ref, row_ref, dots = refs[0], *refs[-2:]
    rows, width = own_ref.shape[0], own_ref.shape[1] - LANES
    turned = padded(own_ref[:, width:].astype(jnp.float32)).T
    meta = [(turned[0:1], turned[1:2] * 256.0 + turned[2:3])]

    def visitors_at(k):
        return padded(own_ref[:, k : k + CHUNK])

    bests, _ = best_of(visitors_at, meta, refs[1:-2], rows, False, dots)
    row_ref[...] = bests[0]


def visit_kernel(visitors, arrays, mine, others, *refs):
    line_refs, block_refs = refs[:visitors], refs[visitors : visitors + arrays]
    row_ref, mine_ref, other_ref, dots = refs[visitors + arrays + 1 :]
    width = block_refs[0].shape[1] - LANES
    rows = (line_refs[0].shape[0] - TAIL) // (2 * width // LANES)
    meta = []
    for ref in line_refs:
        tail = ref[2 * rows * (width // LANES) :, :].astype(jnp.float32)
        for row in (0, 3):
            order = tail[row + 1 : row + 2] * 256.0 + tail[row + 2 : row + 3]
            meta.append((tail[row : row + 1], order))

    def visitors_at(k):
        parts = []
        for ref in line_refs:
            for core in range(2):
                starts = [rows * (2 * block + core) for block in range(k // LANES, (k + CHUNK) // LANES)]
                columns = [ref[start : start + rows, :] for start in starts]
                parts.append(padded(jnp.concatenate(columns, axis=1)))
        return jnp.concatenate(parts, axis=0)

    bests, cols = best_of(visitors_at, meta, block_refs, rows, True, dots)
    for v, best in enumerate(bests):
        row_ref[v : v + 1, :] = best
    for ref, picked in ((mine_ref, mine), (other_ref, others)):
        for row, j in enumerate(picked):
            ref[row : row + 1, :] = cols[j]


def best_of(visitors_at, meta, block_refs, rows, homed, dots):
    width = block_refs[0].shape[1] - LANES
    for k in range(0, width, CHUNK):
        left = jnp.concatenate([ref[:, k : k + CHUNK] for ref in block_refs], axis=0)
        part = lax.dot_general(
            left,
            visitors_at(k),
            (((1,), (1,)), ((), ())),
            preferred_element_type=jnp.float32,
        )
        dots[...] = part if k == 0 else dots[...] + part

    tails = jnp.concatenate([ref[:, width:] for ref in block_refs], axis=0).astype(jnp.float32)
    row_best = [jnp.full((1, LANES), -1.0, jnp.float32) for _ in meta]
    lane = lax.broadcasted_iota(jnp.int32, (rows, LANES), 1)
    col_all = jnp.full((rows, LANES), -1.0, jnp.float32)
    for j in range(dots.shape[0] // rows):
        tail = tails[j * rows : (j + 1) * rows]
        block_cluster, block_order = tail[:, 0:1], tail[:, 1:2] * 256.0 + tail[:, 2:3]
        col_best = jnp.full((rows, 1), -1.0, jnp.float32)
        for v, (cluster, order) in enumerate(meta):
            cosine = dots[j * rows : (j + 1) * rows, v * LANES : (v + 1) * LANES]
            same = (block_cluster == cluster) & (cluster > 0)
            seen = jnp.where(same & (block_order < order), cosine, -1.0)
            row_best[v] = jnp.maximum(row_best[v], jnp.max(seen, axis=0, keepdims=True))
            if homed:
                seen = jnp.where(same & (order < block_order), cosine, -1.0)
                col_best = jnp.maximum(col_best, jnp.max(seen, axis=1, keepdims=True))
        col_all = jnp.where(lane == j, col_best, col_all)
    if not homed:
        return row_best, None
    if rows < LANES:
        fill = jnp.full((LANES - rows, LANES), -1.0, jnp.float32)
        col_all = jnp.concatenate([col_all, fill], axis=0)
    turned = col_all.T
    return row_best, [turned[j : j + 1] for j in range(dots.shape[0] // rows)]


def call(kernel, operands, count, out_rows, total, width):
    return pl.pallas_call(
        kernel,
        in_specs=[VMEM] * len(operands),
        out_specs=[VMEM] * len(out_rows),
        out_shape=[jax.ShapeDtypeStruct((n, LANES), jnp.float32) for n in out_rows],
        scratch_shapes=[pltpu.VMEM((total, count * LANES), jnp.float32)],
        compiler_params=pltpu.CompilerParams(vmem_limit_bytes=24 * 2**20),
        cost_estimate=pl.CostEstimate(
            flops=2 * total * count * LANES * width,
            bytes_accessed=2 * (total + count * LANES) * width,
            transcendentals=0,
        ),
    )(*operands)


def group_trip(groups, first, second):
    return [(2 * k + c, 2 * (k ^ s) + c) for k in range(groups) for c, s in enumerate((first, second))]


def local(embeddings, cluster_ids, order_index):
    rows, width = embeddings.shape
    groups, length = lax.axis_size("group"), lax.axis_size("z")
    z, core = lax.axis_index("z"), lax.axis_index("core")
    plane_axes, line_axes = ("group", "core"), ("z", "core")
    ids = jnp.stack([cluster_ids, order_index])
    (own,) = pack(pack_kernel, [embeddings, ids], [(rows, width + LANES)])
    shapes = [(2 * rows, width + LANES), (2 * rows * width // LANES + TAIL, LANES)]
    both, line = pack(pair_kernel, [own, ids, swap(embeddings), swap(ids)], shapes)

    routes = [ring_pairs(length, shift) for shift in range(1, length // 2 + 1)]
    trips = []
    for first in range(0, len(routes), 2):
        ways = enumerate(routes[first : first + 2][::-1])
        trips.append([(2 * a + way, 2 * b + way) for way, route in ways for a, b in route])
    visitors = [lax.ppermute(line, line_axes, trip) for trip in trips]

    partners = [(s + 1, s) for s in range(1, groups - 1, 2)]
    arrived = [lax.ppermute(both, plane_axes, group_trip(groups, *way)) for way in partners]
    last = groups - 1
    relay = group_trip(groups, last ^ partners[-1][0], last ^ partners[-1][1])
    half = rows // 2
    corner = [arrived[-1][first : first + half] for first in (0, half)]
    corner = [lax.ppermute(part, plane_axes, relay) for part in corner]
    sides = [(block, swap(block)) for block in arrived]
    chunks = [[both, *sides[-1], *corner, *(swap(part) for part in corner)]]
    chunks += [[*sides[k], *sides[k + 1]] for k in range(0, len(sides) - 1, 2)]

    orders = [((2, 5, 6, 0), (4, 3, 7, 1))] + [((0, 3, 4, 7), (2, 1, 6, 5))] * (len(chunks) - 1)
    bests, answers = [], []
    for chunk in chunks:
        bests += call(own_kernel, [own, *chunk], 1, [1], 8 * rows, width)
    for index, (chunk, order) in enumerate(zip(chunks, orders)):
        kernel = functools.partial(visit_kernel, len(visitors), len(chunk), *order)
        count = 2 * len(visitors)
        operands = [*visitors, *chunk, bests[index]]
        answers.append(call(kernel, operands, count, [count, 4, 4], 8 * rows, width))
    bests = [best[0, :rows] for best in bests]
    home = functools.reduce(jnp.maximum, [answer[0] for answer in answers])
    merged = [jnp.maximum(mine, swap(others)) for _, mine, others in answers]

    for index, trip in enumerate(trips):
        part = home[2 * index : 2 * index + 2] if len(trips) > 1 else home
        back = lax.ppermute(part, line_axes, [(b, a) for a, b in trip])
        for here, best in ((2 * z + core, back[0:1]), (2 * z + (core ^ 1), swap(back)[1:2])):
            sent = functools.reduce(jnp.logical_or, [here == a for a, _ in trip])
            bests.append(jnp.where(sent, best[0, :rows], -1.0))
    ways = [(0, 0, partners[-1])]
    ways += [(1 + k // 2, 2 * (k % 2), way) for k, way in enumerate(partners[:-1])]
    for chunk, row, (first, second) in ways:
        for offset, order in ((1, (second, first)), (0, (first, second))):
            got = lax.ppermute(merged[chunk], plane_axes, group_trip(groups, *order))
            bests.append(got[row + offset, :rows])
    bests.append(lax.ppermute(merged[0], "group", flip(groups, last))[2, :rows])
    bests.append(merged[0][3, :rows])
    return functools.reduce(jnp.maximum, bests)


def solution(mesh):
    groups, members = mesh.devices.shape
    fine = Mesh(mesh.devices.reshape(groups, members // 2, 2), AXES)
    placed = (P(AXES, None), P(AXES), P(AXES))
    return jax.shard_map(local, mesh=fine, in_specs=placed, out_specs=P(AXES), check_vma=False)
```

```python
import functools

import jax
import jax.numpy as jnp
from jax import lax
from jax.experimental import pallas as pl
from jax.experimental.pallas import tpu as pltpu
from jax.sharding import Mesh, PartitionSpec as P

AXES = ("group", "z", "core")
LANES = 128
CHUNK = 512
TAIL = 16
VMEM = pl.BlockSpec(memory_space=pltpu.VMEM)


def flip(count, bits):
    return [(k, k ^ bits) for k in range(count)]


def unit_rows(values):
    values = values.astype(jnp.float32)
    total = jnp.sum(values * values, axis=1, keepdims=True) + values.shape[1] * 1e-06
    return (values * lax.rsqrt(total)).astype(jnp.bfloat16)


def ring_pairs(length, shift):
    if 2 * shift < length:
        return [(k, (k + shift) % length) for k in range(length)]
    pairs = [(k, k + shift) for k in range(length // 2)]
    return [pair[:: 1 - 2 * (pair[0] % 2)] for pair in pairs]


def swap(block):
    return lax.ppermute(block, "core", flip(2, 1))


def pack_into(block_ref, start, rows, ids):
    count, width = rows.shape
    place = pl.ds(start, count)
    block_ref[place, :width] = unit_rows(rows)
    meta = jnp.concatenate([ids.astype(jnp.float32), jnp.zeros((6, count), jnp.float32)], axis=0)
    if count < LANES:
        meta = jnp.concatenate([meta, jnp.zeros((8, LANES - count), jnp.float32)], axis=1)
    turned = meta.T[:count]
    cluster, order = turned[:, 0:1] + 1.0, turned[:, 1:2]
    high = jnp.floor(order / 256.0)
    lane = lax.broadcasted_iota(jnp.int32, (count, LANES), 1)
    tail = jnp.where(lane == 0, cluster, jnp.where(lane == 1, high, order - 256.0 * high))
    block_ref[place, width:] = jnp.where(lane < 3, tail, 0.0).astype(jnp.bfloat16)


def pack_kernel(rows_ref, ids_ref, block_ref):
    pack_into(block_ref, 0, rows_ref[...], ids_ref[...])


def pair_kernel(own_ref, own_ids_ref, rows_ref, ids_ref, both_ref, line_ref):
    count, width = rows_ref.shape
    both_ref[:count, :] = own_ref[...]
    pack_into(both_ref, count, rows_ref[...], ids_ref[...])
    for k in range(width // LANES):
        columns = both_ref[:, k * LANES : (k + 1) * LANES]
        line_ref[2 * count * k : 2 * count * (k + 1), :] = columns
    lines = []
    for ref in (own_ids_ref, ids_ref):
        ids = ref[...].astype(jnp.float32)
        high = jnp.floor(ids[1:2] / 256.0)
        lines += [ids[0:1] + 1.0, high, ids[1:2] - 256.0 * high]
    tail = jnp.concatenate(lines + [jnp.zeros((TAIL - 6, count), jnp.float32)], axis=0)
    if count < LANES:
        tail = jnp.concatenate([tail, jnp.zeros((TAIL, LANES - count), jnp.float32)], axis=1)
    line_ref[2 * count * (width // LANES) :, :] = tail.astype(jnp.bfloat16)


def pack(kernel, operands, shapes):
    rows, width = operands[-2].shape
    return pl.pallas_call(
        kernel,
        in_specs=[VMEM] * len(operands),
        out_specs=[VMEM] * len(shapes),
        out_shape=[jax.ShapeDtypeStruct(shape, jnp.bfloat16) for shape in shapes],
        compiler_params=pltpu.CompilerParams(vmem_limit_bytes=8 * 2**20),
        cost_estimate=pl.CostEstimate(
            flops=4 * rows * width, bytes_accessed=4 * rows * width, transcendentals=rows
        ),
    )(*operands)


def padded(rows):
    spare = -rows.shape[0] % LANES
    if not spare:
        return rows
    return jnp.concatenate([rows, jnp.zeros((spare, rows.shape[1]), rows.dtype)], axis=0)


def own_kernel(*refs):
    own_ref, row_ref, dots = refs[0], *refs[-2:]
    rows, width = own_ref.shape[0], own_ref.shape[1] - LANES
    turned = padded(own_ref[:, width:].astype(jnp.float32)).T
    meta = [(turned[0:1], turned[1:2] * 256.0 + turned[2:3])]

    def visitors_at(k):
        return padded(own_ref[:, k : k + CHUNK])

    bests, _ = best_of(visitors_at, meta, refs[1:-2], rows, False, dots)
    row_ref[...] = bests[0]


def visit_kernel(visitors, arrays, mine, others, *refs):
    line_refs, block_refs = refs[:visitors], refs[visitors : visitors + arrays]
    row_ref, mine_ref, other_ref, dots = refs[visitors + arrays + 1 :]
    width = block_refs[0].shape[1] - LANES
    rows = (line_refs[0].shape[0] - TAIL) // (2 * width // LANES)
    meta = []
    for ref in line_refs:
        tail = ref[2 * rows * (width // LANES) :, :].astype(jnp.float32)
        for row in (0, 3):
            order = tail[row + 1 : row + 2] * 256.0 + tail[row + 2 : row + 3]
            meta.append((tail[row : row + 1], order))

    def visitors_at(k):
        parts = []
        for ref in line_refs:
            for core in range(2):
                starts = [rows * (2 * block + core) for block in range(k // LANES, (k + CHUNK) // LANES)]
                columns = [ref[start : start + rows, :] for start in starts]
                parts.append(padded(jnp.concatenate(columns, axis=1)))
        return jnp.concatenate(parts, axis=0)

    bests, cols = best_of(visitors_at, meta, block_refs, rows, True, dots)
    for v, best in enumerate(bests):
        row_ref[v : v + 1, :] = best
    for ref, picked in ((mine_ref, mine), (other_ref, others)):
        for row, j in enumerate(picked):
            ref[row : row + 1, :] = cols[j]


def best_of(visitors_at, meta, block_refs, rows, homed, dots):
    width = block_refs[0].shape[1] - LANES
    for k in range(0, width, CHUNK):
        left = jnp.concatenate([ref[:, k : k + CHUNK] for ref in block_refs], axis=0)
        part = lax.dot_general(
            left,
            visitors_at(k),
            (((1,), (1,)), ((), ())),
            preferred_element_type=jnp.float32,
        )
        dots[...] = part if k == 0 else dots[...] + part

    tails = jnp.concatenate([ref[:, width:] for ref in block_refs], axis=0).astype(jnp.float32)
    lowest = jnp.full((rows, LANES), -1.0, jnp.float32)
    row_best = [lowest for _ in meta]
    lane = lax.broadcasted_iota(jnp.int32, (rows, LANES), 1)
    col_all = lowest
    for j in range(tails.shape[0] // rows):
        tail = tails[j * rows : (j + 1) * rows]
        block_cluster, block_order = tail[:, 0:1], tail[:, 1:2] * 256.0 + tail[:, 2:3]
        col_best = lowest
        for v, (cluster, order) in enumerate(meta):
            cosine = jnp.where(
                block_cluster == cluster,
                dots[j * rows : (j + 1) * rows, v * LANES : (v + 1) * LANES],
                -1.0,
            )
            seen = jnp.where(block_order < order, cosine, -1.0)
            row_best[v] = jnp.maximum(row_best[v], seen)
            if homed:
                col_best = jnp.maximum(col_best, jnp.where(order < block_order, cosine, -1.0))
        if homed:
            col_all = jnp.where(lane == j, jnp.max(col_best, axis=1, keepdims=True), col_all)
    row_best = [jnp.max(best, axis=0, keepdims=True) for best in row_best]
    if not homed:
        return row_best, None
    if rows < LANES:
        fill = jnp.full((LANES - rows, LANES), -1.0, jnp.float32)
        col_all = jnp.concatenate([col_all, fill], axis=0)
    turned = col_all.T
    return row_best, [turned[j : j + 1] for j in range(dots.shape[0] // rows)]


def call(kernel, operands, count, out_rows, total, width):
    return pl.pallas_call(
        kernel,
        in_specs=[VMEM] * len(operands),
        out_specs=[VMEM] * len(out_rows),
        out_shape=[jax.ShapeDtypeStruct((n, LANES), jnp.float32) for n in out_rows],
        scratch_shapes=[pltpu.VMEM((total, count * LANES), jnp.float32)],
        compiler_params=pltpu.CompilerParams(vmem_limit_bytes=24 * 2**20),
        cost_estimate=pl.CostEstimate(
            flops=2 * total * count * LANES * width,
            bytes_accessed=2 * (total + count * LANES) * width,
            transcendentals=0,
        ),
    )(*operands)


def group_trip(groups, first, second):
    return [(2 * k + c, 2 * (k ^ s) + c) for k in range(groups) for c, s in enumerate((first, second))]


def local(embeddings, cluster_ids, order_index):
    rows, width = embeddings.shape
    groups, length = lax.axis_size("group"), lax.axis_size("z")
    z, core = lax.axis_index("z"), lax.axis_index("core")
    plane_axes, line_axes = ("group", "core"), ("z", "core")
    ids = jnp.stack([cluster_ids, order_index])
    (own,) = pack(pack_kernel, [embeddings, ids], [(rows, width + LANES)])
    shapes = [(2 * rows, width + LANES), (2 * rows * width // LANES + TAIL, LANES)]
    both, line = pack(pair_kernel, [own, ids, swap(embeddings), swap(ids)], shapes)

    routes = [ring_pairs(length, shift) for shift in range(1, length // 2 + 1)]
    trips = []
    for first in range(0, len(routes), 2):
        ways = enumerate(routes[first : first + 2][::-1])
        trips.append([(2 * a + way, 2 * b + way) for way, route in ways for a, b in route])
    visitors = [lax.ppermute(line, line_axes, trip) for trip in trips]

    partners = [(s, s + 1) for s in range(1, groups - 1, 2)]
    arrived = [lax.ppermute(both, plane_axes, group_trip(groups, *way)) for way in partners]
    last = groups - 1
    relay = group_trip(groups, last ^ partners[-1][0], last ^ partners[-1][1])
    half = rows // 2
    corner = [arrived[-1][first : first + half] for first in (0, half)]
    corner = [lax.ppermute(part, plane_axes, relay) for part in corner]
    sides = [(block, swap(block)) for block in arrived]
    chunks = [[both, *sides[-1], *corner, *(swap(part) for part in corner)]]
    chunks += [[*sides[k], *sides[k + 1]] for k in range(0, len(sides) - 1, 2)]

    orders = [((2, 5, 6, 0), (4, 3, 7, 1))] + [((0, 3, 4, 7), (2, 1, 6, 5))] * (len(chunks) - 1)
    bests, answers = [], []
    for chunk in chunks:
        bests += call(own_kernel, [own, *chunk], 1, [1], 8 * rows, width)
    for index, (chunk, order) in enumerate(zip(chunks, orders)):
        kernel = functools.partial(visit_kernel, len(visitors), len(chunk), *order)
        count = 2 * len(visitors)
        operands = [*visitors, *chunk, bests[index]]
        answers.append(call(kernel, operands, count, [count, 4, 4], 8 * rows, width))
    bests = [best[0, :rows] for best in bests]
    home = functools.reduce(jnp.maximum, [answer[0] for answer in answers])
    merged = [jnp.maximum(mine, swap(others)) for _, mine, others in answers]

    for index, trip in enumerate(trips):
        part = home[2 * index : 2 * index + 2] if len(trips) > 1 else home
        back = lax.ppermute(part, line_axes, [(b, a) for a, b in trip])
        for here, best in ((2 * z + core, back[0:1]), (2 * z + (core ^ 1), swap(back)[1:2])):
            sent = functools.reduce(jnp.logical_or, [here == a for a, _ in trip])
            bests.append(jnp.where(sent, best[0, :rows], -1.0))
    ways = [(0, 0, partners[-1])]
    ways += [(1 + k // 2, 2 * (k % 2), way) for k, way in enumerate(partners[:-1])]
    for chunk, row, (first, second) in ways:
        for offset, order in ((1, (second, first)), (0, (first, second))):
            got = lax.ppermute(merged[chunk], plane_axes, group_trip(groups, *order))
            bests.append(got[row + offset, :rows])
    bests.append(lax.ppermute(merged[0], "group", flip(groups, last))[2, :rows])
    bests.append(merged[0][3, :rows])
    return functools.reduce(jnp.maximum, bests)


def solution(mesh):
    groups, members = mesh.devices.shape
    fine = Mesh(mesh.devices.reshape(groups, members // 2, 2), AXES)
    placed = (P(AXES, None), P(AXES), P(AXES))
    return jax.shard_map(local, mesh=fine, in_specs=placed, out_specs=P(AXES), check_vma=False)
```

```python
import functools

import jax
import jax.numpy as jnp
from jax import lax
from jax.experimental import pallas as pl
from jax.experimental.pallas import tpu as pltpu
from jax.sharding import Mesh, PartitionSpec as P

AXES = ("group", "z", "core")
LANES = 128
CHUNK = 512
TAIL = 16
VMEM = pl.BlockSpec(memory_space=pltpu.VMEM)


def flip(count, bits):
    return [(k, k ^ bits) for k in range(count)]


def unit_rows(values):
    values = values.astype(jnp.float32)
    total = jnp.sum(values * values, axis=1, keepdims=True) + values.shape[1] * 1e-06
    return (values * lax.rsqrt(total)).astype(jnp.bfloat16)


def ring_pairs(length, shift):
    if 2 * shift < length:
        return [(k, (k + shift) % length) for k in range(length)]
    pairs = [(k, k + shift) for k in range(length // 2)]
    return [pair[:: 1 - 2 * (pair[0] % 2)] for pair in pairs]


def swap(block):
    return lax.ppermute(block, "core", flip(2, 1))


def pack_into(block_ref, start, rows, ids):
    count, width = rows.shape
    place = pl.ds(start, count)
    block_ref[place, :width] = unit_rows(rows)
    meta = jnp.concatenate([ids.astype(jnp.float32), jnp.zeros((6, count), jnp.float32)], axis=0)
    if count < LANES:
        meta = jnp.concatenate([meta, jnp.zeros((8, LANES - count), jnp.float32)], axis=1)
    turned = meta.T[:count]
    cluster, order = turned[:, 0:1] + 1.0, turned[:, 1:2]
    high = jnp.floor(order / 256.0)
    lane = lax.broadcasted_iota(jnp.int32, (count, LANES), 1)
    tail = jnp.where(lane == 0, cluster, jnp.where(lane == 1, high, order - 256.0 * high))
    block_ref[place, width:] = jnp.where(lane < 3, tail, 0.0).astype(jnp.bfloat16)


def pack_kernel(rows_ref, ids_ref, block_ref):
    pack_into(block_ref, 0, rows_ref[...], ids_ref[...])


def pair_kernel(own_ref, own_ids_ref, rows_ref, ids_ref, both_ref, line_ref):
    count, width = rows_ref.shape
    both_ref[:count, :] = own_ref[...]
    pack_into(both_ref, count, rows_ref[...], ids_ref[...])
    for k in range(width // LANES):
        columns = both_ref[:, k * LANES : (k + 1) * LANES]
        line_ref[2 * count * k : 2 * count * (k + 1), :] = columns
    lines = []
    for ref in (own_ids_ref, ids_ref):
        ids = ref[...].astype(jnp.float32)
        high = jnp.floor(ids[1:2] / 256.0)
        lines += [ids[0:1] + 1.0, high, ids[1:2] - 256.0 * high]
    tail = jnp.concatenate(lines + [jnp.zeros((TAIL - 6, count), jnp.float32)], axis=0)
    if count < LANES:
        tail = jnp.concatenate([tail, jnp.zeros((TAIL, LANES - count), jnp.float32)], axis=1)
    line_ref[2 * count * (width // LANES) :, :] = tail.astype(jnp.bfloat16)


def pack(kernel, operands, shapes):
    rows, width = operands[-2].shape
    return pl.pallas_call(
        kernel,
        in_specs=[VMEM] * len(operands),
        out_specs=[VMEM] * len(shapes),
        out_shape=[jax.ShapeDtypeStruct(shape, jnp.bfloat16) for shape in shapes],
        compiler_params=pltpu.CompilerParams(vmem_limit_bytes=8 * 2**20),
        cost_estimate=pl.CostEstimate(
            flops=4 * rows * width, bytes_accessed=4 * rows * width, transcendentals=rows
        ),
    )(*operands)


def padded(rows):
    spare = -rows.shape[0] % LANES
    if not spare:
        return rows
    return jnp.concatenate([rows, jnp.zeros((spare, rows.shape[1]), rows.dtype)], axis=0)


def own_kernel(*refs):
    own_ref, row_ref, dots = refs[0], *refs[-2:]
    rows, width = own_ref.shape[0], own_ref.shape[1] - LANES
    turned = padded(own_ref[:, width:].astype(jnp.float32)).T
    meta = [(turned[0:1], turned[1:2] * 256.0 + turned[2:3])]

    def visitors_at(k):
        return padded(own_ref[:, k : k + CHUNK])

    bests, _ = best_of(visitors_at, meta, refs[1:-2], rows, False, dots)
    row_ref[...] = bests[0]


def visit_kernel(visitors, arrays, mine, others, *refs):
    line_refs, block_refs = refs[:visitors], refs[visitors : visitors + arrays]
    row_ref, mine_ref, other_ref, dots = refs[visitors + arrays + 1 :]
    width = block_refs[0].shape[1] - LANES
    rows = (line_refs[0].shape[0] - TAIL) // (2 * width // LANES)
    meta = []
    for ref in line_refs:
        tail = ref[2 * rows * (width // LANES) :, :].astype(jnp.float32)
        for row in (0, 3):
            order = tail[row + 1 : row + 2] * 256.0 + tail[row + 2 : row + 3]
            meta.append((tail[row : row + 1], order))

    def visitors_at(k):
        parts = []
        for ref in line_refs:
            for core in range(2):
                starts = [rows * (2 * block + core) for block in range(k // LANES, (k + CHUNK) // LANES)]
                columns = [ref[start : start + rows, :] for start in starts]
                parts.append(padded(jnp.concatenate(columns, axis=1)))
        return jnp.concatenate(parts, axis=0)

    bests, cols = best_of(visitors_at, meta, block_refs, rows, True, dots)
    for v, best in enumerate(bests):
        row_ref[v : v + 1, :] = best
    for ref, picked in ((mine_ref, mine), (other_ref, others)):
        for row, j in enumerate(picked):
            ref[row : row + 1, :] = cols[j]


def best_of(visitors_at, meta, block_refs, rows, homed, dots):
    width = block_refs[0].shape[1] - LANES
    for k in range(0, width, CHUNK):
        left = jnp.concatenate([ref[:, k : k + CHUNK] for ref in block_refs], axis=0)
        part = lax.dot_general(
            left,
            visitors_at(k),
            (((1,), (1,)), ((), ())),
            preferred_element_type=jnp.float32,
        )
        dots[...] = part if k == 0 else dots[...] + part

    tails = jnp.concatenate([ref[:, width:] for ref in block_refs], axis=0).astype(jnp.float32)
    lowest = jnp.full((rows, LANES), -1.0, jnp.float32)
    row_best = [lowest for _ in meta]
    lane = lax.broadcasted_iota(jnp.int32, (rows, LANES), 1)
    col_all = lowest
    for j in range(tails.shape[0] // rows):
        tail = tails[j * rows : (j + 1) * rows]
        block_cluster, block_order = tail[:, 0:1], tail[:, 1:2] * 256.0 + tail[:, 2:3]
        col_best = lowest
        for v, (cluster, order) in enumerate(meta):
            cosine = jnp.where(
                block_cluster == cluster,
                dots[j * rows : (j + 1) * rows, v * LANES : (v + 1) * LANES],
                -1.0,
            )
            seen = jnp.where(block_order < order, cosine, -1.0)
            row_best[v] = jnp.maximum(row_best[v], seen)
            if homed:
                col_best = jnp.maximum(col_best, jnp.where(order < block_order, cosine, -1.0))
        if homed:
            col_all = jnp.where(lane == j, jnp.max(col_best, axis=1, keepdims=True), col_all)
    row_best = [jnp.max(best, axis=0, keepdims=True) for best in row_best]
    if not homed:
        return row_best, None
    if rows < LANES:
        fill = jnp.full((LANES - rows, LANES), -1.0, jnp.float32)
        col_all = jnp.concatenate([col_all, fill], axis=0)
    turned = col_all.T
    return row_best, [turned[j : j + 1] for j in range(dots.shape[0] // rows)]


def call(kernel, operands, count, out_rows, total, width):
    return pl.pallas_call(
        kernel,
        in_specs=[VMEM] * len(operands),
        out_specs=[VMEM] * len(out_rows),
        out_shape=[jax.ShapeDtypeStruct((n, LANES), jnp.float32) for n in out_rows],
        scratch_shapes=[pltpu.VMEM((total, count * LANES), jnp.float32)],
        compiler_params=pltpu.CompilerParams(vmem_limit_bytes=24 * 2**20),
        cost_estimate=pl.CostEstimate(
            flops=2 * total * count * LANES * width,
            bytes_accessed=2 * (total + count * LANES) * width,
            transcendentals=0,
        ),
    )(*operands)


def group_trip(groups, first, second):
    return [(2 * k + c, 2 * (k ^ s) + c) for k in range(groups) for c, s in enumerate((first, second))]


def local(embeddings, cluster_ids, order_index):
    rows, width = embeddings.shape
    groups, length = lax.axis_size("group"), lax.axis_size("z")
    z, core = lax.axis_index("z"), lax.axis_index("core")
    plane_axes, line_axes = ("group", "core"), ("z", "core")
    ids = jnp.stack([cluster_ids, order_index])
    (own,) = pack(pack_kernel, [embeddings, ids], [(rows, width + LANES)])
    shapes = [(2 * rows, width + LANES), (2 * rows * width // LANES + TAIL, LANES)]
    both, line = pack(pair_kernel, [own, ids, swap(embeddings), swap(ids)], shapes)

    routes = [ring_pairs(length, shift) for shift in range(1, length // 2 + 1)]
    trips = []
    for first in range(0, len(routes), 2):
        ways = enumerate(routes[first : first + 2][::-1])
        trips.append([(2 * a + way, 2 * b + way) for way, route in ways for a, b in route])
    visitors = [lax.ppermute(line, line_axes, trip) for trip in trips]

    partners = [(s, s + 1) for s in range(1, groups - 1, 2)]
    arrived = [lax.ppermute(both, plane_axes, group_trip(groups, *way)) for way in partners]
    last = groups - 1
    relay = group_trip(groups, last ^ partners[-1][0], last ^ partners[-1][1])
    half = rows // 2
    corner = [arrived[-1][first : first + half] for first in (0, half)]
    corner = [lax.ppermute(part, plane_axes, relay) for part in corner]
    sides = [(block, swap(block)) for block in arrived]
    chunks = [[both, *sides[-1], *corner, *(swap(part) for part in corner)]]
    chunks += [[*sides[k], *sides[k + 1]] for k in range(0, len(sides) - 1, 2)]

    orders = [((2, 5, 6, 0), (4, 3, 7, 1))] + [((0, 3, 4, 7), (2, 1, 6, 5))] * (len(chunks) - 1)
    bests, answers = [], []
    for chunk in chunks:
        bests += call(own_kernel, [own, *chunk], 1, [1], 8 * rows, width)
    for index, (chunk, order) in enumerate(zip(chunks, orders)):
        kernel = functools.partial(visit_kernel, len(visitors), len(chunk), *order)
        count = 2 * len(visitors)
        operands = [*visitors, *chunk, bests[index]]
        answers.append(call(kernel, operands, count, [count, 4, 4], 8 * rows, width))
    bests = [best[0, :rows] for best in bests]
    home = functools.reduce(jnp.maximum, [answer[0] for answer in answers])
    merged = [jnp.maximum(mine, swap(others)) for _, mine, others in answers]

    for index, trip in enumerate(trips):
        part = home[2 * index : 2 * index + 2] if len(trips) > 1 else home
        back = lax.ppermute(part, line_axes, [(b, a) for a, b in trip])
        for here, best in ((2 * z + core, back[0:1]), (2 * z + (core ^ 1), swap(back)[1:2])):
            sent = functools.reduce(jnp.logical_or, [here == a for a, _ in trip])
            bests.append(jnp.where(sent, best[0, :rows], -1.0))
    ways = [(0, 0, partners[-1])]
    ways += [(1 + k // 2, 2 * (k % 2), way) for k, way in enumerate(partners[:-1])]
    for chunk, row, (first, second) in ways:
        for offset, order in ((0, (first, second)), (1, (second, first))):
            got = lax.ppermute(merged[chunk], plane_axes, group_trip(groups, *order))
            bests.append(got[row + offset, :rows])
    bests.append(lax.ppermute(merged[0], "group", flip(groups, last))[2, :rows])
    bests.append(merged[0][3, :rows])
    return functools.reduce(jnp.maximum, bests)


def solution(mesh):
    groups, members = mesh.devices.shape
    fine = Mesh(mesh.devices.reshape(groups, members // 2, 2), AXES)
    placed = (P(AXES, None), P(AXES), P(AXES))
    return jax.shard_map(local, mesh=fine, in_specs=placed, out_specs=P(AXES), check_vma=False)
```

```python
import functools

import jax
import jax.numpy as jnp
from jax import lax
from jax.experimental import pallas as pl
from jax.experimental.pallas import tpu as pltpu
from jax.sharding import Mesh, PartitionSpec as P

AXES = ("group", "z", "core")
LANES = 128
CHUNK = 256
TAIL = 16
VMEM = pl.BlockSpec(memory_space=pltpu.VMEM)


def flip(count, bits):
    return [(k, k ^ bits) for k in range(count)]


def unit_rows(values):
    values = values.astype(jnp.float32)
    total = jnp.sum(values * values, axis=1, keepdims=True) + values.shape[1] * 1e-06
    return (values * lax.rsqrt(total)).astype(jnp.bfloat16)


def ring_pairs(length, shift):
    if 2 * shift < length:
        return [(k, (k + shift) % length) for k in range(length)]
    pairs = [(k, k + shift) for k in range(length // 2)]
    return [pair[:: 1 - 2 * (pair[0] % 2)] for pair in pairs]


def swap(block):
    return lax.ppermute(block, "core", flip(2, 1))


def pack_into(block_ref, start, rows, ids):
    count, width = rows.shape
    place = pl.ds(start, count)
    block_ref[place, :width] = unit_rows(rows)
    meta = jnp.concatenate([ids.astype(jnp.float32), jnp.zeros((6, count), jnp.float32)], axis=0)
    if count < LANES:
        meta = jnp.concatenate([meta, jnp.zeros((8, LANES - count), jnp.float32)], axis=1)
    turned = meta.T[:count]
    cluster, order = turned[:, 0:1] + 1.0, turned[:, 1:2]
    high = jnp.floor(order / 256.0)
    lane = lax.broadcasted_iota(jnp.int32, (count, LANES), 1)
    tail = jnp.where(lane == 0, cluster, jnp.where(lane == 1, high, order - 256.0 * high))
    block_ref[place, width:] = jnp.where(lane < 3, tail, 0.0).astype(jnp.bfloat16)


def pack_kernel(rows_ref, ids_ref, block_ref):
    pack_into(block_ref, 0, rows_ref[...], ids_ref[...])


def pair_kernel(own_ref, own_ids_ref, rows_ref, ids_ref, both_ref, line_ref):
    count, width = rows_ref.shape
    both_ref[:count, :] = own_ref[...]
    pack_into(both_ref, count, rows_ref[...], ids_ref[...])
    for k in range(width // LANES):
        columns = both_ref[:, k * LANES : (k + 1) * LANES]
        line_ref[2 * count * k : 2 * count * (k + 1), :] = columns
    lines = []
    for ref in (own_ids_ref, ids_ref):
        ids = ref[...].astype(jnp.float32)
        high = jnp.floor(ids[1:2] / 256.0)
        lines += [ids[0:1] + 1.0, high, ids[1:2] - 256.0 * high]
    tail = jnp.concatenate(lines + [jnp.zeros((TAIL - 6, count), jnp.float32)], axis=0)
    if count < LANES:
        tail = jnp.concatenate([tail, jnp.zeros((TAIL, LANES - count), jnp.float32)], axis=1)
    line_ref[2 * count * (width // LANES) :, :] = tail.astype(jnp.bfloat16)


def pack(kernel, operands, shapes):
    rows, width = operands[-2].shape
    return pl.pallas_call(
        kernel,
        in_specs=[VMEM] * len(operands),
        out_specs=[VMEM] * len(shapes),
        out_shape=[jax.ShapeDtypeStruct(shape, jnp.bfloat16) for shape in shapes],
        compiler_params=pltpu.CompilerParams(vmem_limit_bytes=8 * 2**20),
        cost_estimate=pl.CostEstimate(
            flops=4 * rows * width, bytes_accessed=4 * rows * width, transcendentals=rows
        ),
    )(*operands)


def padded(rows):
    spare = -rows.shape[0] % LANES
    if not spare:
        return rows
    return jnp.concatenate([rows, jnp.zeros((spare, rows.shape[1]), rows.dtype)], axis=0)


def own_kernel(*refs):
    own_ref, row_ref, dots = refs[0], *refs[-2:]
    rows, width = own_ref.shape[0], own_ref.shape[1] - LANES
    turned = padded(own_ref[:, width:].astype(jnp.float32)).T
    meta = [(turned[0:1], turned[1:2] * 256.0 + turned[2:3])]

    def visitors_at(k):
        return padded(own_ref[:, k : k + CHUNK])

    bests, _ = best_of(visitors_at, meta, refs[1:-2], rows, False, dots)
    row_ref[...] = bests[0]


def visit_kernel(visitors, arrays, mine, others, *refs):
    line_refs, block_refs = refs[:visitors], refs[visitors : visitors + arrays]
    row_ref, mine_ref, other_ref, dots = refs[visitors + arrays + 1 :]
    width = block_refs[0].shape[1] - LANES
    rows = (line_refs[0].shape[0] - TAIL) // (2 * width // LANES)
    meta = []
    for ref in line_refs:
        tail = ref[2 * rows * (width // LANES) :, :].astype(jnp.float32)
        for row in (0, 3):
            order = tail[row + 1 : row + 2] * 256.0 + tail[row + 2 : row + 3]
            meta.append((tail[row : row + 1], order))

    def visitors_at(k):
        parts = []
        for ref in line_refs:
            for core in range(2):
                starts = [rows * (2 * block + core) for block in range(k // LANES, (k + CHUNK) // LANES)]
                columns = [ref[start : start + rows, :] for start in starts]
                parts.append(padded(jnp.concatenate(columns, axis=1)))
        return jnp.concatenate(parts, axis=0)

    bests, cols = best_of(visitors_at, meta, block_refs, rows, True, dots)
    for v, best in enumerate(bests):
        row_ref[v : v + 1, :] = best
    for ref, picked in ((mine_ref, mine), (other_ref, others)):
        for row, j in enumerate(picked):
            ref[row : row + 1, :] = cols[j]


def best_of(visitors_at, meta, block_refs, rows, homed, dots):
    width = block_refs[0].shape[1] - LANES
    for k in range(0, width, CHUNK):
        left = jnp.concatenate([ref[:, k : k + CHUNK] for ref in block_refs], axis=0)
        part = lax.dot_general(
            left,
            visitors_at(k),
            (((1,), (1,)), ((), ())),
            preferred_element_type=jnp.float32,
        )
        dots[...] = part if k == 0 else dots[...] + part

    tails = jnp.concatenate([ref[:, width:] for ref in block_refs], axis=0).astype(jnp.float32)
    lowest = jnp.full((rows, LANES), -1.0, jnp.float32)
    row_best = [lowest for _ in meta]
    lane = lax.broadcasted_iota(jnp.int32, (rows, LANES), 1)
    col_all = lowest
    for j in range(tails.shape[0] // rows):
        tail = tails[j * rows : (j + 1) * rows]
        block_cluster, block_order = tail[:, 0:1], tail[:, 1:2] * 256.0 + tail[:, 2:3]
        col_best = lowest
        for v, (cluster, order) in enumerate(meta):
            cosine = jnp.where(
                block_cluster == cluster,
                dots[j * rows : (j + 1) * rows, v * LANES : (v + 1) * LANES],
                -1.0,
            )
            seen = jnp.where(block_order < order, cosine, -1.0)
            row_best[v] = jnp.maximum(row_best[v], seen)
            if homed:
                col_best = jnp.maximum(col_best, jnp.where(order < block_order, cosine, -1.0))
        if homed:
            col_all = jnp.where(lane == j, jnp.max(col_best, axis=1, keepdims=True), col_all)
    row_best = [jnp.max(best, axis=0, keepdims=True) for best in row_best]
    if not homed:
        return row_best, None
    if rows < LANES:
        fill = jnp.full((LANES - rows, LANES), -1.0, jnp.float32)
        col_all = jnp.concatenate([col_all, fill], axis=0)
    turned = col_all.T
    return row_best, [turned[j : j + 1] for j in range(dots.shape[0] // rows)]


def call(kernel, operands, count, out_rows, total, width):
    return pl.pallas_call(
        kernel,
        in_specs=[VMEM] * len(operands),
        out_specs=[VMEM] * len(out_rows),
        out_shape=[jax.ShapeDtypeStruct((n, LANES), jnp.float32) for n in out_rows],
        scratch_shapes=[pltpu.VMEM((total, count * LANES), jnp.float32)],
        compiler_params=pltpu.CompilerParams(vmem_limit_bytes=24 * 2**20),
        cost_estimate=pl.CostEstimate(
            flops=2 * total * count * LANES * width,
            bytes_accessed=2 * (total + count * LANES) * width,
            transcendentals=0,
        ),
    )(*operands)


def group_trip(groups, first, second):
    return [(2 * k + c, 2 * (k ^ s) + c) for k in range(groups) for c, s in enumerate((first, second))]


def local(embeddings, cluster_ids, order_index):
    rows, width = embeddings.shape
    groups, length = lax.axis_size("group"), lax.axis_size("z")
    z, core = lax.axis_index("z"), lax.axis_index("core")
    plane_axes, line_axes = ("group", "core"), ("z", "core")
    ids = jnp.stack([cluster_ids, order_index])
    (own,) = pack(pack_kernel, [embeddings, ids], [(rows, width + LANES)])
    shapes = [(2 * rows, width + LANES), (2 * rows * width // LANES + TAIL, LANES)]
    both, line = pack(pair_kernel, [own, ids, swap(embeddings), swap(ids)], shapes)

    routes = [ring_pairs(length, shift) for shift in range(1, length // 2 + 1)]
    trips = []
    for first in range(0, len(routes), 2):
        ways = enumerate(routes[first : first + 2][::-1])
        trips.append([(2 * a + way, 2 * b + way) for way, route in ways for a, b in route])
    visitors = [lax.ppermute(line, line_axes, trip) for trip in trips]

    partners = [(s, s + 1) for s in range(1, groups - 1, 2)]
    arrived = [lax.ppermute(both, plane_axes, group_trip(groups, *way)) for way in partners]
    last = groups - 1
    relay = group_trip(groups, last ^ partners[-1][0], last ^ partners[-1][1])
    half = rows // 2
    corner = [arrived[-1][first : first + half] for first in (0, half)]
    corner = [lax.ppermute(part, plane_axes, relay) for part in corner]
    sides = [(block, swap(block)) for block in arrived]
    chunks = [[both, *sides[-1], *corner, *(swap(part) for part in corner)]]
    chunks += [[*sides[k], *sides[k + 1]] for k in range(0, len(sides) - 1, 2)]

    orders = [((2, 5, 6, 0), (4, 3, 7, 1))] + [((0, 3, 4, 7), (2, 1, 6, 5))] * (len(chunks) - 1)
    bests, answers = [], []
    for chunk in chunks:
        bests += call(own_kernel, [own, *chunk], 1, [1], 8 * rows, width)
    for index, (chunk, order) in enumerate(zip(chunks, orders)):
        kernel = functools.partial(visit_kernel, len(visitors), len(chunk), *order)
        count = 2 * len(visitors)
        operands = [*visitors, *chunk, bests[index]]
        answers.append(call(kernel, operands, count, [count, 4, 4], 8 * rows, width))
    bests = [best[0, :rows] for best in bests]
    home = functools.reduce(jnp.maximum, [answer[0] for answer in answers])
    merged = [jnp.maximum(mine, swap(others)) for _, mine, others in answers]

    for index, trip in enumerate(trips):
        part = home[2 * index : 2 * index + 2] if len(trips) > 1 else home
        back = lax.ppermute(part, line_axes, [(b, a) for a, b in trip])
        for here, best in ((2 * z + core, back[0:1]), (2 * z + (core ^ 1), swap(back)[1:2])):
            sent = functools.reduce(jnp.logical_or, [here == a for a, _ in trip])
            bests.append(jnp.where(sent, best[0, :rows], -1.0))
    ways = [(0, 0, partners[-1])]
    ways += [(1 + k // 2, 2 * (k % 2), way) for k, way in enumerate(partners[:-1])]
    for chunk, row, (first, second) in ways:
        for offset, order in ((1, (second, first)), (0, (first, second))):
            got = lax.ppermute(merged[chunk], plane_axes, group_trip(groups, *order))
            bests.append(got[row + offset, :rows])
    bests.append(lax.ppermute(merged[0], "group", flip(groups, last))[2, :rows])
    bests.append(merged[0][3, :rows])
    return functools.reduce(jnp.maximum, bests)


def solution(mesh):
    groups, members = mesh.devices.shape
    fine = Mesh(mesh.devices.reshape(groups, members // 2, 2), AXES)
    placed = (P(AXES, None), P(AXES), P(AXES))
    return jax.shard_map(local, mesh=fine, in_specs=placed, out_specs=P(AXES), check_vma=False)
```
